32 devices in a mesh: dp: 4 (over x, core), col: 8 (over z, y).
Axes of the slice: x: 2, y: 2, z: 4, core: 2. Of those that a mesh axis runs over, the one named last changes fastest.
Arguments:
- inputs: bfloat16 [32, 1024, 1024], P('dp', 'col'), may hold values from -6 to 6
- starts: int32 [32, 1024], P('dp', 'col'), may hold values from 0 to 1023, as said below
- cotangent: bfloat16 [32, 1024, 1024], P('dp', 'col'), may hold values from -6 to 6
- first_norm_gain: bfloat16 [1024], replicated, may hold values from 0.5 to 1.5
- shift_one: bfloat16 [1024], replicated, may hold values from -1.75 to 1.75
- w_qkv: bfloat16 [1024, 3072], replicated, may hold values from -0.1875 to 0.1875
- b_qkv: bfloat16 [3072], replicated, may hold values from -1.75 to 1.75
- w_out: bfloat16 [1024, 1024], replicated, may hold values from -1 to 1
- b_out: bfloat16 [1024], replicated, may hold values from -1.75 to 1.75
- second_norm_gain: bfloat16 [1024], replicated, may hold values from 0.5 to 1.5
- shift_two: bfloat16 [1024], replicated, may hold values from -1.75 to 1.75
- w_fc: bfloat16 [1024, 4096], replicated, may hold values from -0.1875 to 0.1875
- b_fc: bfloat16 [4096], replicated, may hold values from -1.75 to 1.75
- w_proj: bfloat16 [4096, 1024], replicated, may hold values from -0.09375 to 0.09375
- b_proj: bfloat16 [1024], replicated, may hold values from -1.75 to 1.75
- prefix_table: float32 [10, 512], replicated, may hold values from -6 to 6
- rep_w1: float32 [512, 512], replicated, may hold values from -0.25 to 0.25
- rep_b1: float32 [512], replicated, may hold values from -3 to 3
- rep_w2: float32 [512, 2048], P(None, 'col'), may hold values from -0.25 to 0.25
- rep_b2: float32 [2048], P('col'), may hold values from -3 to 3
Outputs:
- output: bfloat16 [32, 1024, 1024], P('dp', 'col')
- grad_input: bfloat16 [32, 1024, 1024], P('dp', 'col')
- grad_table: float32 [10, 512], replicated
- grad_w1: float32 [512, 512], replicated
- grad_b1: float32 [512], replicated
- grad_w2: float32 [512, 2048], P(None, 'col')
- grad_b2: float32 [2048], P('col')
The draws below stay inside these ranges and needn't reach their ends.
Inputs may be any that keep to these rules, and one draw needn't show every extreme that they name: starts[r, q] is the first position of the document that holds token q of packed row r: it is equal over a document, equals q at a document's first token; position 0 begins a document, and position 1023 begins a document of one token in every packed row.
All inputs are finite; a program needn't handle non-finite values.
Results may differ from the reference program's by a relative error of at most 0.013.
Values may be sent and summed in bfloat16 or wider, within the bound.
A program may use at most 512 MiB of HBM per device.

```python
import jax
import jax.numpy as jnp
from jax import lax

D = 1024
H = 16
HD = 64
FF = 4096
LEN = 1024
NPRE = 10
PD = 512
PH = 512
ROWS_GRP = 8
ROWS = 32
PCOL = 2048
N_DP = 4
N_COL = 8


def draw_starts(key, part):
    key = jax.random.fold_in(key, 7)
    flag_key, row_key = jax.random.split(key)
    piece_len = LEN // N_COL
    position = jnp.arange(LEN, dtype=jnp.int32)
    flags = jax.random.randint(flag_key, (ROWS, LEN), 0, LEN) < 4
    chosen = jax.random.randint(row_key, (N_DP,), 0, ROWS_GRP)
    row_index = jnp.arange(ROWS, dtype=jnp.int32)
    long_row = row_index % ROWS_GRP == chosen[row_index // ROWS_GRP]
    keep_flag = jnp.logical_not(long_row[:, None]) | (position[None, :] < piece_len)
    flags = flags & keep_flag | (position[None, :] == 0) | (position[None, :] == LEN - 1)
    marks = jnp.where(flags, position[None, :], 0)
    return lax.cummax(marks, axis=1).astype(jnp.int32)


def levels(own_key, extent, cuts, low, high):
    factor_of = 1.0
    for axis_at, parts in cuts:
        heights = jax.random.uniform(jax.random.fold_in(jax.random.fold_in(own_key, 6), axis_at), (parts,), jnp.float32, low / len(cuts), high / len(cuts))
        factor_of = factor_of * jnp.repeat(jnp.exp(heights), extent[axis_at] // parts).reshape((-1,) + (1,) * (len(extent) - 1 - axis_at))
    return factor_of


def normal_values(stream_key, extent, width, bound, cuts=(), kind=jnp.bfloat16):
    values = width * jax.random.normal(stream_key, extent, jnp.float32)
    if cuts:
        values = values * levels(stream_key, extent, cuts, -0.22, 0.18)
    return jnp.clip(values, -bound, bound).astype(kind)


def setup_inputs(seed: int = 0) -> dict:
    keys = jax.random.split(jax.random.key(seed), 21)
    return {
        "inputs": normal_values(keys[0], (ROWS, LEN, D), 1.0, 6.0, ((0, 4), (1, 8))),
        "starts": draw_starts(jax.random.fold_in(keys[20], 71), 0),
        "cotangent": normal_values(keys[2], (ROWS, LEN, D), 1.0, 6.0, ((0, 4), (1, 8))),
        "first_norm_gain": jnp.clip(1.0 + 0.1 * jax.random.normal(keys[3], (D,), jnp.float32), 0.5, 1.5).astype(jnp.bfloat16),
        "shift_one": normal_values(keys[4], (D,), 0.3, 1.75),
        "w_qkv": normal_values(keys[5], (D, 3 * D), D ** -0.5, 0.1875),
        "b_qkv": normal_values(keys[6], (3 * D,), 0.3, 1.75),
        "w_out": normal_values(keys[7], (D, D), (D // 32) ** -0.5, 1.0),
        "b_out": normal_values(keys[8], (D,), 0.3, 1.75),
        "second_norm_gain": jnp.clip(1.0 + 0.1 * jax.random.normal(keys[9], (D,), jnp.float32), 0.5, 1.5).astype(jnp.bfloat16),
        "shift_two": normal_values(keys[10], (D,), 0.3, 1.75),
        "w_fc": normal_values(keys[11], (D, FF), D ** -0.5, 0.1875),
        "b_fc": normal_values(keys[12], (FF,), 0.3, 1.75),
        "w_proj": normal_values(keys[13], (FF, D), FF ** -0.5, 0.09375),
        "b_proj": normal_values(keys[14], (D,), 0.3, 1.75),
        "prefix_table": normal_values(keys[15], (NPRE, PD), 1.0, 6.0, (), jnp.float32),
        "rep_w1": normal_values(keys[16], (PD, PH), PD ** -0.5, 0.25, (), jnp.float32),
        "rep_b1": normal_values(keys[17], (PH,), 0.5, 3.0, (), jnp.float32),
        "rep_w2": normal_values(keys[18], (PH, PCOL), PH ** -0.5, 0.25, ((1, 8),), jnp.float32),
        "rep_b2": normal_values(keys[19], (PCOL,), 0.5, 3.0, ((0, 8),), jnp.float32),
    }


@jax.custom_vjp
def low(v):
    return lax.optimization_barrier(v.astype(jnp.bfloat16)).astype(jnp.float32)

@jax.custom_vjp
def low_back(v):
    return v

def low_keep(v):
    return (low(v), None)

def low_pass(kept, grad):
    return (grad,)

def back_keep(v):
    return (v, None)

def back_low(kept, grad):
    return (low(grad),)
low.defvjp(low_keep, low_pass)
low_back.defvjp(back_keep, back_low)
epsilon = 1e-05
gelu_coef = 0.7978845608028654
cubic_coef = 0.044715

def product(pattern, left_side, right_side):
    return jnp.einsum(pattern, left_side, right_side, precision=lax.Precision.HIGHEST)

def layer_normalize(values, norm_gain, norm_shift):
    center = values - lax.optimization_barrier(jnp.mean(values, axis=-1, keepdims=True))
    variance = lax.optimization_barrier(jnp.mean(center * center, axis=-1, keepdims=True))
    return center * lax.rsqrt(variance + epsilon) * norm_gain + norm_shift

def gelu_tanh(values):
    return 0.5 * values * (1.0 + jnp.tanh(gelu_coef * (values + cubic_coef * values * values * values)))

def one_row(frozen, prefix_keys, prefix_values, row_input, row_starts):
    first_norm_gain, shift_one, w_qkv, b_qkv, w_out, b_out, second_norm_gain, shift_two, w_fc, b_fc, w_proj, b_proj = frozen
    score_scale = HD ** (-0.5)
    first_normed_rows = layer_normalize(row_input, first_norm_gain, shift_one)
    mixed_rows = product('ld,de->le', low(first_normed_rows), w_qkv) + b_qkv
    queries = low(low_back(mixed_rows[:, :D])).reshape(LEN, H, HD)
    key_heads = low(low_back(mixed_rows[:, D:2 * D])).reshape(LEN, H, HD)
    values = low(low_back(mixed_rows[:, 2 * D:])).reshape(LEN, H, HD)
    position = jnp.arange(LEN, dtype=jnp.int32)
    allowed = (position[None, :] >= row_starts[:, None]) & (position[None, :] <= position[:, None])
    token_scores = low_back(product('qhe,khe->hqk', queries, key_heads) * score_scale)
    token_scores = jnp.where(allowed[None], token_scores, -jnp.inf)
    prefix_scores = low_back(product('qhe,phe->hqp', queries, prefix_keys) * score_scale)
    scores = jnp.concatenate([prefix_scores, token_scores], axis=-1)
    logsum = jax.nn.logsumexp(scores, axis=-1, keepdims=True)
    soft_weights = low(jnp.exp(scores - logsum))
    attended = product('hqp,phe->qhe', soft_weights[:, :, :NPRE], prefix_values)
    attended = attended + product('hqk,khe->qhe', soft_weights[:, :, NPRE:], values)
    attended = low(low_back(attended.reshape(LEN, D)))
    middle = row_input + low_back(product('ld,de->le', attended, w_out) + b_out)
    second_normed_rows = layer_normalize(middle, second_norm_gain, shift_two)
    upper_rows = low_back(product('ld,df->lf', low(second_normed_rows), w_fc) + b_fc)
    activation = low(gelu_tanh(upper_rows))
    return middle + low_back(product('lf,fd->ld', activation, w_proj) + b_proj)

def reference(inputs, starts, cotangent, first_norm_gain, shift_one, w_qkv, b_qkv, w_out, b_out, second_norm_gain, shift_two, w_fc, b_fc, w_proj, b_proj, prefix_table, rep_w1, rep_b1, rep_w2, rep_b2):
    frozen = tuple((weight_array.astype(jnp.float32) for weight_array in (first_norm_gain, shift_one, w_qkv, b_qkv, w_out, b_out, second_norm_gain, shift_two, w_fc, b_fc, w_proj, b_proj)))

    def forward(table_rows, w_one, b_one, w_two, b_two, rows_input):
        pre_act = low_back(product('pd,dh->ph', low(table_rows), low(w_one)) + b_one)
        hidden = jnp.tanh(pre_act)
        prefix = low(low_back(product('ph,hc->pc', low(hidden), low(w_two)) + b_two))
        prefix_keys = prefix[:, :D].reshape(NPRE, H, HD)
        prefix_values = prefix[:, D:].reshape(NPRE, H, HD)

        def row_step(row_block):
            return one_row(frozen, prefix_keys, prefix_values, row_block[0], row_block[1])
        return lax.map(jax.checkpoint(row_step), (rows_input, starts))
    result, pullback = jax.vjp(forward, prefix_table, rep_w1, rep_b1, rep_w2, rep_b2, inputs.astype(jnp.float32))
    grad_table, grad_w1, grad_b1, grad_w2, grad_b2, grad_input = pullback(cotangent.astype(jnp.float32))
    return (result.astype(jnp.bfloat16), grad_input.astype(jnp.bfloat16), grad_table, grad_w1, grad_b1, grad_w2, grad_b2)
```

```python
import functools

import jax
import jax.numpy as jnp
from jax import lax
from jax.experimental import pallas as pl
from jax.experimental.pallas import tpu as pltpu
from jax.sharding import PartitionSpec as P

H = 16
HEAD = 64
PAIR = 2 * HEAD
BLOCK = 256
PRE = 16

epsilon = 1e-05
gelu_coef = 0.7978845608028654
cubic_coef = 0.044715
low_type = jnp.bfloat16
wide = jnp.float32
NT = (((1,), (1,)), ((), ()))


def layer_normalize(values, norm_gain, norm_shift):
    center = values - jnp.mean(values, axis=-1, keepdims=True)
    inverse = lax.rsqrt(jnp.mean(center * center, axis=-1, keepdims=True) + epsilon)
    normed = center * inverse
    return (normed * norm_gain + norm_shift, normed, inverse)


def norm_backward_pass(gradient, norm_gain, normed, inverse):
    scaled = gradient * norm_gain
    centered = scaled - jnp.mean(scaled, axis=-1, keepdims=True)
    return inverse * (centered - normed * jnp.mean(scaled * normed, axis=-1, keepdims=True))


def gelu_parts(upper_rows):
    tangent = jnp.tanh(gelu_coef * (upper_rows + cubic_coef * upper_rows * upper_rows * upper_rows))
    gelu_value = 0.5 * upper_rows * (1.0 + tangent)
    gelu_slope = 0.5 * (1.0 + tangent) + 0.5 * upper_rows * (
        1.0 - tangent * tangent
    ) * gelu_coef * (1.0 + 3.0 * cubic_coef * upper_rows * upper_rows)
    return (gelu_value, gelu_slope)


def dense_product(pattern, left_side, right_side):
    return jnp.einsum(pattern, left_side, right_side, preferred_element_type=jnp.float32)


def dot_nt(a, b):
    return lax.dot_general(a, b, NT, preferred_element_type=wide)


def dot(a, b):
    return jnp.dot(a, b, preferred_element_type=wide)


def head_mask(values, which):
    lane = lax.broadcasted_iota(jnp.int32, values.shape, 1)
    keep = (lane < HEAD) if which == 0 else (lane >= HEAD)
    return jnp.where(keep, values, jnp.zeros_like(values))


def token_mask(scores, start, block_q, block_k):
    key = block_k * BLOCK + lax.broadcasted_iota(jnp.int32, scores.shape, 0)
    keep = key >= start
    if block_q == block_k:
        query = block_q * BLOCK + lax.broadcasted_iota(jnp.int32, scores.shape, 1)
        keep = keep & (key <= query)
    return jnp.where(keep, scores, -jnp.inf)


def prefix_mask(scores, count):
    key = lax.broadcasted_iota(jnp.int32, scores.shape, 0)
    return jnp.where(key < count, scores, -jnp.inf)


def attention_forward_kernel(
    count, starts_ref, q_ref, k_ref, v_ref, pk_ref, pv_ref, out_ref, lse_ref, vt_ref, pvt_ref, s_ref
):
    length = q_ref.shape[0]
    blocks = length // BLOCK
    vt_ref[...] = v_ref[...].astype(wide).T.astype(low_type)
    pvt_ref[...] = pv_ref[...].astype(wide).T.astype(low_type)
    for i in range(blocks):
        rows = slice(i * BLOCK, (i + 1) * BLOCK)
        start = starts_ref[:, rows]
        query = q_ref[rows, :]
        parts = []
        for h in range(2):
            feats = slice(h * HEAD, (h + 1) * HEAD)
            mine = head_mask(query, h)
            pre = prefix_mask(dot_nt(pk_ref[...], mine), count)
            peak = jnp.max(pre, axis=0, keepdims=True)
            for c in range(i + 1):
                keys = slice(c * BLOCK, (c + 1) * BLOCK)
                s = token_mask(dot_nt(k_ref[keys, :], mine), start, i, c)
                s_ref[h, keys, :] = s
                peak = jnp.maximum(peak, jnp.max(s, axis=0, keepdims=True))
            pre = jnp.exp(pre - peak)
            total = jnp.sum(pre, axis=0, keepdims=True)
            acc = dot(pvt_ref[feats, :], pre.astype(low_type))
            for c in range(i + 1):
                keys = slice(c * BLOCK, (c + 1) * BLOCK)
                p = jnp.exp(s_ref[h, keys, :] - peak)
                total = total + jnp.sum(p, axis=0, keepdims=True)
                acc = acc + dot(vt_ref[feats, keys], p.astype(low_type))
            parts.append(acc / total)
            lse_ref[0, h : h + 1, rows] = peak + jnp.log(total)
        out_ref[rows, :] = jnp.concatenate(parts, axis=0).T.astype(low_type)


def attention_backward_kernel(
    count,
    starts_ref,
    q_ref,
    k_ref,
    v_ref,
    g_ref,
    pk_ref,
    pv_ref,
    lse_ref,
    dq_ref,
    dk_ref,
    dv_ref,
    dpk_ref,
    dpv_ref,
    kt_ref,
    pkt_ref,
    p_ref,
    dp_ref,
    ds_ref,
    dk_acc,
    dv_acc,
):
    length = q_ref.shape[0]
    blocks = length // BLOCK
    kt_ref[...] = k_ref[...].astype(wide).T.astype(low_type)
    pkt_ref[...] = pk_ref[...].astype(wide).T.astype(low_type)
    dk_acc[...] = jnp.zeros_like(dk_acc)
    dv_acc[...] = jnp.zeros_like(dv_acc)
    dpk_ref[...] = jnp.zeros_like(dpk_ref)
    dpv_ref[...] = jnp.zeros_like(dpv_ref)
    for i in range(blocks):
        rows = slice(i * BLOCK, (i + 1) * BLOCK)
        start = starts_ref[:, rows]
        parts = []
        for h in range(2):
            feats = slice(h * HEAD, (h + 1) * HEAD)
            mine = head_mask(q_ref[rows, :], h)
            grad = head_mask(g_ref[rows, :], h)
            lse = lse_ref[0, h : h + 1, rows]
            pre = jnp.exp(prefix_mask(dot_nt(pk_ref[...], mine), count) - lse)
            dpre = dot_nt(pv_ref[...], grad)
            delta = jnp.sum(pre * dpre, axis=0, keepdims=True)
            for c in range(i + 1):
                keys = slice(c * BLOCK, (c + 1) * BLOCK)
                p = jnp.exp(token_mask(dot_nt(k_ref[keys, :], mine), start, i, c) - lse)
                dp = dot_nt(v_ref[keys, :], grad)
                delta = delta + jnp.sum(p * dp, axis=0, keepdims=True)
                p_ref[keys, :] = p
                dp_ref[keys, :] = dp
                dv_acc[keys, :] += dot(p.astype(low_type), grad)
            dpre = (pre * (dpre - delta)).astype(low_type)
            dpv_ref[...] += dot(pre.astype(low_type), grad)
            dpk_ref[...] += dot(dpre, mine)
            acc = dot(pkt_ref[feats, :], dpre)
            for c in range(i + 1):
                keys = slice(c * BLOCK, (c + 1) * BLOCK)
                ds = (p_ref[keys, :] * (dp_ref[keys, :] - delta)).astype(low_type)
                dk_acc[keys, :] += dot(ds, mine)
                acc = acc + dot(kt_ref[feats, keys], ds)
            parts.append(acc)
        dq_ref[rows, :] = (jnp.concatenate(parts, axis=0).T * (HEAD**-0.5)).astype(low_type)
    dk_ref[...] = dk_acc[...].astype(low_type)
    dv_ref[...] = dv_acc[...].astype(low_type)


def attention_forward(starts, qkv, pk, pv, count):
    length, width = qkv.shape[0], qkv.shape[1] // 3
    pairs = width // PAIR
    slab = lambda off: pl.BlockSpec((length, PAIR), lambda p: (0, p + off * pairs))
    small = pl.BlockSpec((PRE, PAIR), lambda p: (0, p))
    return pl.pallas_call(
        functools.partial(attention_forward_kernel, count),
        grid=(pairs,),
        in_specs=[
            pl.BlockSpec((1, length), lambda p: (0, 0)),
            slab(0),
            slab(1),
            slab(2),
            small,
            small,
        ],
        out_specs=[slab(0), pl.BlockSpec((1, 2, length), lambda p: (p, 0, 0))],
        out_shape=[
            jax.ShapeDtypeStruct((length, width), low_type),
            jax.ShapeDtypeStruct((pairs, 2, length), wide),
        ],
        scratch_shapes=[
            pltpu.VMEM((PAIR, length), low_type),
            pltpu.VMEM((PAIR, PRE), low_type),
            pltpu.VMEM((2, length, BLOCK), wide),
        ],
        compiler_params=pltpu.CompilerParams(vmem_limit_bytes=48 << 20),
        cost_estimate=pl.CostEstimate(flops=20_000_000_000, bytes_accessed=10 << 20, transcendentals=0),
    )(starts, qkv, qkv, qkv, pk, pv)


def attention_backward(starts, qkv, grad, pk, pv, lse, count):
    length, width = qkv.shape[0], qkv.shape[1] // 3
    pairs = width // PAIR
    slab = lambda off: pl.BlockSpec((length, PAIR), lambda p: (0, p + off * pairs))
    small = pl.BlockSpec((PRE, PAIR), lambda p: (0, p))
    whole = jax.ShapeDtypeStruct((length, width), low_type)
    return pl.pallas_call(
        functools.partial(attention_backward_kernel, count),
        grid=(pairs,),
        in_specs=[
            pl.BlockSpec((1, length), lambda p: (0, 0)),
            slab(0),
            slab(1),
            slab(2),
            slab(0),
            small,
            small,
            pl.BlockSpec((1, 2, length), lambda p: (p, 0, 0)),
        ],
        out_specs=[slab(0), slab(0), slab(0), small, small],
        out_shape=[whole] * 3 + [jax.ShapeDtypeStruct((PRE, width), wide)] * 2,
        scratch_shapes=[
            pltpu.VMEM((PAIR, length), low_type),
            pltpu.VMEM((PAIR, PRE), low_type),
            pltpu.VMEM((length, BLOCK), wide),
            pltpu.VMEM((length, BLOCK), wide),
            pltpu.VMEM((length, BLOCK), low_type),
            pltpu.VMEM((length, PAIR), wide),
            pltpu.VMEM((length, PAIR), wide),
        ],
        compiler_params=pltpu.CompilerParams(vmem_limit_bytes=48 << 20),
        cost_estimate=pl.CostEstimate(flops=40_000_000_000, bytes_accessed=20 << 20, transcendentals=0),
    )(starts, qkv, qkv, qkv, grad, pk, pv, lse)


def exchange(values):
    return lax.all_to_all(values, "col", split_axis=0, concat_axis=0, tiled=True)


def on_device(
    inputs,
    starts,
    cotangent,
    first_norm_gain,
    shift_one,
    w_qkv,
    b_qkv,
    w_out,
    b_out,
    second_norm_gain,
    shift_two,
    w_fc,
    b_fc,
    w_proj,
    b_proj,
    prefix_table,
    rep_w1,
    rep_b1,
    rep_w2,
    rep_b2,
):
    col_count = lax.axis_size("col")
    row_count, piece_len, model_width = inputs.shape
    assert row_count == col_count
    length = piece_len * col_count
    home = (col_count, piece_len, model_width)

    row_inputs = exchange(inputs).reshape(length, model_width)
    row_starts = exchange(starts).reshape(1, length)
    cotangent, row_inputs = lax.optimization_barrier((cotangent, row_inputs))
    row_cot = exchange(cotangent).reshape(length, model_width)

    pre_act = (
        dense_product("pd,dh->ph", prefix_table.astype(low_type), rep_w1.astype(low_type)) + rep_b1
    )
    hidden = jnp.tanh(pre_act)
    hidden_low = hidden.astype(low_type)
    w2_low = rep_w2.astype(low_type)
    own_cols = (dense_product("ph,hc->pc", hidden_low, w2_low) + rep_b2).astype(low_type)
    prefix_all = lax.all_gather(own_cols, "col", axis=1, tiled=True)
    prefix_rows = prefix_all.shape[0]
    prefix_all = jnp.pad(prefix_all, ((0, PRE - prefix_rows), (0, 0)))
    pk = prefix_all[:, :model_width]
    pv = prefix_all[:, model_width:]

    residual = row_inputs.astype(wide)
    first_gain, second_gain = first_norm_gain.astype(wide), second_norm_gain.astype(wide)
    first_normed, first_standardized, first_inverse = layer_normalize(
        residual, first_gain, shift_one.astype(wide)
    )
    mixed = dot(first_normed.astype(low_type), w_qkv) + b_qkv.astype(wide)
    scale = jnp.where(jnp.arange(3 * model_width) < model_width, HEAD**-0.5, 1.0)
    qkv = (mixed * scale).astype(low_type)
    attended, lse = attention_forward(row_starts, qkv, pk, pv, prefix_rows)
    middle = residual + dot(attended, w_out) + b_out.astype(wide)
    second_normed, second_standardized, second_inverse = layer_normalize(
        middle, second_gain, shift_two.astype(wide)
    )
    upper = dot(second_normed.astype(low_type), w_fc) + b_fc.astype(wide)
    activation, gelu_slope = gelu_parts(upper)
    result = middle + dot(activation.astype(low_type), w_proj) + b_proj.astype(wide)
    output = exchange(result.astype(low_type).reshape(home))

    grad_act = dot_nt(row_cot, w_proj)
    grad_upper = (grad_act * gelu_slope).astype(low_type)
    grad_middle = row_cot.astype(wide) + norm_backward_pass(
        dot_nt(grad_upper, w_fc), second_gain, second_standardized, second_inverse
    )
    grad_attended = dot_nt(grad_middle.astype(low_type), w_out).astype(low_type)
    dq, dk, dv, dpk, dpv = attention_backward(
        row_starts, qkv, grad_attended, pk, pv, lse, prefix_rows
    )
    grad_mixed = jnp.concatenate([dq, dk, dv], axis=-1)
    grad_row = grad_middle + norm_backward_pass(
        dot_nt(grad_mixed, w_qkv), first_gain, first_standardized, first_inverse
    )
    grad_input = exchange(grad_row.astype(low_type).reshape(home))

    prefix_local = jnp.concatenate([dpk[:prefix_rows], dpv[:prefix_rows]], axis=1)
    own_grad = lax.psum_scatter(prefix_local, "col", scatter_dimension=1, tiled=True)
    own_grad = lax.psum(own_grad, "dp")
    own_low = own_grad.astype(low_type)
    grad_w2 = dense_product("ph,pc->hc", hidden_low, own_low)
    grad_b2 = jnp.sum(own_low.astype(wide), axis=0)
    hidden_part = dense_product("pc,hc->ph", own_low, w2_low)
    grad_hidden = lax.psum(hidden_part, "col")
    grad_pre = (grad_hidden * (1.0 - hidden * hidden)).astype(low_type)
    grad_w1 = dense_product("pd,ph->dh", prefix_table.astype(low_type), grad_pre)
    grad_b1 = jnp.sum(grad_pre.astype(wide), axis=0)
    grad_table = dense_product("ph,dh->pd", grad_pre, rep_w1.astype(low_type))
    return (output, grad_input, grad_table, grad_w1, grad_b1, grad_w2, grad_b2)


def solution(mesh):
    rows = P("dp", "col", None)
    return jax.shard_map(
        on_device,
        mesh=mesh,
        in_specs=(rows, P("dp", "col"), rows) + (P(),) * 15 + (P(None, "col"), P("col")),
        out_specs=(rows, rows, P(), P(), P(), P(None, "col"), P("col")),
        check_vma=False,
    )
```

```python
import functools

import jax
import jax.numpy as jnp
from jax import lax
from jax.experimental import pallas as pl
from jax.experimental.pallas import tpu as pltpu
from jax.sharding import PartitionSpec as P

H = 16
HEAD = 64
PAIR = 2 * HEAD
BLOCK = 256
PRE = 16

epsilon = 1e-05
gelu_coef = 0.7978845608028654
cubic_coef = 0.044715
low_type = jnp.bfloat16
wide = jnp.float32
NT = (((1,), (1,)), ((), ()))
TN = (((0,), (0,)), ((), ()))
MESH = pl.DeviceIdType.MESH
ANY = pl.BlockSpec(memory_space=pl.ANY)
VM = pl.BlockSpec(memory_space=pltpu.VMEM)


def standardize(values):
    center = values - jnp.mean(values, axis=-1, keepdims=True)
    inverse = lax.rsqrt(jnp.mean(center * center, axis=-1, keepdims=True) + epsilon)
    return center * inverse, inverse


def norm_backward_pass(gradient, norm_gain, normed, inverse):
    scaled = gradient * norm_gain
    centered = scaled - jnp.mean(scaled, axis=-1, keepdims=True)
    return inverse * (centered - normed * jnp.mean(scaled * normed, axis=-1, keepdims=True))


def gelu_parts(upper):
    square = upper * upper
    tangent = jnp.tanh(upper * (gelu_coef + (gelu_coef * cubic_coef) * square))
    half = 0.5 * upper
    share = 0.5 + 0.5 * tangent
    slope = share + half * (1.0 - tangent * tangent) * (
        gelu_coef + (3.0 * gelu_coef * cubic_coef) * square
    )
    return upper * share, slope


def dot_nt(a, b):
    return lax.dot_general(a, b, NT, preferred_element_type=wide)


def dot(a, b):
    return jnp.dot(a, b, preferred_element_type=wide)


def head_mask(values, which):
    lane = lax.broadcasted_iota(jnp.int32, values.shape, 1)
    keep = (lane < HEAD) if which == 0 else (lane >= HEAD)
    return jnp.where(keep, values, jnp.zeros_like(values))


def token_mask(scores, start, block_q, block_k):
    key = block_k * BLOCK + lax.broadcasted_iota(jnp.int32, scores.shape, 0)
    keep = key >= start
    if block_q == block_k:
        query = block_q * BLOCK + lax.broadcasted_iota(jnp.int32, scores.shape, 1)
        keep = keep & (key <= query)
    return jnp.where(keep, scores, -jnp.inf)


def prefix_mask(scores, count):
    key = lax.broadcasted_iota(jnp.int32, scores.shape, 0)
    return jnp.where(key < count, scores, -jnp.inf)


def attention_forward_kernel(
    count, starts_ref, q_ref, k_ref, v_ref, pk_ref, pv_ref, out_ref, lse_ref, vt_ref, pvt_ref, s_ref
):
    length = q_ref.shape[0]
    blocks = length // BLOCK
    vt_ref[...] = v_ref[...].astype(wide).T.astype(low_type)
    pvt_ref[...] = pv_ref[...].astype(wide).T.astype(low_type)
    for i in range(blocks):
        rows = slice(i * BLOCK, (i + 1) * BLOCK)
        start = starts_ref[:, rows]
        query = q_ref[rows, :]
        parts = []
        for h in range(2):
            feats = slice(h * HEAD, (h + 1) * HEAD)
            mine = head_mask(query, h)
            pre = prefix_mask(dot_nt(pk_ref[...], mine), count)
            peak = jnp.max(pre, axis=0, keepdims=True)
            for c in range(i + 1):
                keys = slice(c * BLOCK, (c + 1) * BLOCK)
                s = token_mask(dot_nt(k_ref[keys, :], mine), start, i, c)
                s_ref[h, keys, :] = s
                peak = jnp.maximum(peak, jnp.max(s, axis=0, keepdims=True))
            pre = jnp.exp(pre - peak)
            total = jnp.sum(pre, axis=0, keepdims=True)
            acc = dot(pvt_ref[feats, :], pre.astype(low_type))
            for c in range(i + 1):
                keys = slice(c * BLOCK, (c + 1) * BLOCK)
                p = jnp.exp(s_ref[h, keys, :] - peak)
                total = total + jnp.sum(p, axis=0, keepdims=True)
                acc = acc + dot(vt_ref[feats, keys], p.astype(low_type))
            parts.append(acc / total)
            lse_ref[0, h : h + 1, rows] = peak + jnp.log(total)
        out_ref[rows, :] = jnp.concatenate(parts, axis=0).T.astype(low_type)


def attention_backward_kernel(
    count,
    starts_ref,
    q_ref,
    k_ref,
    v_ref,
    g_ref,
    pk_ref,
    pv_ref,
    lse_ref,
    dq_ref,
    dk_ref,
    dv_ref,
    dpk_ref,
    dpv_ref,
    kt_ref,
    pkt_ref,
    p_ref,
    dp_ref,
    ds_ref,
    dk_acc,
    dv_acc,
):
    length = q_ref.shape[0]
    blocks = length // BLOCK
    kt_ref[...] = k_ref[...].astype(wide).T.astype(low_type)
    pkt_ref[...] = pk_ref[...].astype(wide).T.astype(low_type)
    dk_acc[...] = jnp.zeros_like(dk_acc)
    dv_acc[...] = jnp.zeros_like(dv_acc)
    dpk_ref[...] = jnp.zeros_like(dpk_ref)
    dpv_ref[...] = jnp.zeros_like(dpv_ref)
    for i in range(blocks):
        rows = slice(i * BLOCK, (i + 1) * BLOCK)
        start = starts_ref[:, rows]
        parts = []
        for h in range(2):
            feats = slice(h * HEAD, (h + 1) * HEAD)
            mine = head_mask(q_ref[rows, :], h)
            grad = head_mask(g_ref[rows, :], h)
            lse = lse_ref[0, h : h + 1, rows]
            pre = jnp.exp(prefix_mask(dot_nt(pk_ref[...], mine), count) - lse)
            dpre = dot_nt(pv_ref[...], grad)
            delta = jnp.sum(pre * dpre, axis=0, keepdims=True)
            for c in range(i + 1):
                keys = slice(c * BLOCK, (c + 1) * BLOCK)
                p = jnp.exp(token_mask(dot_nt(k_ref[keys, :], mine), start, i, c) - lse)
                dp = dot_nt(v_ref[keys, :], grad)
                delta = delta + jnp.sum(p * dp, axis=0, keepdims=True)
                p_ref[keys, :] = p
                dp_ref[keys, :] = dp
                dv_acc[keys, :] += dot(p.astype(low_type), grad)
            dpre = (pre * (dpre - delta)).astype(low_type)
            dpv_ref[...] += dot(pre.astype(low_type), grad)
            dpk_ref[...] += dot(dpre, mine)
            acc = dot(pkt_ref[feats, :], dpre)
            for c in range(i + 1):
                keys = slice(c * BLOCK, (c + 1) * BLOCK)
                ds = (p_ref[keys, :] * (dp_ref[keys, :] - delta)).astype(low_type)
                dk_acc[keys, :] += dot(ds, mine)
                acc = acc + dot(kt_ref[feats, keys], ds)
            parts.append(acc)
        dq_ref[rows, :] = (jnp.concatenate(parts, axis=0).T * (HEAD**-0.5)).astype(low_type)
    dk_ref[...] = dk_acc[...].astype(low_type)
    dv_ref[...] = dv_acc[...].astype(low_type)


def attention_forward(starts, qkv, pk, pv, count):
    length, width = qkv.shape[0], qkv.shape[1] // 3
    pairs = width // PAIR
    slab = lambda off: pl.BlockSpec((length, PAIR), lambda p: (0, p + off * pairs))
    small = pl.BlockSpec((PRE, PAIR), lambda p: (0, p))
    return pl.pallas_call(
        functools.partial(attention_forward_kernel, count),
        grid=(pairs,),
        in_specs=[
            pl.BlockSpec((1, length), lambda p: (0, 0)),
            slab(0),
            slab(1),
            slab(2),
            small,
            small,
        ],
        out_specs=[slab(0), pl.BlockSpec((1, 2, length), lambda p: (p, 0, 0))],
        out_shape=[
            jax.ShapeDtypeStruct((length, width), low_type),
            jax.ShapeDtypeStruct((pairs, 2, length), wide),
        ],
        scratch_shapes=[
            pltpu.VMEM((PAIR, length), low_type),
            pltpu.VMEM((PAIR, PRE), low_type),
            pltpu.VMEM((2, length, BLOCK), wide),
        ],
        compiler_params=pltpu.CompilerParams(vmem_limit_bytes=48 << 20),
        cost_estimate=pl.CostEstimate(flops=20_000_000_000, bytes_accessed=10 << 20, transcendentals=0),
    )(starts, qkv, qkv, qkv, pk, pv)


def attention_backward(starts, qkv, grad, pk, pv, lse, count):
    length, width = qkv.shape[0], qkv.shape[1] // 3
    pairs = width // PAIR
    slab = lambda off: pl.BlockSpec((length, PAIR), lambda p: (0, p + off * pairs))
    small = pl.BlockSpec((PRE, PAIR), lambda p: (0, p))
    whole = jax.ShapeDtypeStruct((length, width), low_type)
    return pl.pallas_call(
        functools.partial(attention_backward_kernel, count),
        grid=(pairs,),
        in_specs=[
            pl.BlockSpec((1, length), lambda p: (0, 0)),
            slab(0),
            slab(1),
            slab(2),
            slab(0),
            small,
            small,
            pl.BlockSpec((1, 2, length), lambda p: (p, 0, 0)),
        ],
        out_specs=[slab(0), slab(0), slab(0), small, small],
        out_shape=[whole] * 3 + [jax.ShapeDtypeStruct((PRE, width), wide)] * 2,
        scratch_shapes=[
            pltpu.VMEM((PAIR, length), low_type),
            pltpu.VMEM((PAIR, PRE), low_type),
            pltpu.VMEM((length, BLOCK), wide),
            pltpu.VMEM((length, BLOCK), wide),
            pltpu.VMEM((length, BLOCK), low_type),
            pltpu.VMEM((length, PAIR), wide),
            pltpu.VMEM((length, PAIR), wide),
        ],
        compiler_params=pltpu.CompilerParams(vmem_limit_bytes=48 << 20),
        cost_estimate=pl.CostEstimate(flops=40_000_000_000, bytes_accessed=20 << 20, transcendentals=0),
    )(starts, qkv, qkv, qkv, grad, pk, pv, lse)


def greet(peers):
    barrier = pltpu.get_barrier_semaphore()
    for peer in peers:
        pl.semaphore_signal(barrier, inc=1, device_id=peer, device_id_type=MESH)
    pl.semaphore_wait(barrier, len(peers))


def far_first(count):
    return sorted(range(1, count), key=lambda d: (abs(2 * d - count), d))


def arrive_kernel(
    n,
    x_hbm,
    starts_hbm,
    w_hbm,
    table_ref,
    w1_ref,
    b1_ref,
    w2_ref,
    b2_ref,
    gain_ref,
    shift_ref,
    bias_ref,
    x_out,
    starts_out,
    qkv_out,
    pk_out,
    pv_out,
    hidden_out,
    x_rows,
    h_rows,
    qkv_rows,
    w_rows,
    own_pre,
    pre_slots,
    x_send,
    x_recv,
    s_send,
    s_recv,
    p_send,
    p_recv,
    local_sem,
    store_sem,
):
    me = lax.axis_index("col")
    piece, width = x_hbm.shape[1], x_hbm.shape[2]
    greet([{"col": lax.rem(me + d, n)} for d in range(1, n)])
    mine = pl.ds(pl.multiple_of(me * piece, piece), piece)
    sends = []
    for d in far_first(n):
        peer = {"col": lax.rem(me + d, n)}
        copy = pltpu.make_async_remote_copy(
            src_ref=x_hbm.at[lax.rem(me + d, n)],
            dst_ref=x_rows.at[mine, :],
            send_sem=x_send.at[d],
            recv_sem=x_recv.at[d],
            device_id=peer,
            device_id_type=MESH,
        )
        copy.start()
        small = pltpu.make_async_remote_copy(
            src_ref=starts_hbm.at[lax.rem(me + d, n)],
            dst_ref=starts_out.at[me],
            send_sem=s_send.at[d],
            recv_sem=s_recv.at[d],
            device_id=peer,
            device_id_type=MESH,
        )
        small.start()
        sends += [(d, copy), (d, small)]
    own_x = pltpu.make_async_copy(x_hbm.at[me], x_rows.at[mine, :], local_sem.at[0])
    own_x.start()
    own_starts = pltpu.make_async_copy(starts_hbm.at[me], starts_out.at[me], local_sem.at[1])
    own_starts.start()
    load_w = pltpu.make_async_copy(w_hbm, w_rows, local_sem.at[2])
    load_w.start()

    hidden = jnp.tanh(dot(table_ref[...].astype(low_type), w1_ref[...].astype(low_type)) + b1_ref[...])
    rows = hidden.shape[0]
    hidden_out[...] = jnp.concatenate([hidden, jnp.zeros((PRE - rows, hidden.shape[1]), wide)], 0)
    own = dot(hidden.astype(low_type), w2_ref[...].astype(low_type)) + b2_ref[...]
    own = jnp.concatenate([own, jnp.zeros((PRE - rows, own.shape[1]), wide)], 0).astype(low_type)
    own_pre[...] = own
    pre_slots[me] = own
    for d in far_first(n):
        copy = pltpu.make_async_remote_copy(
            src_ref=own_pre,
            dst_ref=pre_slots.at[me],
            send_sem=p_send.at[d],
            recv_sem=p_recv.at[d],
            device_id={"col": lax.rem(me + d, n)},
            device_id_type=MESH,
        )
        copy.start()
        sends.append((d, copy))

    gain, shift = gain_ref[...].astype(wide), shift_ref[...].astype(wide)
    group = max(1, BLOCK // piece)
    order = [0] + far_first(n)[::-1]
    own_x.wait()
    load_w.wait()
    stores = []
    for g in range(0, n, group):
        spots = []
        for j, d in enumerate(order[g : g + group]):
            source = lax.rem(me + n - d, n)
            spot = pl.ds(pl.multiple_of(source * piece, piece), piece)
            spots.append(spot)
            if d:
                pltpu.make_async_remote_copy(
                    src_ref=x_hbm.at[source],
                    dst_ref=x_rows.at[spot, :],
                    send_sem=x_send.at[d],
                    recv_sem=x_recv.at[d],
                    device_id={"col": source},
                    device_id_type=MESH,
                ).wait_recv()
            store = pltpu.make_async_copy(x_rows.at[spot, :], x_out.at[spot, :], store_sem.at[0, d])
            store.start()
            stores.append(store)
            normed, _ = standardize(x_rows[spot, :].astype(wide))
            h_rows[j * piece : (j + 1) * piece, :] = (normed * gain + shift).astype(low_type)
        for c in range(0, 3 * width, width // 2):
            cols = slice(c, c + width // 2)
            part = dot(h_rows[...], w_rows[:, cols]) + bias_ref[:, cols].astype(wide)
            if c < width:
                part = part * (HEAD**-0.5)
            part = part.astype(low_type)
            for j, spot in enumerate(spots):
                qkv_rows[spot, cols] = part[j * piece : (j + 1) * piece, :]
        for j, d in enumerate(order[g : g + group]):
            store = pltpu.make_async_copy(
                qkv_rows.at[spots[j], :], qkv_out.at[spots[j], :], store_sem.at[1, d]
            )
            store.start()
            stores.append(store)
    for d in far_first(n):
        source = lax.rem(me + n - d, n)
        for src, dst, send, recv in (
            (starts_hbm.at[source], starts_out.at[source], s_send, s_recv),
            (own_pre, pre_slots.at[source], p_send, p_recv),
        ):
            pltpu.make_async_remote_copy(
                src_ref=src,
                dst_ref=dst,
                send_sem=send.at[d],
                recv_sem=recv.at[d],
                device_id={"col": source},
                device_id_type=MESH,
            ).wait_recv()
    part_width = own.shape[1]
    for j in range(n):
        lo = j * part_width
        if lo < width:
            pk_out[:, lo : lo + part_width] = pre_slots[j]
        else:
            pv_out[:, lo - width : lo - width + part_width] = pre_slots[j]
    for _, copy in sends:
        copy.wait_send()
    own_starts.wait()
    for store in stores:
        store.wait()


def arrive(inputs, starts, w_qkv, table, w1, b1, w2, b2, gain, shift, bias):
    n, piece, width = inputs.shape
    length = n * piece
    part_width = w2.shape[1]
    dma = pltpu.SemaphoreType.DMA
    return pl.pallas_call(
        functools.partial(arrive_kernel, n),
        in_specs=[ANY, ANY, ANY] + [VM] * 8,
        out_specs=[ANY, ANY, ANY, VM, VM, VM],
        out_shape=[
            jax.ShapeDtypeStruct((length, width), low_type),
            jax.ShapeDtypeStruct((n, 1, piece), jnp.int32),
            jax.ShapeDtypeStruct((length, 3 * width), low_type),
            jax.ShapeDtypeStruct((PRE, width), low_type),
            jax.ShapeDtypeStruct((PRE, width), low_type),
            jax.ShapeDtypeStruct((PRE, w1.shape[1]), wide),
        ],
        scratch_shapes=[
            pltpu.VMEM((length, width), low_type),
            pltpu.VMEM((BLOCK, width), low_type),
            pltpu.VMEM((length, 3 * width), low_type),
            pltpu.VMEM(w_qkv.shape, low_type),
            pltpu.VMEM((PRE, part_width), low_type),
            pltpu.VMEM((n, PRE, part_width), low_type),
            dma((n,)),
            dma((n,)),
            dma((n,)),
            dma((n,)),
            dma((n,)),
            dma((n,)),
            dma((3,)),
            dma((2, n)),
        ],
        compiler_params=pltpu.CompilerParams(
            collective_id=0, has_side_effects=True, vmem_limit_bytes=56 << 20
        ),
    )(inputs, starts, w_qkv, table, w1, b1, w2, b2, gain, shift, bias)


def leave_kernel(
    n,
    n_dp,
    dq_hbm,
    dk_hbm,
    dv_hbm,
    w_hbm,
    x_hbm,
    mid_hbm,
    gain_ref,
    dpk_ref,
    dpv_ref,
    hidden_ref,
    table_ref,
    w1_ref,
    w2_ref,
    grad_out,
    table_out,
    gw1_out,
    gb1_out,
    gw2_out,
    gb2_out,
    g_rows,
    w_rows,
    x_rows,
    mid_rows,
    staged,
    local_pre,
    col_slots,
    dp_own,
    dp_slots,
    hid_own,
    hid_slots,
    send_sem,
    recv_sem,
    c_send,
    c_recv,
    d_send,
    d_recv,
    h_send,
    h_recv,
    load_sem,
    local_sem,
):
    me = lax.axis_index("col")
    me_dp = lax.axis_index("dp")
    piece, width = grad_out.shape[1], grad_out.shape[2]
    length = n * piece
    loads = []
    for j, (src, dst) in enumerate(
        (
            (dq_hbm, g_rows.at[:, 0:width]),
            (dk_hbm, g_rows.at[:, width : 2 * width]),
            (dv_hbm, g_rows.at[:, 2 * width : 3 * width]),
            (w_hbm, w_rows),
            (x_hbm, x_rows),
            (mid_hbm, mid_rows),
        )
    ):
        load = pltpu.make_async_copy(src, dst, load_sem.at[j])
        load.start()
        loads.append(load)
    greet(
        [{"col": lax.rem(me + d, n)} for d in range(1, n)]
        + [{"dp": lax.rem(me_dp + d, n_dp)} for d in range(1, n_dp)]
    )
    part_width = w2_ref.shape[1]
    local_pre[:, 0:width] = dpk_ref[...]
    local_pre[:, width : 2 * width] = dpv_ref[...]
    sends = []

    def push(src, dst, send, recv, d, axis, me_at, count):
        copy = pltpu.make_async_remote_copy(
            src_ref=src,
            dst_ref=dst,
            send_sem=send.at[d],
            recv_sem=recv.at[d],
            device_id={axis: lax.rem(me_at + d, count)},
            device_id_type=MESH,
        )
        copy.start()
        sends.append(copy)

    def catch(src, dst, send, recv, d, axis, source):
        pltpu.make_async_remote_copy(
            src_ref=src,
            dst_ref=dst,
            send_sem=send.at[d],
            recv_sem=recv.at[d],
            device_id={axis: source},
            device_id_type=MESH,
        ).wait_recv()

    def slice_of(owner):
        return local_pre.at[:, pl.ds(pl.multiple_of(owner * part_width, part_width), part_width)]

    for d in far_first(n):
        push(slice_of(lax.rem(me + d, n)), col_slots.at[me], c_send, c_recv, d, "col", me, n)
    col_slots[me] = local_pre[:, pl.ds(pl.multiple_of(me * part_width, part_width), part_width)]
    for load in loads:
        load.wait()
    gain = gain_ref[...].astype(wide)
    hidden = hidden_ref[...]
    hidden_low = hidden.astype(low_type)
    w2_low = w2_ref[...].astype(low_type)

    def gradient_group(g, order):
        group = order[g : g + max(1, BLOCK // piece)]
        spots = [lax.rem(me + d, n) for d in group]
        parts = [
            g_rows[pl.ds(pl.multiple_of(spot * piece, piece), piece), :] for spot in spots
        ]
        block = jnp.concatenate(parts, axis=0)
        back = dot_nt(block, w_rows[...])
        for j, (d, spot) in enumerate(zip(group, spots)):
            rows = pl.ds(pl.multiple_of(spot * piece, piece), piece)
            normed, inverse = standardize(x_rows[rows, :].astype(wide))
            total = mid_rows[rows, :] + norm_backward_pass(
                back[j * piece : (j + 1) * piece, :], gain, normed, inverse
            )
            staged[d] = total.astype(low_type)
            if d:
                push(staged.at[d], grad_out.at[me], send_sem, recv_sem, d, "col", me, n)
            else:
                pltpu.make_async_copy(staged.at[0], grad_out.at[me], local_sem.at[0]).start()

    order = far_first(n) + [0]
    step = max(1, BLOCK // piece)
    groups = list(range(0, n, step))
    gradient_group(groups[0], order)
    for d in range(1, n):
        source = lax.rem(me + n - d, n)
        catch(slice_of(source), col_slots.at[source], c_send, c_recv, d, "col", source)
    total = col_slots[0]
    for j in range(1, n):
        total = total + col_slots[j]
    dp_own[...] = total
    dp_slots[me_dp] = total
    for d in range(1, n_dp):
        push(dp_own, dp_slots.at[me_dp], d_send, d_recv, d, "dp", me_dp, n_dp)
    gradient_group(groups[1], order)
    for d in range(1, n_dp):
        source = lax.rem(me_dp + n_dp - d, n_dp)
        catch(dp_own, dp_slots.at[source], d_send, d_recv, d, "dp", source)
    total = dp_slots[0]
    for j in range(1, n_dp):
        total = total + dp_slots[j]
    own_low = total.astype(low_type)
    part = dot_nt(own_low, w2_low)
    hid_own[...] = part
    hid_slots[me] = part
    for d in far_first(n):
        push(hid_own, hid_slots.at[me], h_send, h_recv, d, "col", me, n)
    for g in groups[2:]:
        gradient_group(g, order)
    gw2_out[...] = lax.dot_general(hidden_low, own_low, TN, preferred_element_type=wide)
    gb2_out[...] = jnp.sum(own_low.astype(wide), axis=0, keepdims=True)
    for d in range(1, n):
        source = lax.rem(me + n - d, n)
        catch(hid_own, hid_slots.at[source], h_send, h_recv, d, "col", source)
    total = hid_slots[0]
    for j in range(1, n):
        total = total + hid_slots[j]
    grad_pre = (total * (1.0 - hidden * hidden)).astype(low_type)
    rows = table_ref.shape[0]
    table = jnp.concatenate(
        [table_ref[...], jnp.zeros((PRE - rows, table_ref.shape[1]), wide)], 0
    ).astype(low_type)
    gw1_out[...] = lax.dot_general(table, grad_pre, TN, preferred_element_type=wide)
    gb1_out[...] = jnp.sum(grad_pre.astype(wide), axis=0, keepdims=True)
    table_out[...] = dot_nt(grad_pre, w1_ref[...].astype(low_type))[:rows, :]
    for d in range(1, n):
        source = lax.rem(me + n - d, n)
        catch(staged.at[d], grad_out.at[source], send_sem, recv_sem, d, "col", source)
    pltpu.make_async_copy(staged.at[0], grad_out.at[me], local_sem.at[0]).wait()
    for copy in sends:
        copy.wait_send()


def leave(n, n_dp, dq, dk, dv, w_qkv, rows, mid, gain, dpk, dpv, hidden, table, w1, w2):
    length, width = rows.shape
    piece = length // n
    part_width = w2.shape[1]
    dma = pltpu.SemaphoreType.DMA
    shape = jax.ShapeDtypeStruct
    return pl.pallas_call(
        functools.partial(leave_kernel, n, n_dp),
        in_specs=[ANY] * 6 + [VM] * 7,
        out_specs=[ANY] + [VM] * 5,
        out_shape=[
            shape((n, piece, width), low_type),
            shape(table.shape, wide),
            shape(w1.shape, wide),
            shape((1, w1.shape[1]), wide),
            shape(w2.shape, wide),
            shape((1, part_width), wide),
        ],
        scratch_shapes=[
            pltpu.VMEM((length, 3 * width), low_type),
            pltpu.VMEM(w_qkv.shape, low_type),
            pltpu.VMEM((length, width), low_type),
            pltpu.VMEM((length, width), wide),
            pltpu.VMEM((n, piece, width), low_type),
            pltpu.VMEM((PRE, 2 * width), wide),
            pltpu.VMEM((n, PRE, part_width), wide),
            pltpu.VMEM((PRE, part_width), wide),
            pltpu.VMEM((n_dp, PRE, part_width), wide),
            pltpu.VMEM((PRE, w1.shape[1]), wide),
            pltpu.VMEM((n, PRE, w1.shape[1]), wide),
            dma((n,)),
            dma((n,)),
            dma((n,)),
            dma((n,)),
            dma((n_dp,)),
            dma((n_dp,)),
            dma((n,)),
            dma((n,)),
            dma((6,)),
            dma((1,)),
        ],
        compiler_params=pltpu.CompilerParams(
            collective_id=1, has_side_effects=True, vmem_limit_bytes=56 << 20
        ),
    )(dq, dk, dv, w_qkv, rows, mid, gain, dpk, dpv, hidden, table, w1, w2)


def feed_forward_kernel(
    att_ref,
    x_ref,
    w_out_ref,
    b_out_ref,
    gain_ref,
    shift_ref,
    w_fc_ref,
    b_fc_ref,
    w_proj_ref,
    b_proj_ref,
    out_ref,
    mid_ref,
    slope_ref,
    h_ref,
    acc_ref,
):
    step = pl.program_id(0)
    chunks = [slice(r, r + 2 * BLOCK) for r in range(0, att_ref.shape[0], 2 * BLOCK)]

    @pl.when(step == 0)
    def _():
        for r in chunks:
            mid = x_ref[r, :].astype(wide) + dot(att_ref[r, :], w_out_ref[...])
            mid = mid + b_out_ref[...].astype(wide)
            mid_ref[r, :] = mid
            normed, _ = standardize(mid)
            h = normed * gain_ref[...].astype(wide) + shift_ref[...].astype(wide)
            h_ref[r, :] = h.astype(low_type)
            acc_ref[r, :] = mid + b_proj_ref[...].astype(wide)

    for r in chunks:
        upper = dot(h_ref[r, :], w_fc_ref[...]) + b_fc_ref[...].astype(wide)
        value, slope = gelu_parts(upper)
        slope_ref[r, :] = slope.astype(low_type)
        acc_ref[r, :] += dot(value.astype(low_type), w_proj_ref[...])

    @pl.when(step == pl.num_programs(0) - 1)
    def _():
        out_ref[...] = acc_ref[...].astype(low_type)


def feed_forward(att, rows, w_out, b_out, gain, shift, w_fc, b_fc, w_proj, b_proj):
    length, width = rows.shape
    inner = w_fc.shape[1]
    tile = min(1024, inner)
    full = lambda a: pl.BlockSpec(a.shape, lambda t: (0,) * a.ndim)
    whole = pl.BlockSpec((length, width), lambda t: (0, 0))
    return pl.pallas_call(
        feed_forward_kernel,
        grid=(inner // tile,),
        in_specs=[
            full(att),
            full(rows),
            full(w_out),
            full(b_out),
            full(gain),
            full(shift),
            pl.BlockSpec((width, tile), lambda t: (0, t)),
            pl.BlockSpec((1, tile), lambda t: (0, t)),
            pl.BlockSpec((tile, width), lambda t: (t, 0)),
            full(b_proj),
        ],
        out_specs=[whole, whole, pl.BlockSpec((length, tile), lambda t: (0, t))],
        out_shape=[
            jax.ShapeDtypeStruct((length, width), low_type),
            jax.ShapeDtypeStruct((length, width), wide),
            jax.ShapeDtypeStruct((length, inner), low_type),
        ],
        scratch_shapes=[pltpu.VMEM((length, width), low_type), pltpu.VMEM((length, width), wide)],
        compiler_params=pltpu.CompilerParams(vmem_limit_bytes=56 << 20),
        cost_estimate=pl.CostEstimate(
            flops=2 * length * width * (width + 2 * inner),
            bytes_accessed=40 << 20,
            transcendentals=length * inner,
        ),
    )(att, rows, w_out, b_out, gain, shift, w_fc, b_fc, w_proj, b_proj)


def feed_backward_kernel(
    cot_ref,
    slope_ref,
    w_proj_ref,
    w_fc_ref,
    mid_ref,
    gain_ref,
    w_out_ref,
    grad_mid_ref,
    grad_att_ref,
    acc_ref,
):
    step = pl.program_id(0)
    chunks = [slice(r, r + 2 * BLOCK) for r in range(0, cot_ref.shape[0], 2 * BLOCK)]

    @pl.when(step == 0)
    def _():
        acc_ref[...] = jnp.zeros_like(acc_ref)

    for r in chunks:
        grad_act = dot_nt(cot_ref[r, :], w_proj_ref[...])
        grad_upper = (grad_act * slope_ref[r, :].astype(wide)).astype(low_type)
        acc_ref[r, :] += dot_nt(grad_upper, w_fc_ref[...])

    @pl.when(step == pl.num_programs(0) - 1)
    def _():
        for r in chunks:
            normed, inverse = standardize(mid_ref[r, :])
            grad_mid = cot_ref[r, :].astype(wide) + norm_backward_pass(
                acc_ref[r, :], gain_ref[...].astype(wide), normed, inverse
            )
            grad_mid_ref[r, :] = grad_mid
            grad_att_ref[r, :] = dot_nt(grad_mid.astype(low_type), w_out_ref[...]).astype(low_type)


def feed_backward(cot, slope, w_proj, w_fc, mid, gain, w_out):
    length, width = cot.shape
    inner = w_fc.shape[1]
    tile = min(1024, inner)
    full = lambda a: pl.BlockSpec(a.shape, lambda t: (0,) * a.ndim)
    whole = pl.BlockSpec((length, width), lambda t: (0, 0))
    return pl.pallas_call(
        feed_backward_kernel,
        grid=(inner // tile,),
        in_specs=[
            full(cot),
            pl.BlockSpec((length, tile), lambda t: (0, t)),
            pl.BlockSpec((tile, width), lambda t: (t, 0)),
            pl.BlockSpec((width, tile), lambda t: (0, t)),
            full(mid),
            full(gain),
            full(w_out),
        ],
        out_specs=[whole, whole],
        out_shape=[
            jax.ShapeDtypeStruct((length, width), wide),
            jax.ShapeDtypeStruct((length, width), low_type),
        ],
        scratch_shapes=[pltpu.VMEM((length, width), wide)],
        compiler_params=pltpu.CompilerParams(vmem_limit_bytes=56 << 20),
        cost_estimate=pl.CostEstimate(
            flops=2 * length * width * (width + 2 * inner),
            bytes_accessed=40 << 20,
            transcendentals=0,
        ),
    )(cot, slope, w_proj, w_fc, mid, gain, w_out)


def exchange(values):
    return lax.all_to_all(values, "col", split_axis=0, concat_axis=0, tiled=True)


def on_device(
    inputs,
    starts,
    cotangent,
    first_norm_gain,
    shift_one,
    w_qkv,
    b_qkv,
    w_out,
    b_out,
    second_norm_gain,
    shift_two,
    w_fc,
    b_fc,
    w_proj,
    b_proj,
    prefix_table,
    rep_w1,
    rep_b1,
    rep_w2,
    rep_b2,
):
    col_count, dp_count = lax.axis_size("col"), lax.axis_size("dp")
    row_count, piece_len, model_width = inputs.shape
    assert row_count == col_count
    length = piece_len * col_count
    home = (col_count, piece_len, model_width)
    prefix_rows = prefix_table.shape[0]
    flat = lambda v: v.reshape(1, -1)

    rows, row_starts, qkv, pk, pv, hidden = arrive(
        inputs,
        starts.reshape(col_count, 1, piece_len),
        w_qkv,
        prefix_table,
        rep_w1,
        flat(rep_b1),
        rep_w2,
        flat(rep_b2),
        flat(first_norm_gain),
        flat(shift_one),
        flat(b_qkv),
    )
    cotangent, qkv = lax.optimization_barrier((cotangent, qkv))
    row_cot = exchange(cotangent).reshape(length, model_width)
    row_starts = row_starts.reshape(1, length)

    attended, lse = attention_forward(row_starts, qkv, pk, pv, prefix_rows)
    result, middle, slope = feed_forward(
        attended,
        rows,
        w_out,
        flat(b_out),
        flat(second_norm_gain),
        flat(shift_two),
        w_fc,
        flat(b_fc),
        w_proj,
        flat(b_proj),
    )
    output = exchange(result.reshape(home))

    grad_middle, grad_attended = feed_backward(
        row_cot, slope, w_proj, w_fc, middle, flat(second_norm_gain), w_out
    )
    dq, dk, dv, dpk, dpv = attention_backward(
        row_starts, qkv, grad_attended, pk, pv, lse, prefix_rows
    )
    dq, output = lax.optimization_barrier((dq, output))
    grad_input, grad_table, grad_w1, grad_b1, grad_w2, grad_b2 = leave(
        col_count,
        dp_count,
        dq,
        dk,
        dv,
        w_qkv,
        rows,
        grad_middle,
        flat(first_norm_gain),
        dpk,
        dpv,
        hidden,
        prefix_table,
        rep_w1,
        rep_w2,
    )
    return (
        output,
        grad_input,
        grad_table,
        grad_w1,
        grad_b1.reshape(-1),
        grad_w2,
        grad_b2.reshape(-1),
    )


def solution(mesh):
    rows = P("dp", "col", None)
    return jax.shard_map(
        on_device,
        mesh=mesh,
        in_specs=(rows, P("dp", "col"), rows) + (P(),) * 15 + (P(None, "col"), P("col")),
        out_specs=(rows, rows, P(), P(), P(), P(None, "col"), P("col")),
        check_vma=False,
    )
```

```python
import functools

import jax
import jax.numpy as jnp
from jax import lax
from jax.experimental import pallas as pl
from jax.experimental.pallas import tpu as pltpu
from jax.sharding import PartitionSpec as P

H = 16
HEAD = 64
PAIR = 2 * HEAD
BLOCK = 256
PRE = 16
VMEM_BYTES = 62 << 20

epsilon = 1e-05
gelu_coef = 0.7978845608028654
cubic_coef = 0.044715
low_type = jnp.bfloat16
wide = jnp.float32
NT = (((1,), (1,)), ((), ()))
TN = (((0,), (0,)), ((), ()))
MESH = pl.DeviceIdType.MESH
ANY = pl.BlockSpec(memory_space=pl.ANY)
VM = pl.BlockSpec(memory_space=pltpu.VMEM)


def standardize(values):
    center = values - jnp.mean(values, axis=-1, keepdims=True)
    inverse = lax.rsqrt(jnp.mean(center * center, axis=-1, keepdims=True) + epsilon)
    return center * inverse, inverse


def norm_backward_pass(gradient, norm_gain, normed, inverse):
    scaled = gradient * norm_gain
    centered = scaled - jnp.mean(scaled, axis=-1, keepdims=True)
    return inverse * (centered - normed * jnp.mean(scaled * normed, axis=-1, keepdims=True))


def gelu_parts(upper):
    square = upper * upper
    tangent = jnp.tanh(upper * (gelu_coef + (gelu_coef * cubic_coef) * square))
    half = 0.5 * upper
    share = 0.5 + 0.5 * tangent
    slope = share + half * (1.0 - tangent * tangent) * (
        gelu_coef + (3.0 * gelu_coef * cubic_coef) * square
    )
    return upper * share, slope


def dot_nt(a, b):
    return lax.dot_general(a, b, NT, preferred_element_type=wide)


def dot(a, b):
    return jnp.dot(a, b, preferred_element_type=wide)


def head_mask(values, which):
    lane = lax.broadcasted_iota(jnp.int32, values.shape, 1)
    keep = (lane < HEAD) if which == 0 else (lane >= HEAD)
    return jnp.where(keep, values, jnp.zeros_like(values))


def token_mask(scores, start, block_q, block_k):
    key = block_k * BLOCK + lax.broadcasted_iota(jnp.int32, scores.shape, 0)
    keep = key >= start
    if block_q == block_k:
        query = block_q * BLOCK + lax.broadcasted_iota(jnp.int32, scores.shape, 1)
        keep = keep & (key <= query)
    return jnp.where(keep, scores, -jnp.inf)


def prefix_mask(scores, count):
    key = lax.broadcasted_iota(jnp.int32, scores.shape, 0)
    return jnp.where(key < count, scores, -jnp.inf)


def masked(scores, count, start, block_q, block_k):
    if block_k < 0:
        return prefix_mask(scores, count)
    return token_mask(scores, start, block_q, block_k)


def key_chunks(block_q):
    tokens = [(c, PRE + c * BLOCK, PRE + (c + 1) * BLOCK) for c in range(block_q + 1)]
    return [(-1, 0, PRE)] + tokens


def transposed(values):
    return values.astype(wide).T.astype(low_type)


def attention_forward_pair(count, blocks, starts, q, k, v, pk, pv, out, lse, ke, vt, s_all, p_all, o_two):
    ke[0:PRE, :] = pk[...]
    ke[PRE:, :] = k[...]
    vt[:, 0:PRE] = transposed(pv[...])
    vt[:, PRE:] = transposed(v[...])
    units = [(i, h) for i in range(blocks) for h in range(2)]

    def view(u):
        return slice((u % 2) * BLOCK, (u % 2 + 1) * BLOCK)

    def score(u):
        i, h = units[u]
        rows = slice(i * BLOCK, (i + 1) * BLOCK)
        mine = head_mask(q[rows, :], h)
        start = starts[:, rows]
        peak = None
        for c, lo, hi in key_chunks(i):
            s = masked(dot_nt(ke[lo:hi, :], mine), count, start, i, c)
            s_all[lo:hi, view(u)] = s
            top = jnp.max(s, axis=0, keepdims=True)
            peak = top if peak is None else jnp.maximum(peak, top)
        return peak

    def weigh(u, peak):
        i, h = units[u]
        total = 0.0
        for _, lo, hi in key_chunks(i):
            p = jnp.exp(s_all[lo:hi, view(u)] - peak)
            total = total + jnp.sum(p, axis=0, keepdims=True)
            p_all[lo:hi, view(u)] = p.astype(low_type)
        lse[h : h + 1, i * BLOCK : (i + 1) * BLOCK] = peak + jnp.log(total)
        return total

    def collect(u, total):
        i, h = units[u]
        used = PRE + (i + 1) * BLOCK
        feats = slice(h * HEAD, (h + 1) * HEAD)
        o_two[i % 2, feats, :] = dot(vt[feats, 0:used], p_all[0:used, view(u)]) / total
        if h == 1:
            out[i * BLOCK : (i + 1) * BLOCK, :] = o_two[i % 2].T.astype(low_type)

    peak = score(0)
    for u in range(len(units)):
        following = score(u + 1) if u + 1 < len(units) else None
        total = weigh(u, peak)
        collect(u, total)
        peak = following


def attention_backward_pair(
    count, blocks, starts, q, k, v, g, pk, pv, lse, dpk, dpv, ke, ve, kt, s_all, dp_all, p_all, dk, dv
):
    ke[0:PRE, :] = pk[...]
    ke[PRE:, :] = k[...]
    ve[0:PRE, :] = pv[...]
    ve[PRE:, :] = v[...]
    kt[:, 0:PRE] = transposed(pk[...])
    kt[:, PRE:] = transposed(k[...])

    def place(i, h):
        first = (2 * (i % 2) + h) * BLOCK
        return slice(first, first + BLOCK)

    def score(i):
        rows = slice(i * BLOCK, (i + 1) * BLOCK)
        for h in range(2):
            mine, grad = head_mask(q[rows, :], h), head_mask(g[rows, :], h)
            for _, lo, hi in key_chunks(i):
                s_all[lo:hi, place(i, h)] = dot_nt(ke[lo:hi, :], mine)
                dp_all[lo:hi, place(i, h)] = dot_nt(ve[lo:hi, :], grad)

    def weigh(i):
        rows = slice(i * BLOCK, (i + 1) * BLOCK)
        start = starts[:, rows]
        for h in range(2):
            at = place(i, h)
            low_at = slice(at.start, at.stop)
            ds_at = slice(4 * BLOCK + at.start, 4 * BLOCK + at.stop)
            shift = lse[h : h + 1, rows]
            delta = 0.0
            for c, lo, hi in key_chunks(i):
                p = jnp.exp(masked(s_all[lo:hi, at], count, start, i, c) - shift)
                s_all[lo:hi, at] = p
                delta = delta + jnp.sum(p * dp_all[lo:hi, at], axis=0, keepdims=True)
                p_all[lo:hi, low_at] = p.astype(low_type)
            for _, lo, hi in key_chunks(i):
                ds = s_all[lo:hi, at] * (dp_all[lo:hi, at] - delta)
                p_all[lo:hi, ds_at] = ds.astype(low_type)

    def collect(i):
        rows = slice(i * BLOCK, (i + 1) * BLOCK)
        used = PRE + (i + 1) * BLOCK
        old = used - BLOCK if i else 0
        mine = jnp.concatenate([head_mask(q[rows, :], h) for h in range(2)], 0)
        grad = jnp.concatenate([head_mask(g[rows, :], h) for h in range(2)], 0)
        first = 2 * (i % 2) * BLOCK
        both = slice(first, first + 2 * BLOCK)
        ds_both = slice(4 * BLOCK + first, 4 * BLOCK + first + 2 * BLOCK)
        dv_part = dot(p_all[0:used, both], grad)
        dk_part = dot(p_all[0:used, ds_both], mine)
        if old:
            dv[0:old, :] += dv_part[:old]
            dk[0:old, :] += dk_part[:old]
        dv[old:used, :] = dv_part[old:]
        dk[old:used, :] = dk_part[old:]
        parts = []
        for h in range(2):
            feats = slice(h * HEAD, (h + 1) * HEAD)
            ds_at = slice(ds_both.start + h * BLOCK, ds_both.start + (h + 1) * BLOCK)
            parts.append(dot(kt[feats, 0:used], p_all[0:used, ds_at]))
        return (jnp.concatenate(parts, 0).T * (HEAD**-0.5)).astype(low_type)

    score(0)
    for i in range(blocks):
        if i + 1 < blocks:
            score(i + 1)
        weigh(i)
        dq = collect(i)
        q[i * BLOCK : (i + 1) * BLOCK, :] = dq
    k[...] = dk[PRE:, :].astype(low_type)
    v[...] = dv[PRE:, :].astype(low_type)
    dpk[...] = dk[:PRE, :]
    dpv[...] = dv[:PRE, :]


def far_first(count):
    return sorted(range(1, count), key=lambda d: (abs(2 * d - count), d))


def block_kernel(
    n,
    n_dp,
    x_hbm,
    starts_hbm,
    cot_hbm,
    w_qkv_hbm,
    w_out_hbm,
    w_fc_hbm,
    w_proj_hbm,
    gain1_ref,
    shift1_ref,
    b_qkv_ref,
    b_out_ref,
    gain2_ref,
    shift2_ref,
    b_fc_ref,
    b_proj_ref,
    table_ref,
    w1_ref,
    b1_ref,
    w2_ref,
    b2_ref,
    out_hbm,
    grad_hbm,
    table_out,
    gw1_out,
    gb1_out,
    gw2_out,
    gb2_out,
    x_rows,
    cot_rows,
    q_s,
    k_s,
    v_s,
    a_s,
    mid,
    h_rows,
    acc_a,
    acc_b,
    slope,
    w_qkv,
    w_out,
    w_fc,
    w_proj,
    lse,
    ke,
    ve,
    kt,
    dk,
    dv,
    starts_slots,
    starts_row,
    own_pre,
    pre_slots,
    pk_s,
    pv_s,
    hid,
    dp_pre,
    col_slots,
    dp_own,
    dp_slots,
    hid_own,
    hid_slots,
    o_two,
    x_send,
    x_recv,
    s_send,
    s_recv,
    p_send,
    p_recv,
    c_send,
    c_recv,
    o_send,
    o_recv,
    g_send,
    g_recv,
    r_send,
    r_recv,
    d_send,
    d_recv,
    e_send,
    e_recv,
    local_sem,
    fc_sem,
    proj_sem,
):
    me, me_dp = lax.axis_index("col"), lax.axis_index("dp")
    piece, width = x_hbm.shape[1], x_hbm.shape[2]
    length = n * piece
    blocks = length // BLOCK
    pairs = width // PAIR
    inner = b_fc_ref.shape[0]
    tile = w_fc.shape[2]
    tiles = inner // tile
    rows_pre = table_ref.shape[0]
    group = BLOCK // piece
    part_width = w2_ref.shape[1]
    per_part = part_width // PAIR
    far = far_first(n)

    def spot(at):
        return pl.ds(pl.multiple_of(at * piece, piece), piece)

    def to(d):
        return lax.rem(me + d, n)

    def source(d):
        return lax.rem(me + n - d, n)

    def remote(src, dst, send, recv, d, axis, peer):
        return pltpu.make_async_remote_copy(
            src_ref=src,
            dst_ref=dst,
            send_sem=send.at[d],
            recv_sem=recv.at[d],
            device_id={axis: peer},
            device_id_type=MESH,
        )

    def vector(ref):
        return ref[...].astype(wide).reshape(1, -1)

    def fc_load(t, slot):
        cols = pl.ds(pl.multiple_of(t * tile, tile), tile)
        return pltpu.make_async_copy(w_fc_hbm.at[:, cols], w_fc.at[slot], fc_sem.at[slot])

    def proj_load(t, slot):
        rows = pl.ds(pl.multiple_of(t * tile, tile), tile)
        return pltpu.make_async_copy(w_proj_hbm.at[rows, :], w_proj.at[slot], proj_sem.at[slot])

    load_qkv = pltpu.make_async_copy(w_qkv_hbm, w_qkv, local_sem.at[0])
    load_qkv.start()
    barrier = pltpu.get_barrier_semaphore()
    for d in range(1, n):
        pl.semaphore_signal(barrier, inc=1, device_id={"col": to(d)}, device_id_type=MESH)
    for d in range(1, n_dp):
        pl.semaphore_signal(
            barrier, inc=1, device_id={"dp": lax.rem(me_dp + d, n_dp)}, device_id_type=MESH
        )
    pl.semaphore_wait(barrier, n - 1 + n_dp - 1)

    x_sends, late = [], []
    for d in far:
        copy = remote(x_hbm.at[to(d)], x_rows.at[spot(me), :], x_send, x_recv, d, "col", to(d))
        copy.start()
        x_sends.append(copy)
        copy = remote(starts_hbm, starts_slots.at[me], s_send, s_recv, d, "col", to(d))
        copy.start()
        late.append(copy)
    own_x = pltpu.make_async_copy(x_hbm.at[me], x_rows.at[spot(me), :], local_sem.at[1])
    own_x.start()
    own_cot = pltpu.make_async_copy(cot_hbm.at[me], cot_rows.at[spot(me), :], local_sem.at[2])
    own_cot.start()
    own_starts = pltpu.make_async_copy(starts_hbm, starts_slots.at[me], local_sem.at[3])
    own_starts.start()
    load_out = pltpu.make_async_copy(w_out_hbm, w_out, local_sem.at[4])
    load_out.start()
    fc_load(0, 0).start()
    proj_load(0, 0).start()

    hidden = jnp.tanh(
        dot(table_ref[...].astype(low_type), w1_ref[...].astype(low_type)) + vector(b1_ref)
    )
    hid[...] = jnp.concatenate([hidden, jnp.zeros((PRE - rows_pre, hidden.shape[1]), wide)], 0)
    own = dot(hidden.astype(low_type), w2_ref[...].astype(low_type)) + vector(b2_ref)
    own = jnp.concatenate([own, jnp.zeros((PRE - rows_pre, part_width), wide)], 0).astype(low_type)
    own_pre[...] = own
    pre_slots[me] = own
    for d in far:
        copy = remote(own_pre, pre_slots.at[me], p_send, p_recv, d, "col", to(d))
        copy.start()
        late.append(copy)

    gain1, shift1 = vector(gain1_ref), vector(shift1_ref)
    near = [0] + far[::-1]
    own_x.wait()
    load_qkv.wait()
    cot_sends = []
    for at in range(0, n, group):
        members = near[at : at + group]
        if at + group >= n:
            for copy in x_sends:
                copy.wait_send()
            for d in far:
                copy = remote(
                    cot_hbm.at[to(d)], cot_rows.at[spot(me), :], c_send, c_recv, d, "col", to(d)
                )
                copy.start()
                cot_sends.append(copy)
        for j, d in enumerate(members):
            rows = spot(source(d))
            if d:
                remote(
                    x_hbm.at[me], x_rows.at[rows, :], x_send, x_recv, d, "col", source(d)
                ).wait_recv()
            normed, _ = standardize(x_rows[rows, :].astype(wide))
            h_rows[j * piece : (j + 1) * piece, :] = (normed * gain1 + shift1).astype(low_type)
        normed = h_rows[0:BLOCK, :]
        for c in range(0, 3 * width, width // 2):
            part = dot(normed, w_qkv[:, c : c + width // 2])
            part = part + b_qkv_ref[c : c + width // 2].astype(wide).reshape(1, -1)
            if c < width:
                part = part * (HEAD**-0.5)
            part = part.astype(low_type)
            slabs = (q_s, k_s, v_s)[c // width]
            for m in range(width // 2 // PAIR):
                pair = (c % width) // PAIR + m
                for j, d in enumerate(members):
                    slabs[pair, spot(source(d)), :] = part[
                        j * piece : (j + 1) * piece, m * PAIR : (m + 1) * PAIR
                    ]
    for d in far:
        remote(starts_hbm, starts_slots.at[source(d)], s_send, s_recv, d, "col", source(d)).wait_recv()
        remote(own_pre, pre_slots.at[source(d)], p_send, p_recv, d, "col", source(d)).wait_recv()
    own_starts.wait()
    for j in range(n):
        starts_row[:, j * piece : (j + 1) * piece] = starts_slots[j, pl.ds(me, 1), :]
        for m in range(per_part):
            pair = j * per_part + m
            slab = pre_slots[j][:, m * PAIR : (m + 1) * PAIR]
            if pair < pairs:
                pk_s[pair] = slab
            else:
                pv_s[pair - pairs] = slab

    def forward_pair(p, carry):
        attention_forward_pair(
            rows_pre,
            blocks,
            starts_row,
            q_s.at[p],
            k_s.at[p],
            v_s.at[p],
            pk_s.at[p],
            pv_s.at[p],
            a_s.at[p],
            lse.at[p],
            ke,
            kt,
            acc_a,
            slope,
            o_two,
        )
        return carry

    lax.fori_loop(0, pairs, forward_pair, 0)

    load_out.wait()
    gain2, shift2 = vector(gain2_ref), vector(shift2_ref)
    half = [slice(r, r + 2 * BLOCK) for r in range(0, length, 2 * BLOCK)]
    for r in half:
        att = jnp.concatenate([a_s[p, r, :] for p in range(pairs)], axis=1)
        middle = x_rows[r, :].astype(wide) + dot(att, w_out[...]) + vector(b_out_ref)
        mid[r, :] = middle
        normed, _ = standardize(middle)
        h_rows[r, :] = (normed * gain2 + shift2).astype(low_type)
        acc_a[r, :] = middle + vector(b_proj_ref)

    def forward_tile(t, carry):
        slot = lax.rem(t, 2)
        fc_load(t, slot).wait()
        proj_load(t, slot).wait()

        @pl.when(t + 1 < tiles)
        def _():
            fc_load(t + 1, 1 - slot).start()
            proj_load(t + 1, 1 - slot).start()

        cols = pl.ds(pl.multiple_of(t * tile, tile), tile)
        bias = b_fc_ref[cols].astype(wide).reshape(1, -1)
        for r in half:
            upper = dot(h_rows[r, :], w_fc[slot]) + bias
            value, steep = gelu_parts(upper)
            slope[r, cols] = steep.astype(low_type)
            acc_a[r, :] += dot(value.astype(low_type), w_proj[slot])
        return carry

    lax.fori_loop(0, tiles, forward_tile, 0)
    h_rows[...] = acc_a[0:length, :].astype(low_type)
    for d in far:
        copy = remote(
            h_rows.at[spot(to(d)), :], out_hbm.at[me], o_send, o_recv, d, "col", to(d)
        )
        copy.start()
        late.append(copy)
    own_out = pltpu.make_async_copy(h_rows.at[spot(me), :], out_hbm.at[me], local_sem.at[5])
    own_out.start()

    acc_a[...] = jnp.zeros_like(acc_a)
    own_cot.wait()
    for d in far:
        remote(
            cot_hbm.at[me], cot_rows.at[spot(source(d)), :], c_send, c_recv, d, "col", source(d)
        ).wait_recv()

    def backward_tile(step, carry):
        t = tiles - 1 - step
        slot = lax.rem(t, 2)

        @pl.when(step >= 2)
        def _():
            fc_load(t, slot).wait()
            proj_load(t, slot).wait()

        cols = pl.ds(pl.multiple_of(t * tile, tile), tile)
        for r in half:
            grad_act = dot_nt(cot_rows[r, :], w_proj[slot])
            grad_upper = (grad_act * slope[r, cols].astype(wide)).astype(low_type)
            acc_a[r, :] += dot_nt(grad_upper, w_fc[slot])

        @pl.when(t >= 2)
        def _():
            fc_load(t - 2, slot).start()
            proj_load(t - 2, slot).start()

        return carry

    lax.fori_loop(0, tiles, backward_tile, 0)
    for r in half:
        normed, inverse = standardize(mid[r, :])
        grad_mid = cot_rows[r, :].astype(wide) + norm_backward_pass(
            acc_a[r, :], gain2, normed, inverse
        )
        mid[r, :] = grad_mid
        grad_att = dot_nt(grad_mid.astype(low_type), w_out[...]).astype(low_type)
        for p in range(pairs):
            a_s[p, r, :] = grad_att[:, p * PAIR : (p + 1) * PAIR]

    def backward_pair(p, carry):
        attention_backward_pair(
            rows_pre,
            blocks,
            starts_row,
            q_s.at[p],
            k_s.at[p],
            v_s.at[p],
            a_s.at[p],
            pk_s.at[p],
            pv_s.at[p],
            lse.at[p],
            dp_pre.at[p],
            dp_pre.at[pairs + p],
            ke,
            ve,
            kt,
            acc_a,
            acc_b,
            slope,
            dk,
            dv,
        )
        return carry

    lax.fori_loop(0, pairs, backward_pair, 0)

    def own_part(owner):
        return dp_pre.at[pl.ds(owner * per_part, per_part)]

    for d in far:
        copy = remote(own_part(to(d)), col_slots.at[me], r_send, r_recv, d, "col", to(d))
        copy.start()
        late.append(copy)
    col_slots[me] = dp_pre[pl.ds(me * per_part, per_part)]
    order = far + [0]

    def gradient_group(at):
        members = order[at : at + group]
        grads = []
        for d in members:
            rows = spot(to(d))
            grads.append(
                jnp.concatenate(
                    [slabs[p, rows, :] for slabs in (q_s, k_s, v_s) for p in range(pairs)], axis=1
                )
            )
        back = dot_nt(jnp.concatenate(grads, axis=0), w_qkv[...])
        for j, d in enumerate(members):
            rows = spot(to(d))
            normed, inverse = standardize(x_rows[rows, :].astype(wide))
            total = mid[rows, :] + norm_backward_pass(
                back[j * piece : (j + 1) * piece, :], gain1, normed, inverse
            )
            here = cot_rows.at[d * piece : (d + 1) * piece, :]
            here[...] = total.astype(low_type)
            if d:
                copy = remote(here, grad_hbm.at[me], g_send, g_recv, d, "col", to(d))
                copy.start()
                late.append(copy)
            else:
                pltpu.make_async_copy(here, grad_hbm.at[me], local_sem.at[6]).start()

    hidden = hid[...]
    gradient_group(0)
    for d in far:
        remote(own_part(me), col_slots.at[source(d)], r_send, r_recv, d, "col", source(d)).wait_recv()
    total = col_slots[0]
    for j in range(1, n):
        total = total + col_slots[j]
    total = jnp.concatenate([total[m] for m in range(per_part)], axis=1)
    dp_own[...] = total
    dp_slots[me_dp] = total
    for d in range(1, n_dp):
        copy = remote(
            dp_own, dp_slots.at[me_dp], d_send, d_recv, d, "dp", lax.rem(me_dp + d, n_dp)
        )
        copy.start()
        late.append(copy)
    gradient_group(group)
    for d in range(1, n_dp):
        peer = lax.rem(me_dp + n_dp - d, n_dp)
        remote(dp_own, dp_slots.at[peer], d_send, d_recv, d, "dp", peer).wait_recv()
    total = dp_slots[0]
    for j in range(1, n_dp):
        total = total + dp_slots[j]
    own_low = total.astype(low_type)
    part = dot_nt(own_low, w2_ref[...].astype(low_type))
    hid_own[...] = part
    hid_slots[me] = part
    for d in far:
        copy = remote(hid_own, hid_slots.at[me], e_send, e_recv, d, "col", to(d))
        copy.start()
        late.append(copy)
    for at in range(2 * group, n, group):
        gradient_group(at)
    gw2_out[...] = lax.dot_general(
        hidden.astype(low_type), own_low, TN, preferred_element_type=wide
    )
    gb2_out[...] = jnp.sum(own_low.astype(wide), axis=0)
    for d in far:
        remote(hid_own, hid_slots.at[source(d)], e_send, e_recv, d, "col", source(d)).wait_recv()
    total = hid_slots[0]
    for j in range(1, n):
        total = total + hid_slots[j]
    grad_pre = (total * (1.0 - hidden * hidden)).astype(low_type)
    table = jnp.concatenate(
        [table_ref[...], jnp.zeros((PRE - rows_pre, table_ref.shape[1]), wide)], 0
    ).astype(low_type)
    gw1_out[...] = lax.dot_general(table, grad_pre, TN, preferred_element_type=wide)
    gb1_out[...] = jnp.sum(grad_pre.astype(wide), axis=0)
    table_out[...] = dot_nt(grad_pre, w1_ref[...].astype(low_type))[:rows_pre, :]

    here = cot_rows.at[0:piece, :]
    for d in far:
        remote(here, out_hbm.at[source(d)], o_send, o_recv, d, "col", source(d)).wait_recv()
        remote(here, grad_hbm.at[source(d)], g_send, g_recv, d, "col", source(d)).wait_recv()
    own_out.wait()
    pltpu.make_async_copy(here, grad_hbm.at[me], local_sem.at[6]).wait()
    for copy in cot_sends + late:
        copy.wait_send()


def on_device(*operands):
    n, n_dp = lax.axis_size("col"), lax.axis_size("dp")
    inputs, starts, cotangent, w_qkv, w_out = [operands[j] for j in (0, 1, 2, 5, 7)]
    w_fc, w_proj, table, w1, w2 = [operands[j] for j in (11, 13, 15, 16, 18)]
    row_count, piece, width = inputs.shape
    assert row_count == n and BLOCK % piece == 0
    length, inner = n * piece, w_fc.shape[1]
    pairs, tile = width // PAIR, min(1024, inner)
    part_width, mid_width = w2.shape[1], w1.shape[1]
    per_part = part_width // PAIR
    ext = PRE + length
    dma = pltpu.SemaphoreType.DMA
    shape = jax.ShapeDtypeStruct
    vmem = pltpu.VMEM
    slabs = vmem((pairs, length, PAIR), low_type)
    ordered = [operands[j] for j in (0, 1, 2, 5, 7, 11, 13)]
    ordered += [operands[j] for j in (3, 4, 6, 8, 9, 10, 12, 14, 15, 16, 17, 18, 19)]
    return tuple(
        pl.pallas_call(
            functools.partial(block_kernel, n, n_dp),
            in_specs=[ANY] * 7 + [VM] * 13,
            out_specs=[ANY, ANY] + [VM] * 5,
            out_shape=[
                shape((n, piece, width), low_type),
                shape((n, piece, width), low_type),
                shape(table.shape, wide),
                shape(w1.shape, wide),
                shape((mid_width,), wide),
                shape(w2.shape, wide),
                shape((part_width,), wide),
            ],
            scratch_shapes=[
                vmem((length, width), low_type),
                vmem((length, width), low_type),
                slabs,
                slabs,
                slabs,
                slabs,
                vmem((length, width), wide),
                vmem((length, width), low_type),
                vmem((ext, width), wide),
                vmem((ext, width), wide),
                vmem((ext, inner), low_type),
                vmem(w_qkv.shape, low_type),
                vmem(w_out.shape, low_type),
                vmem((2, width, tile), low_type),
                vmem((2, tile, width), low_type),
                vmem((pairs, 2, length), wide),
                vmem((ext, PAIR), low_type),
                vmem((ext, PAIR), low_type),
                vmem((PAIR, ext), low_type),
                vmem((ext, PAIR), wide),
                vmem((ext, PAIR), wide),
                vmem((n,) + starts.shape, jnp.int32),
                vmem((1, length), jnp.int32),
                vmem((PRE, part_width), low_type),
                vmem((n, PRE, part_width), low_type),
                vmem((pairs, PRE, PAIR), low_type),
                vmem((pairs, PRE, PAIR), low_type),
                vmem((PRE, mid_width), wide),
                vmem((2 * pairs, PRE, PAIR), wide),
                vmem((n, per_part, PRE, PAIR), wide),
                vmem((PRE, part_width), wide),
                vmem((n_dp, PRE, part_width), wide),
                vmem((PRE, mid_width), wide),
                vmem((n, PRE, mid_width), wide),
                vmem((2, PAIR, BLOCK), wide),
            ]
            + [dma((n,))] * 14
            + [dma((n_dp,))] * 2
            + [dma((n,))] * 2
            + [dma((7,)), dma((2,)), dma((2,))],
            compiler_params=pltpu.CompilerParams(
                collective_id=0, has_side_effects=True, vmem_limit_bytes=VMEM_BYTES
            ),
        )(*ordered)
    )


def solution(mesh):
    rows = P("dp", "col", None)
    return jax.shard_map(
        on_device,
        mesh=mesh,
        in_specs=(rows, P("dp", "col"), rows) + (P(),) * 15 + (P(None, "col"), P("col")),
        out_specs=(rows, rows, P(), P(), P(), P(None, "col"), P("col")),
        check_vma=False,
    )
```

```python
import functools

import jax
import jax.numpy as jnp
from jax import lax
from jax.experimental import pallas as pl
from jax.experimental.pallas import tpu as pltpu
from jax.sharding import PartitionSpec as P

H = 16
HEAD = 64
PAIR = 2 * HEAD
BLOCK = 256
PRE = 16
VMEM_BYTES = 62 << 20

epsilon = 1e-05
gelu_coef = 0.7978845608028654
cubic_coef = 0.044715
low_type = jnp.bfloat16
wide = jnp.float32
NT = (((1,), (1,)), ((), ()))
TN = (((0,), (0,)), ((), ()))
MESH = pl.DeviceIdType.MESH
ANY = pl.BlockSpec(memory_space=pl.ANY)
VM = pl.BlockSpec(memory_space=pltpu.VMEM)


def standardize(values):
    center = values - jnp.mean(values, axis=-1, keepdims=True)
    inverse = lax.rsqrt(jnp.mean(center * center, axis=-1, keepdims=True) + epsilon)
    return center * inverse, inverse


def norm_backward_pass(gradient, norm_gain, normed, inverse):
    scaled = gradient * norm_gain
    centered = scaled - jnp.mean(scaled, axis=-1, keepdims=True)
    return inverse * (centered - normed * jnp.mean(scaled * normed, axis=-1, keepdims=True))


def gelu_parts(upper):
    square = upper * upper
    tangent = jnp.tanh(upper * (gelu_coef + (gelu_coef * cubic_coef) * square))
    half = 0.5 * upper
    share = 0.5 + 0.5 * tangent
    slope = share + half * (1.0 - tangent * tangent) * (
        gelu_coef + (3.0 * gelu_coef * cubic_coef) * square
    )
    return upper * share, slope


def dot_nt(a, b):
    return lax.dot_general(a, b, NT, preferred_element_type=wide)


def dot(a, b):
    return jnp.dot(a, b, preferred_element_type=wide)


def head_mask(values, which):
    lane = lax.broadcasted_iota(jnp.int32, values.shape, 1)
    keep = (lane < HEAD) if which == 0 else (lane >= HEAD)
    return jnp.where(keep, values, jnp.zeros_like(values))


def token_mask(scores, start, block_q, block_k):
    key = block_k * BLOCK + lax.broadcasted_iota(jnp.int32, scores.shape, 0)
    keep = key >= start
    if block_q == block_k:
        query = block_q * BLOCK + lax.broadcasted_iota(jnp.int32, scores.shape, 1)
        keep = keep & (key <= query)
    return jnp.where(keep, scores, -jnp.inf)


def prefix_mask(scores, count):
    key = lax.broadcasted_iota(jnp.int32, scores.shape, 0)
    return jnp.where(key < count, scores, -jnp.inf)


def masked(scores, count, start, block_q, block_k):
    if block_k < 0:
        return prefix_mask(scores, count)
    return token_mask(scores, start, block_q, block_k)


def key_chunks(block_q):
    tokens = [(c, PRE + c * BLOCK, PRE + (c + 1) * BLOCK) for c in range(block_q + 1)]
    return [(-1, 0, PRE)] + tokens


def transposed(values):
    return values.astype(wide).T.astype(low_type)


def attention_forward_pair(count, blocks, starts, q, k, v, pk, pv, out, lse, ke, vt, s_all, p_all, o_two):
    ke[0:PRE, :] = pk[...]
    ke[PRE:, :] = k[...]
    vt[:, 0:PRE] = transposed(pv[...])
    vt[:, PRE:] = transposed(v[...])
    units = [(i, h) for i in range(blocks) for h in range(2)]

    def view(u):
        return slice((u % 2) * BLOCK, (u % 2 + 1) * BLOCK)

    def score(u):
        i, h = units[u]
        rows = slice(i * BLOCK, (i + 1) * BLOCK)
        mine = head_mask(q[rows, :], h)
        start = starts[:, rows]
        peak = None
        for c, lo, hi in key_chunks(i):
            s = masked(dot_nt(ke[lo:hi, :], mine), count, start, i, c)
            s_all[lo:hi, view(u)] = s
            top = jnp.max(s, axis=0, keepdims=True)
            peak = top if peak is None else jnp.maximum(peak, top)
        return peak

    def weigh(u, peak):
        i, h = units[u]
        total = 0.0
        for _, lo, hi in key_chunks(i):
            p = jnp.exp(s_all[lo:hi, view(u)] - peak)
            total = total + jnp.sum(p, axis=0, keepdims=True)
            p_all[lo:hi, view(u)] = p.astype(low_type)
        lse[h : h + 1, i * BLOCK : (i + 1) * BLOCK] = peak + jnp.log(total)
        return total

    def collect(u, total):
        i, h = units[u]
        used = PRE + (i + 1) * BLOCK
        feats = slice(h * HEAD, (h + 1) * HEAD)
        o_two[i % 2, feats, :] = dot(vt[feats, 0:used], p_all[0:used, view(u)]) / total
        if h == 1:
            out[i * BLOCK : (i + 1) * BLOCK, :] = o_two[i % 2].T.astype(low_type)

    peak = score(0)
    for u in range(len(units)):
        following = score(u + 1) if u + 1 < len(units) else None
        total = weigh(u, peak)
        collect(u, total)
        peak = following


def attention_backward_pair(
    count, blocks, starts, q, k, v, g, pk, pv, lse, delta, dpk, dpv, ke, ve, kt, p_all, dk, dv
):
    ke[0:PRE, :] = pk[...]
    ke[PRE:, :] = k[...]
    ve[0:PRE, :] = pv[...]
    ve[PRE:, :] = v[...]
    kt[:, 0:PRE] = transposed(pk[...])
    kt[:, PRE:] = transposed(k[...])
    length = blocks * BLOCK

    def weigh(i, h):
        rows = slice(i * BLOCK, (i + 1) * BLOCK)
        mine, grad = head_mask(q[rows, :], h), head_mask(g[rows, :], h)
        start = starts[:, rows]
        shift, middle = lse[h : h + 1, rows], delta[h : h + 1, rows]
        p_at = slice(h * length + i * BLOCK, h * length + (i + 1) * BLOCK)
        ds_at = slice((2 + h) * length + i * BLOCK, (2 + h) * length + (i + 1) * BLOCK)
        for c, lo, hi in key_chunks(i):
            s = masked(dot_nt(ke[lo:hi, :], mine), count, start, i, c)
            p = jnp.exp(s - shift)
            p_all[lo:hi, p_at] = p.astype(low_type)
            ds = p * (dot_nt(ve[lo:hi, :], grad) - middle)
            p_all[lo:hi, ds_at] = ds.astype(low_type)

    def collect_keys(c, h):
        lo, hi, first = (0, PRE, 0) if c < 0 else (PRE + c * BLOCK, PRE + (c + 1) * BLOCK, c * BLOCK)
        mine, grad = head_mask(q[first:length, :], h), head_mask(g[first:length, :], h)
        dv_part = dot(p_all[lo:hi, h * length + first : (h + 1) * length], grad)
        dk_part = dot(p_all[lo:hi, (2 + h) * length + first : (3 + h) * length], mine)
        if h == 0:
            dv[lo:hi, :] = dv_part
            dk[lo:hi, :] = dk_part
        elif c < 0:
            dpv[...] = dv[lo:hi, :] + dv_part
            dpk[...] = dk[lo:hi, :] + dk_part
        else:
            rows = slice(c * BLOCK, (c + 1) * BLOCK)
            v[rows, :] = (dv[lo:hi, :] + dv_part).astype(low_type)
            k[rows, :] = (dk[lo:hi, :] + dk_part).astype(low_type)

    def collect_queries(i, h):
        used = PRE + (i + 1) * BLOCK
        feats = slice(h * HEAD, (h + 1) * HEAD)
        ds_at = slice((2 + h) * length + i * BLOCK, (2 + h) * length + (i + 1) * BLOCK)
        return dot(kt[feats, 0:used], p_all[0:used, ds_at])

    for h in range(2):
        for i in range(blocks):
            weigh(i, h)
    for h in range(2):
        for c in range(-1, blocks):
            collect_keys(c, h)
    for i in range(blocks):
        both = jnp.concatenate([collect_queries(i, 0), collect_queries(i, 1)], 0)
        q[i * BLOCK : (i + 1) * BLOCK, :] = (both.T * (HEAD**-0.5)).astype(low_type)


def block_kernel(
    n,
    n_dp,
    x_hbm,
    starts_hbm,
    cot_hbm,
    w_qkv_hbm,
    w_out_hbm,
    w_fc_hbm,
    w_proj_hbm,
    gain1_ref,
    shift1_ref,
    b_qkv_ref,
    b_out_ref,
    gain2_ref,
    shift2_ref,
    b_fc_ref,
    b_proj_ref,
    table_ref,
    w1_ref,
    b1_ref,
    w2_ref,
    b2_ref,
    out_hbm,
    grad_hbm,
    table_out,
    gw1_out,
    gb1_out,
    gw2_out,
    gb2_out,
    x_rows,
    cot_rows,
    q_s,
    k_s,
    v_s,
    a_s,
    g_s,
    mid,
    h_rows,
    acc_a,
    slope,
    w_qkv,
    w_out,
    w_fc,
    w_proj,
    lse,
    delta,
    ke,
    ve,
    kt,
    dk,
    dv,
    starts_slots,
    starts_row,
    own_pre,
    pre_slots,
    pk_s,
    pv_s,
    hid,
    dp_pre,
    col_slots,
    dp_own,
    dp_own_low,
    dp_slots,
    hid_own,
    hid_slots,
    o_two,
    x_send,
    x_recv,
    s_send,
    s_recv,
    p_send,
    p_recv,
    c_send,
    c_recv,
    o_send,
    o_recv,
    g_send,
    g_recv,
    r_send,
    r_recv,
    d_send,
    d_recv,
    e_send,
    e_recv,
    local_sem,
    fc_sem,
    proj_sem,
    x_here,
    cot_here,
):
    me, me_dp = lax.axis_index("col"), lax.axis_index("dp")
    piece, width = x_hbm.shape[1], x_hbm.shape[2]
    length = n * piece
    blocks = length // BLOCK
    pairs = width // PAIR
    inner = b_fc_ref.shape[0]
    tile = w_fc.shape[2]
    tiles = inner // tile
    rows_pre = table_ref.shape[0]
    group = BLOCK // piece
    part_width = w2_ref.shape[1]
    per_part = part_width // PAIR
    groups = n // group
    heads = 2 * pairs

    def spot(at):
        return pl.ds(pl.multiple_of(at * piece, piece), piece)

    def near(k):
        odd, half = lax.rem(k, 2), lax.div(k + 1, 2)
        return odd * (n - half) + (1 - odd) * half

    def far(m):
        return near(n - 1 - m)

    def each(count, step):
        def body(k, carry):
            step(k)
            return carry

        lax.fori_loop(0, count, body, 0)

    def to(d):
        return lax.rem(me + d, n)

    def source(d):
        return lax.rem(me + n - d, n)

    def remote(src, dst, send, recv, d, axis, peer):
        return pltpu.make_async_remote_copy(
            src_ref=src,
            dst_ref=dst,
            send_sem=send.at[d],
            recv_sem=recv.at[d],
            device_id={axis: peer},
            device_id_type=MESH,
        )

    def vector(ref):
        return ref[...].astype(wide).reshape(1, -1)

    def fc_load(t, slot):
        cols = pl.ds(pl.multiple_of(t * tile, tile), tile)
        return pltpu.make_async_copy(w_fc_hbm.at[:, cols], w_fc.at[slot], fc_sem.at[slot])

    def proj_load(t, slot):
        rows = pl.ds(pl.multiple_of(t * tile, tile), tile)
        return pltpu.make_async_copy(w_proj_hbm.at[rows, :], w_proj.at[slot], proj_sem.at[slot])

    load_qkv = pltpu.make_async_copy(w_qkv_hbm, w_qkv, local_sem.at[0])
    load_qkv.start()
    barrier = pltpu.get_barrier_semaphore()
    for d in range(1, n):
        pl.semaphore_signal(barrier, inc=1, device_id={"col": to(d)}, device_id_type=MESH)
    for d in range(1, n_dp):
        pl.semaphore_signal(
            barrier, inc=1, device_id={"dp": lax.rem(me_dp + d, n_dp)}, device_id_type=MESH
        )
    pl.semaphore_wait(barrier, n - 1 + n_dp - 1)

    def x_copy(d, peer):
        return remote(x_hbm.at[peer], x_rows.at[spot(me), :], x_send, x_recv, d, "col", peer)

    def starts_copy(d, peer):
        return remote(starts_hbm, starts_slots.at[me], s_send, s_recv, d, "col", peer)

    def pre_copy(d, peer):
        return remote(own_pre, pre_slots.at[me], p_send, p_recv, d, "col", peer)

    def cot_copy(d, peer):
        return remote(cot_hbm.at[peer], cot_rows.at[spot(me), :], c_send, c_recv, d, "col", peer)

    def out_copy(d, peer):
        return remote(h_rows.at[spot(peer), :], out_hbm.at[me], o_send, o_recv, d, "col", peer)

    def grad_copy(d, here, peer):
        return remote(here, grad_hbm.at[me], g_send, g_recv, d, "col", peer)

    def send_inputs(m):
        x_copy(far(m), to(far(m))).start()
        starts_copy(far(m), to(far(m))).start()

    each(n - 1, send_inputs)
    own_x = pltpu.make_async_copy(x_hbm.at[me], x_rows.at[spot(me), :], local_sem.at[1])
    own_x.start()
    own_cot = pltpu.make_async_copy(cot_hbm.at[me], cot_rows.at[spot(me), :], local_sem.at[2])
    own_cot.start()
    own_starts = pltpu.make_async_copy(starts_hbm, starts_slots.at[me], local_sem.at[3])
    own_starts.start()
    load_out = pltpu.make_async_copy(w_out_hbm, w_out, local_sem.at[4])
    load_out.start()
    fc_load(0, 0).start()
    proj_load(0, 0).start()

    hidden = jnp.tanh(
        dot(table_ref[...].astype(low_type), w1_ref[...].astype(low_type)) + vector(b1_ref)
    )
    hid[...] = jnp.concatenate([hidden, jnp.zeros((PRE - rows_pre, hidden.shape[1]), wide)], 0)
    own = dot(hidden.astype(low_type), w2_ref[...].astype(low_type)) + vector(b2_ref)
    own = jnp.concatenate([own, jnp.zeros((PRE - rows_pre, part_width), wide)], 0).astype(low_type)
    own_pre[...] = own
    pre_slots[me] = own
    each(n - 1, lambda m: pre_copy(far(m), to(far(m))).start())

    gain1, shift1 = vector(gain1_ref), vector(shift1_ref)
    own_x.wait()
    load_qkv.wait()

    def greet_peers(sem):
        def greet(m):
            pl.semaphore_signal(sem, inc=1, device_id={"col": to(m + 1)}, device_id_type=MESH)

        each(n - 1, greet)

    def qkv_group(g):
        places = []
        for j in range(group):
            k = g * group + j
            d = near(k)
            rows = spot(source(d))
            places.append(rows)

            @pl.when(k > 0)
            def _():
                remote(
                    x_hbm.at[me], x_rows.at[rows, :], x_send, x_recv, d, "col", source(d)
                ).wait_recv()

            normed, _ = standardize(x_rows[rows, :].astype(wide))
            h_rows[j * piece : (j + 1) * piece, :] = (normed * gain1 + shift1).astype(low_type)

        @pl.when(g == groups - 1)
        def _():
            greet_peers(x_here)

        normed = h_rows[0:BLOCK, :]
        for c in range(0, 3 * width, width // 2):
            part = dot(normed, w_qkv[:, c : c + width // 2])
            part = part + b_qkv_ref[c : c + width // 2].astype(wide).reshape(1, -1)
            if c < width:
                part = part * (HEAD**-0.5)
            part = part.astype(low_type)
            slabs = (q_s, k_s, v_s)[c // width]
            for m in range(width // 2 // PAIR):
                pair = (c % width) // PAIR + m
                for j in range(group):
                    slabs[pair, places[j], :] = part[
                        j * piece : (j + 1) * piece, m * PAIR : (m + 1) * PAIR
                    ]

    each(groups, qkv_group)

    pl.semaphore_wait(x_here, n - 1)
    each(n - 1, lambda m: cot_copy(far(m), to(far(m))).start())

    def catch_small(m):
        d = m + 1
        peer = source(d)
        remote(starts_hbm, starts_slots.at[peer], s_send, s_recv, d, "col", peer).wait_recv()
        remote(own_pre, pre_slots.at[peer], p_send, p_recv, d, "col", peer).wait_recv()

    each(n - 1, catch_small)
    own_starts.wait()
    for j in range(n):
        starts_row[:, j * piece : (j + 1) * piece] = starts_slots[j, pl.ds(me, 1), :]
        for m in range(per_part):
            pair = j * per_part + m
            slab = pre_slots[j][:, m * PAIR : (m + 1) * PAIR]
            if pair < pairs:
                pk_s[pair] = slab
            else:
                pv_s[pair - pairs] = slab

    def forward_pair(p):
        attention_forward_pair(
            rows_pre,
            blocks,
            starts_row,
            q_s.at[p],
            k_s.at[p],
            v_s.at[p],
            pk_s.at[p],
            pv_s.at[p],
            a_s.at[p],
            lse.at[p],
            ke,
            kt,
            acc_a,
            slope,
            o_two,
        )

    each(pairs, forward_pair)

    load_out.wait()
    gain2, shift2 = vector(gain2_ref), vector(shift2_ref)
    big = 2 * BLOCK

    def project(b):
        r = pl.ds(pl.multiple_of(b * BLOCK, BLOCK), BLOCK)
        att = jnp.concatenate([a_s[p, r, :] for p in range(pairs)], axis=1)
        middle = x_rows[r, :].astype(wide) + dot(att, w_out[...]) + vector(b_out_ref)
        mid[r, :] = middle
        normed, _ = standardize(middle)
        h_rows[r, :] = (normed * gain2 + shift2).astype(low_type)
        acc_a[r, :] = middle + vector(b_proj_ref)

    each(blocks, project)

    def forward_tile(t):
        slot = lax.rem(t, 2)
        fc_load(t, slot).wait()
        proj_load(t, slot).wait()

        @pl.when(t + 1 < tiles)
        def _():
            fc_load(t + 1, 1 - slot).start()
            proj_load(t + 1, 1 - slot).start()

        cols = pl.ds(pl.multiple_of(t * tile, tile), tile)
        bias = b_fc_ref[cols].astype(wide).reshape(1, -1)

        def half(b):
            r = pl.ds(pl.multiple_of(b * big, big), big)
            upper = dot(h_rows[r, :], w_fc[slot]) + bias
            value, steep = gelu_parts(upper)
            slope[r, cols] = steep.astype(low_type)
            acc_a[r, :] += dot(value.astype(low_type), w_proj[slot])

        each(length // big, half)

    each(tiles, forward_tile)

    def settle(b):
        r = pl.ds(pl.multiple_of(b * BLOCK, BLOCK), BLOCK)
        h_rows[r, :] = acc_a[r, :].astype(low_type)
        acc_a[r, :] = jnp.zeros((BLOCK, width), wide)

    each(blocks, settle)
    own_out = pltpu.make_async_copy(h_rows.at[spot(me), :], out_hbm.at[me], local_sem.at[5])
    own_out.start()
    own_cot.wait()

    def catch_cot(m):
        d = m + 1
        peer = source(d)
        remote(
            cot_hbm.at[me], cot_rows.at[spot(peer), :], c_send, c_recv, d, "col", peer
        ).wait_recv()

    each(n - 1, catch_cot)
    greet_peers(cot_here)

    def backward_tile(step):
        t = tiles - 1 - step
        slot = lax.rem(t, 2)

        @pl.when(step >= 2)
        def _():
            fc_load(t, slot).wait()
            proj_load(t, slot).wait()

        @pl.when(step == 1)
        def _():
            pl.semaphore_wait(cot_here, n - 1)
            each(n - 1, lambda m: out_copy(far(m), to(far(m))).start())

        cols = pl.ds(pl.multiple_of(t * tile, tile), tile)

        def half(b):
            r = pl.ds(pl.multiple_of(b * big, big), big)
            grad_act = dot_nt(cot_rows[r, :], w_proj[slot])
            grad_upper = (grad_act * slope[r, cols].astype(wide)).astype(low_type)
            acc_a[r, :] += dot_nt(grad_upper, w_fc[slot])

        each(length // big, half)

        @pl.when(t >= 2)
        def _():
            fc_load(t - 2, slot).start()
            proj_load(t - 2, slot).start()

    each(tiles, backward_tile)
    feature_head = lax.broadcasted_iota(jnp.int32, (heads, width), 1) // HEAD
    which = lax.broadcasted_iota(jnp.int32, (heads, width), 0)
    member = jnp.where(feature_head == which, 1.0, 0.0).astype(low_type)

    def attend_gradient(b):
        r = pl.ds(pl.multiple_of(b * BLOCK, BLOCK), BLOCK)
        normed, inverse = standardize(mid[r, :])
        grad_mid = cot_rows[r, :].astype(wide) + norm_backward_pass(
            acc_a[r, :], gain2, normed, inverse
        )
        mid[r, :] = grad_mid
        grad_att = dot_nt(grad_mid.astype(low_type), w_out[...]).astype(low_type)
        att = jnp.concatenate([a_s[p, r, :] for p in range(pairs)], axis=1)
        both = grad_att.astype(wide) * att.astype(wide)
        both_low = both.astype(low_type)
        rest = (both - both_low.astype(wide)).astype(low_type)
        sums = dot_nt(member, both_low) + dot_nt(member, rest)
        for p in range(pairs):
            g_s[p, r, :] = grad_att[:, p * PAIR : (p + 1) * PAIR]
            delta[p, :, r] = sums[2 * p : 2 * p + 2, :]

    each(blocks, attend_gradient)

    def backward_pair(p):
        attention_backward_pair(
            rows_pre,
            blocks,
            starts_row,
            q_s.at[p],
            k_s.at[p],
            v_s.at[p],
            g_s.at[p],
            pk_s.at[p],
            pv_s.at[p],
            lse.at[p],
            delta.at[p],
            dp_pre.at[p],
            dp_pre.at[pairs + p],
            ke,
            ve,
            kt,
            slope,
            dk,
            dv,
        )

    each(pairs, backward_pair)

    def part_copy(d, peer):
        mine = dp_pre.at[pl.ds(peer * per_part, per_part)]
        return remote(mine, col_slots.at[me], r_send, r_recv, d, "col", peer)

    def dp_copy(d, peer):
        return remote(dp_own, dp_slots.at[me_dp], d_send, d_recv, d, "dp", peer)

    def hid_copy(d, peer):
        return remote(hid_own, hid_slots.at[me], e_send, e_recv, d, "col", peer)

    each(n - 1, lambda m: part_copy(far(m), to(far(m))).start())
    col_slots[me] = dp_pre[pl.ds(me * per_part, per_part)]

    def sum_slots(slots, count):
        return lax.fori_loop(1, count, lambda j, total: total + slots[j], slots[0])

    def gradient_group(g):
        grads, places = [], []
        for j in range(group):
            rows = spot(to(far(g * group + j)))
            places.append(rows)
            grads.append(
                jnp.concatenate(
                    [slabs[p, rows, :] for slabs in (q_s, k_s, v_s) for p in range(pairs)], axis=1
                )
            )
        back = dot_nt(jnp.concatenate(grads, axis=0), w_qkv[...])
        for j in range(group):
            at = g * group + j
            d = far(at)
            rows = places[j]
            normed, inverse = standardize(x_rows[rows, :].astype(wide))
            total = mid[rows, :] + norm_backward_pass(
                back[j * piece : (j + 1) * piece, :], gain1, normed, inverse
            )
            here = cot_rows.at[spot(at), :]
            here[...] = total.astype(low_type)

            @pl.when(at < n - 1)
            def _():
                grad_copy(d, here, to(d)).start()

            @pl.when(at == n - 1)
            def _():
                pltpu.make_async_copy(here, grad_hbm.at[me], local_sem.at[6]).start()

        @pl.when(g == 0)
        def _():
            def catch_part(m):
                d = m + 1
                peer = source(d)
                mine = dp_pre.at[pl.ds(me * per_part, per_part)]
                remote(mine, col_slots.at[peer], r_send, r_recv, d, "col", peer).wait_recv()

            each(n - 1, catch_part)
            total = sum_slots(col_slots, n)
            total = jnp.concatenate([total[m] for m in range(per_part)], axis=1)
            dp_own[...] = total
            dp_slots[me_dp] = total
            for d in range(1, n_dp):
                dp_copy(d, lax.rem(me_dp + d, n_dp)).start()

        @pl.when(g == 1)
        def _():
            for d in range(1, n_dp):
                peer = lax.rem(me_dp + n_dp - d, n_dp)
                remote(dp_own, dp_slots.at[peer], d_send, d_recv, d, "dp", peer).wait_recv()
            own_grad = sum_slots(dp_slots, n_dp)
            dp_own_low[...] = own_grad.astype(low_type)
            part = dot_nt(dp_own_low[...], w2_ref[...].astype(low_type))
            hid_own[...] = part
            hid_slots[me] = part
            each(n - 1, lambda m: hid_copy(far(m), to(far(m))).start())

    each(groups, gradient_group)
    hidden = hid[...]
    own_low = dp_own_low[...]
    gw2_out[...] = lax.dot_general(
        hidden.astype(low_type), own_low, TN, preferred_element_type=wide
    )
    gb2_out[...] = jnp.sum(own_low.astype(wide), axis=0)

    def catch_hid(m):
        d = m + 1
        peer = source(d)
        remote(hid_own, hid_slots.at[peer], e_send, e_recv, d, "col", peer).wait_recv()

    each(n - 1, catch_hid)
    grad_pre = (sum_slots(hid_slots, n) * (1.0 - hidden * hidden)).astype(low_type)
    table = jnp.concatenate(
        [table_ref[...], jnp.zeros((PRE - rows_pre, table_ref.shape[1]), wide)], 0
    ).astype(low_type)
    gw1_out[...] = lax.dot_general(table, grad_pre, TN, preferred_element_type=wide)
    gb1_out[...] = jnp.sum(grad_pre.astype(wide), axis=0)
    table_out[...] = dot_nt(grad_pre, w1_ref[...].astype(low_type))[:rows_pre, :]

    def finish(m):
        d = m + 1
        peer, here = source(d), cot_rows.at[0:piece, :]
        remote(here, out_hbm.at[peer], o_send, o_recv, d, "col", peer).wait_recv()
        remote(here, grad_hbm.at[peer], g_send, g_recv, d, "col", peer).wait_recv()
        x_copy(d, to(d)).wait_send()
        starts_copy(d, to(d)).wait_send()
        pre_copy(d, to(d)).wait_send()
        cot_copy(d, to(d)).wait_send()
        out_copy(d, to(d)).wait_send()
        grad_copy(d, here, to(d)).wait_send()
        part_copy(d, to(d)).wait_send()
        hid_copy(d, to(d)).wait_send()

    each(n - 1, finish)
    for d in range(1, n_dp):
        dp_copy(d, lax.rem(me_dp + d, n_dp)).wait_send()
    own_out.wait()
    pltpu.make_async_copy(cot_rows.at[0:piece, :], grad_hbm.at[me], local_sem.at[6]).wait()


def on_device(*operands):
    n, n_dp = lax.axis_size("col"), lax.axis_size("dp")
    inputs, starts, cotangent, w_qkv, w_out = [operands[j] for j in (0, 1, 2, 5, 7)]
    w_fc, w_proj, table, w1, w2 = [operands[j] for j in (11, 13, 15, 16, 18)]
    row_count, piece, width = inputs.shape
    assert row_count == n and BLOCK % piece == 0
    length, inner = n * piece, w_fc.shape[1]
    pairs, tile = width // PAIR, min(1024, inner)
    part_width, mid_width = w2.shape[1], w1.shape[1]
    per_part = part_width // PAIR
    ext = PRE + length
    dma = pltpu.SemaphoreType.DMA
    shape = jax.ShapeDtypeStruct
    vmem = pltpu.VMEM
    slabs = vmem((pairs, length, PAIR), low_type)
    ordered = [operands[j] for j in (0, 1, 2, 5, 7, 11, 13)]
    ordered += [operands[j] for j in (3, 4, 6, 8, 9, 10, 12, 14, 15, 16, 17, 18, 19)]
    return tuple(
        pl.pallas_call(
            functools.partial(block_kernel, n, n_dp),
            in_specs=[ANY] * 7 + [VM] * 13,
            out_specs=[ANY, ANY] + [VM] * 5,
            out_shape=[
                shape((n, piece, width), low_type),
                shape((n, piece, width), low_type),
                shape(table.shape, wide),
                shape(w1.shape, wide),
                shape((mid_width,), wide),
                shape(w2.shape, wide),
                shape((part_width,), wide),
            ],
            scratch_shapes=[
                vmem((length, width), low_type),
                vmem((length, width), low_type),
                slabs,
                slabs,
                slabs,
                slabs,
                slabs,
                vmem((length, width), wide),
                vmem((length, width), low_type),
                vmem((ext, width), wide),
                vmem((ext, inner), low_type),
                vmem(w_qkv.shape, low_type),
                vmem(w_out.shape, low_type),
                vmem((2, width, tile), low_type),
                vmem((2, tile, width), low_type),
                vmem((pairs, 2, length), wide),
                vmem((pairs, 2, length), wide),
                vmem((ext, PAIR), low_type),
                vmem((ext, PAIR), low_type),
                vmem((PAIR, ext), low_type),
                vmem((ext, PAIR), wide),
                vmem((ext, PAIR), wide),
                vmem((n,) + starts.shape, jnp.int32),
                vmem((1, length), jnp.int32),
                vmem((PRE, part_width), low_type),
                vmem((n, PRE, part_width), low_type),
                vmem((pairs, PRE, PAIR), low_type),
                vmem((pairs, PRE, PAIR), low_type),
                vmem((PRE, mid_width), wide),
                vmem((2 * pairs, PRE, PAIR), wide),
                vmem((n, per_part, PRE, PAIR), wide),
                vmem((PRE, part_width), wide),
                vmem((PRE, part_width), low_type),
                vmem((n_dp, PRE, part_width), wide),
                vmem((PRE, mid_width), wide),
                vmem((n, PRE, mid_width), wide),
                vmem((2, PAIR, BLOCK), wide),
            ]
            + [dma((n,))] * 14
            + [dma((n_dp,))] * 2
            + [dma((n,))] * 2
            + [dma((7,)), dma((2,)), dma((2,))]
            + [pltpu.SemaphoreType.REGULAR] * 2,
            compiler_params=pltpu.CompilerParams(
                collective_id=0, has_side_effects=True, vmem_limit_bytes=VMEM_BYTES
            ),
        )(*ordered)
    )


def solution(mesh):
    rows = P("dp", "col", None)
    return jax.shard_map(
        on_device,
        mesh=mesh,
        in_specs=(rows, P("dp", "col"), rows) + (P(),) * 15 + (P(None, "col"), P("col")),
        out_specs=(rows, rows, P(), P(), P(), P(None, "col"), P("col")),
        check_vma=False,
    )
```

```python
import functools

import jax
import jax.numpy as jnp
from jax import lax
from jax.experimental import pallas as pl
from jax.experimental.pallas import tpu as pltpu
from jax.sharding import PartitionSpec as P

H = 16
HEAD = 64
PAIR = 2 * HEAD
BLOCK = 256
PRE = 16
VMEM_BYTES = 62 << 20

epsilon = 1e-05
gelu_coef = 0.7978845608028654
cubic_coef = 0.044715
low_type = jnp.bfloat16
wide = jnp.float32
NT = (((1,), (1,)), ((), ()))
TN = (((0,), (0,)), ((), ()))
MESH = pl.DeviceIdType.MESH
ANY = pl.BlockSpec(memory_space=pl.ANY)
VM = pl.BlockSpec(memory_space=pltpu.VMEM)


def standardize(values):
    center = values - jnp.mean(values, axis=-1, keepdims=True)
    inverse = lax.rsqrt(jnp.mean(center * center, axis=-1, keepdims=True) + epsilon)
    return center * inverse, inverse


def norm_backward_pass(gradient, norm_gain, normed, inverse):
    scaled = gradient * norm_gain
    centered = scaled - jnp.mean(scaled, axis=-1, keepdims=True)
    return inverse * (centered - normed * jnp.mean(scaled * normed, axis=-1, keepdims=True))


def gelu_parts(upper):
    square = upper * upper
    tangent = jnp.tanh(upper * (gelu_coef + (gelu_coef * cubic_coef) * square))
    half = 0.5 * upper
    share = 0.5 + 0.5 * tangent
    slope = share + half * (1.0 - tangent * tangent) * (
        gelu_coef + (3.0 * gelu_coef * cubic_coef) * square
    )
    return upper * share, slope


def dot_nt(a, b):
    return lax.dot_general(a, b, NT, preferred_element_type=wide)


def dot(a, b):
    return jnp.dot(a, b, preferred_element_type=wide)


def head_mask(values, which):
    lane = lax.broadcasted_iota(jnp.int32, values.shape, 1)
    keep = (lane < HEAD) if which == 0 else (lane >= HEAD)
    return jnp.where(keep, values, jnp.zeros_like(values))


def token_mask(scores, start, block_q, block_k):
    key = block_k * BLOCK + lax.broadcasted_iota(jnp.int32, scores.shape, 0)
    keep = key >= start
    if block_q == block_k:
        query = block_q * BLOCK + lax.broadcasted_iota(jnp.int32, scores.shape, 1)
        keep = keep & (key <= query)
    return jnp.where(keep, scores, -jnp.inf)


def prefix_mask(scores, count):
    key = lax.broadcasted_iota(jnp.int32, scores.shape, 0)
    return jnp.where(key < count, scores, -jnp.inf)


def masked(scores, count, start, block_q, block_k):
    if block_k < 0:
        return prefix_mask(scores, count)
    return token_mask(scores, start, block_q, block_k)


def key_chunks(block_q):
    tokens = [(c, PRE + c * BLOCK, PRE + (c + 1) * BLOCK) for c in range(block_q + 1)]
    return [(-1, 0, PRE)] + tokens


def transposed(values):
    return values.astype(wide).T.astype(low_type)


def attention_forward_pair(count, blocks, starts, q, k, v, pk, pv, out, lse, ke, vt, s_all, p_all, o_two):
    ke[0:PRE, :] = pk[...]
    ke[PRE:, :] = k[...]
    vt[:, 0:PRE] = transposed(pv[...])
    vt[:, PRE:] = transposed(v[...])
    units = [(i, h) for i in range(blocks) for h in range(2)]

    def view(u):
        return slice((u % 2) * BLOCK, (u % 2 + 1) * BLOCK)

    def score(u):
        i, h = units[u]
        rows = slice(i * BLOCK, (i + 1) * BLOCK)
        mine = head_mask(q[rows, :], h)
        start = starts[:, rows]
        peak = None
        for c, lo, hi in key_chunks(i):
            s = masked(dot_nt(ke[lo:hi, :], mine), count, start, i, c)
            s_all[lo:hi, view(u)] = s
            top = jnp.max(s, axis=0, keepdims=True)
            peak = top if peak is None else jnp.maximum(peak, top)
        return peak

    def weigh(u, peak):
        i, h = units[u]
        total = 0.0
        for _, lo, hi in key_chunks(i):
            p = jnp.exp(s_all[lo:hi, view(u)] - peak)
            total = total + jnp.sum(p, axis=0, keepdims=True)
            p_all[lo:hi, view(u)] = p.astype(low_type)
        lse[h : h + 1, i * BLOCK : (i + 1) * BLOCK] = peak + jnp.log(total)
        return total

    def collect(u, total):
        i, h = units[u]
        used = PRE + (i + 1) * BLOCK
        feats = slice(h * HEAD, (h + 1) * HEAD)
        o_two[i % 2, feats, :] = dot(vt[feats, 0:used], p_all[0:used, view(u)]) / total
        if h == 1:
            out[i * BLOCK : (i + 1) * BLOCK, :] = o_two[i % 2].T.astype(low_type)

    peak = score(0)
    for u in range(len(units)):
        following = score(u + 1) if u + 1 < len(units) else None
        total = weigh(u, peak)
        collect(u, total)
        peak = following


FINAL, STORE, ADD = range(3)


def lower_first_part(blocks):
    low, high = range(blocks // 2), range(blocks // 2, blocks)
    work = [(i, range(-1, 0)) for i in low] + [(i, range(-1, i + 1)) for i in high]
    keys = [(c, range(c, blocks), FINAL) for c in high] + [(c, high, STORE) for c in low]
    keys += [(-1, range(blocks), FINAL)]
    return work, keys, [(i, range(-1, i + 1), FINAL) for i in high]


def lower_second_part(blocks):
    low = range(blocks // 2)
    work = [(i, range(-1, i + 1)) for i in low]
    keys = [(c, range(c, blocks // 2), ADD) for c in low]
    return work, keys, [(i, range(-1, i + 1), FINAL) for i in low]


def upper_first_part(blocks):
    half = blocks // 2
    work = [(i, range(-1, min(i + 1, half))) for i in range(blocks)]
    keys = [(c, range(max(c, 0), blocks), FINAL) for c in range(-1, half)]
    queries = [(i, chunks, FINAL if i < half else STORE) for i, chunks in work]
    return work, keys, queries


def upper_second_part(blocks):
    high = range(blocks // 2, blocks)
    work = [(i, range(blocks // 2, i + 1)) for i in high]
    keys = [(c, range(c, blocks), FINAL) for c in high]
    return work, keys, [(i, chunks, ADD) for i, chunks in work]


def key_rows(c):
    return (0, PRE) if c < 0 else (PRE + c * BLOCK, PRE + (c + 1) * BLOCK)


def attention_backward_part(
    plan, count, starts, q, k, v, g, pk, pv, lse, delta, dpk, dpv, ke, ve, kt, p_all, dk, dv, keep, keep_q
):
    work, keys, queries = plan
    length = q.shape[0]
    half = length // 2
    used = sorted({c for _, chunks in work for c in chunks})
    if used[0] < 0:
        ke[0:PRE, :] = pk[...]
        ve[0:PRE, :] = pv[...]
        kt[:, 0:PRE] = transposed(pk[...])
    first, last = max(used[0], 0) * BLOCK, (used[-1] + 1) * BLOCK
    ke[PRE + first : PRE + last, :] = k[first:last, :]
    ve[PRE + first : PRE + last, :] = v[first:last, :]
    kt[:, PRE + first : PRE + last] = transposed(k[first:last, :])

    def weigh(i, chunks, h):
        rows = slice(i * BLOCK, (i + 1) * BLOCK)
        mine, grad = head_mask(q[rows, :], h), head_mask(g[rows, :], h)
        start = starts[:, rows]
        shift, middle = lse[h : h + 1, rows], delta[h : h + 1, rows]
        p_at = slice(h * length + i * BLOCK, h * length + (i + 1) * BLOCK)
        ds_at = slice((2 + h) * length + i * BLOCK, (2 + h) * length + (i + 1) * BLOCK)
        for c in chunks:
            lo, hi = key_rows(c)
            s = masked(dot_nt(ke[lo:hi, :], mine), count, start, i, c)
            p = jnp.exp(s - shift)
            p_all[lo:hi, p_at] = p.astype(low_type)
            ds = p * (dot_nt(ve[lo:hi, :], grad) - middle)
            p_all[lo:hi, ds_at] = ds.astype(low_type)

    def collect_keys(c, members, mode, h):
        lo, hi = key_rows(c)
        a, b = members[0] * BLOCK, (members[-1] + 1) * BLOCK
        mine, grad = head_mask(q[a:b, :], h), head_mask(g[a:b, :], h)
        dv_part = dot(p_all[lo:hi, h * length + a : h * length + b], grad)
        dk_part = dot(p_all[lo:hi, (2 + h) * length + a : (2 + h) * length + b], mine)
        if h == 0:
            dv[lo:hi, :] = dv_part
            dk[lo:hi, :] = dk_part
            return
        dv_part = dv[lo:hi, :] + dv_part
        dk_part = dk[lo:hi, :] + dk_part
        if c < 0:
            dpv[...] = dv_part
            dpk[...] = dk_part
            return
        rows = slice(c * BLOCK, (c + 1) * BLOCK)
        if mode == STORE:
            keep[rows, :] = dk_part
            keep[half + rows.start : half + rows.stop, :] = dv_part
            return
        if mode == ADD:
            dk_part = dk_part + keep[rows, :]
            dv_part = dv_part + keep[half + rows.start : half + rows.stop, :]
        v[rows, :] = dv_part.astype(low_type)
        k[rows, :] = dk_part.astype(low_type)

    def collect_queries(i, chunks, mode):
        lo, hi = key_rows(chunks[0])[0], key_rows(chunks[-1])[1]
        parts = []
        for h in range(2):
            feats = slice(h * HEAD, (h + 1) * HEAD)
            ds_at = slice((2 + h) * length + i * BLOCK, (2 + h) * length + (i + 1) * BLOCK)
            parts.append(dot(kt[feats, lo:hi], p_all[lo:hi, ds_at]))
        both = jnp.concatenate(parts, 0)
        kept = slice(i * BLOCK - half, (i + 1) * BLOCK - half)
        if mode == STORE:
            keep_q[:, kept] = both
            return
        if mode == ADD:
            both = both + keep_q[:, kept]
        q[i * BLOCK : (i + 1) * BLOCK, :] = (both.T * (HEAD**-0.5)).astype(low_type)

    for h in range(2):
        for i, chunks in work:
            weigh(i, chunks, h)
    for h in range(2):
        for c, members, mode in keys:
            collect_keys(c, members, mode, h)
    for i, chunks, mode in queries:
        collect_queries(i, chunks, mode)


def block_kernel(
    n,
    n_dp,
    x_hbm,
    starts_hbm,
    cot_hbm,
    w_qkv_hbm,
    w_out_hbm,
    w_fc_hbm,
    w_proj_hbm,
    gain1_ref,
    shift1_ref,
    b_qkv_ref,
    b_out_ref,
    gain2_ref,
    shift2_ref,
    b_fc_ref,
    b_proj_ref,
    table_ref,
    w1_ref,
    b1_ref,
    w2_ref,
    b2_ref,
    out_hbm,
    grad_hbm,
    table_out,
    gw1_out,
    gb1_out,
    gw2_out,
    gb2_out,
    x_rows,
    cot_rows,
    q_s,
    k_s,
    v_s,
    a_s,
    g_s,
    mid,
    h_rows,
    acc_a,
    slope,
    w_qkv,
    w_out,
    w_fc,
    w_proj,
    lse,
    delta,
    ke,
    ve,
    kt,
    dk,
    dv,
    starts_slots,
    starts_row,
    own_pre,
    pre_slots,
    pk_s,
    pv_s,
    hid,
    dp_pre,
    col_slots,
    dp_own,
    dp_slots,
    hid_own,
    hid_slots,
    o_two,
    x_send,
    x_recv,
    s_send,
    s_recv,
    p_send,
    p_recv,
    c_send,
    c_recv,
    o_send,
    o_recv,
    g_send,
    g_recv,
    r_send,
    r_recv,
    d_send,
    d_recv,
    e_send,
    e_recv,
    local_sem,
    fc_sem,
    proj_sem,
    x_here,
    cot_here,
):
    me, me_dp = lax.axis_index("col"), lax.axis_index("dp")
    piece, width = x_hbm.shape[1], x_hbm.shape[2]
    length = n * piece
    blocks = length // BLOCK
    pairs = width // PAIR
    inner = b_fc_ref.shape[0]
    tile = w_fc.shape[2]
    tiles = inner // tile
    rows_pre = table_ref.shape[0]
    group = BLOCK // piece
    part_width = w2_ref.shape[1]
    per_part = part_width // PAIR
    groups = n // group
    heads = 2 * pairs

    def spot(at):
        return pl.ds(pl.multiple_of(at * piece, piece), piece)

    def each(count, step):
        def body(k, carry):
            step(k)
            return carry

        lax.fori_loop(0, count, body, 0)

    reach = n // 2
    mine_base = lax.div(me, reach) * reach
    other_base = reach - mine_base
    seat = lax.rem(me, reach)

    def peer_at(m, sign):
        same = lax.div(m, reach)
        step = lax.rem(m, reach) + same
        base = other_base + same * (mine_base - other_base)
        return base + lax.rem(seat + 2 * reach + sign * step, reach)

    def to(m):
        return peer_at(m, 1)

    def source(m):
        return peer_at(m, -1)

    def remote(src, dst, send, recv, d, axis, peer):
        return pltpu.make_async_remote_copy(
            src_ref=src,
            dst_ref=dst,
            send_sem=send.at[d],
            recv_sem=recv.at[d],
            device_id={axis: peer},
            device_id_type=MESH,
        )

    def vector(ref):
        return ref[...].astype(wide).reshape(1, -1)

    def fc_load(t, slot):
        cols = pl.ds(pl.multiple_of(t * tile, tile), tile)
        return pltpu.make_async_copy(w_fc_hbm.at[:, cols], w_fc.at[slot], fc_sem.at[slot])

    def proj_load(t, slot):
        rows = pl.ds(pl.multiple_of(t * tile, tile), tile)
        return pltpu.make_async_copy(w_proj_hbm.at[rows, :], w_proj.at[slot], proj_sem.at[slot])

    load_qkv = pltpu.make_async_copy(w_qkv_hbm, w_qkv, local_sem.at[0])
    load_qkv.start()
    barrier = pltpu.get_barrier_semaphore()
    for m in range(n - 1):
        peer = to(jnp.int32(m))
        pl.semaphore_signal(barrier, inc=1, device_id={"col": peer}, device_id_type=MESH)
    for d in range(1, n_dp):
        pl.semaphore_signal(
            barrier, inc=1, device_id={"dp": lax.rem(me_dp + d, n_dp)}, device_id_type=MESH
        )
    pl.semaphore_wait(barrier, n - 1 + n_dp - 1)

    def x_copy(d, peer):
        return remote(x_hbm.at[peer], x_rows.at[spot(me), :], x_send, x_recv, d, "col", peer)

    def starts_copy(d, peer):
        return remote(starts_hbm, starts_slots.at[me], s_send, s_recv, d, "col", peer)

    def pre_copy(d, peer):
        return remote(own_pre, pre_slots.at[me], p_send, p_recv, d, "col", peer)

    def cot_copy(d, peer):
        return remote(cot_hbm.at[peer], cot_rows.at[spot(me), :], c_send, c_recv, d, "col", peer)

    def out_copy(d, peer):
        return remote(h_rows.at[spot(peer), :], out_hbm.at[me], o_send, o_recv, d, "col", peer)

    def grad_copy(d, here, peer):
        return remote(here, grad_hbm.at[me], g_send, g_recv, d, "col", peer)

    def send_inputs(m):
        x_copy(m, to(m)).start()
        starts_copy(m, to(m)).start()

    each(n - 1, send_inputs)
    own_x = pltpu.make_async_copy(x_hbm.at[me], x_rows.at[spot(me), :], local_sem.at[1])
    own_x.start()
    own_cot = pltpu.make_async_copy(cot_hbm.at[me], cot_rows.at[spot(me), :], local_sem.at[2])
    own_cot.start()
    own_starts = pltpu.make_async_copy(starts_hbm, starts_slots.at[me], local_sem.at[3])
    own_starts.start()
    load_out = pltpu.make_async_copy(w_out_hbm, w_out, local_sem.at[4])
    load_out.start()
    fc_load(0, 0).start()
    proj_load(0, 0).start()

    hidden = jnp.tanh(
        dot(table_ref[...].astype(low_type), w1_ref[...].astype(low_type)) + vector(b1_ref)
    )
    hid[...] = jnp.concatenate([hidden, jnp.zeros((PRE - rows_pre, hidden.shape[1]), wide)], 0)
    own = dot(hidden.astype(low_type), w2_ref[...].astype(low_type)) + vector(b2_ref)
    own = jnp.concatenate([own, jnp.zeros((PRE - rows_pre, part_width), wide)], 0).astype(low_type)
    own_pre[...] = own
    pre_slots[me] = own
    each(n - 1, lambda m: pre_copy(m, to(m)).start())

    gain1, shift1 = vector(gain1_ref), vector(shift1_ref)
    own_x.wait()
    load_qkv.wait()

    def greet_peers(sem):
        def greet(m):
            pl.semaphore_signal(sem, inc=1, device_id={"col": to(m)}, device_id_type=MESH)

        each(n - 1, greet)

    def qkv_group(g):
        places = []
        for j in range(group):
            d = n - 1 - (g * group + j)
            rows = spot(source(d))
            places.append(rows)

            @pl.when(d < n - 1)
            def _():
                remote(
                    x_hbm.at[me], x_rows.at[rows, :], x_send, x_recv, d, "col", source(d)
                ).wait_recv()

            normed, _ = standardize(x_rows[rows, :].astype(wide))
            h_rows[j * piece : (j + 1) * piece, :] = (normed * gain1 + shift1).astype(low_type)

        @pl.when(g == groups - 1)
        def _():
            greet_peers(x_here)

        normed = h_rows[0:BLOCK, :]
        for c in range(0, 3 * width, width // 2):
            part = dot(normed, w_qkv[:, c : c + width // 2])
            part = part + b_qkv_ref[c : c + width // 2].astype(wide).reshape(1, -1)
            if c < width:
                part = part * (HEAD**-0.5)
            part = part.astype(low_type)
            slabs = (q_s, k_s, v_s)[c // width]
            for m in range(width // 2 // PAIR):
                pair = (c % width) // PAIR + m
                for j in range(group):
                    slabs[pair, places[j], :] = part[
                        j * piece : (j + 1) * piece, m * PAIR : (m + 1) * PAIR
                    ]

    each(groups, qkv_group)

    pl.semaphore_wait(x_here, n - 1)
    each(n - 1, lambda m: cot_copy(m, to(m)).start())

    def catch_small(m):
        d = m
        peer = source(d)
        remote(starts_hbm, starts_slots.at[peer], s_send, s_recv, d, "col", peer).wait_recv()
        remote(own_pre, pre_slots.at[peer], p_send, p_recv, d, "col", peer).wait_recv()

    each(n - 1, catch_small)
    own_starts.wait()
    for j in range(n):
        starts_row[:, j * piece : (j + 1) * piece] = starts_slots[j, pl.ds(me, 1), :]
        for m in range(per_part):
            pair = j * per_part + m
            slab = pre_slots[j][:, m * PAIR : (m + 1) * PAIR]
            if pair < pairs:
                pk_s[pair] = slab
            else:
                pv_s[pair - pairs] = slab

    def forward_pair(p):
        attention_forward_pair(
            rows_pre,
            blocks,
            starts_row,
            q_s.at[p],
            k_s.at[p],
            v_s.at[p],
            pk_s.at[p],
            pv_s.at[p],
            a_s.at[p],
            lse.at[p],
            ke,
            kt,
            acc_a,
            slope,
            o_two,
        )

    each(pairs, forward_pair)

    load_out.wait()
    gain2, shift2 = vector(gain2_ref), vector(shift2_ref)
    big = 2 * BLOCK

    def project(b):
        r = pl.ds(pl.multiple_of(b * BLOCK, BLOCK), BLOCK)
        att = jnp.concatenate([a_s[p, r, :] for p in range(pairs)], axis=1)
        middle = x_rows[r, :].astype(wide) + dot(att, w_out[...]) + vector(b_out_ref)
        mid[r, :] = middle
        normed, _ = standardize(middle)
        h_rows[r, :] = (normed * gain2 + shift2).astype(low_type)
        acc_a[r, :] = middle + vector(b_proj_ref)

    each(blocks, project)

    def forward_tile(t):
        slot = lax.rem(t, 2)
        fc_load(t, slot).wait()
        proj_load(t, slot).wait()

        @pl.when(t + 1 < tiles)
        def _():
            fc_load(t + 1, 1 - slot).start()
            proj_load(t + 1, 1 - slot).start()

        cols = pl.ds(pl.multiple_of(t * tile, tile), tile)
        bias = b_fc_ref[cols].astype(wide).reshape(1, -1)

        def half(b):
            r = pl.ds(pl.multiple_of(b * big, big), big)
            upper = dot(h_rows[r, :], w_fc[slot]) + bias
            value, steep = gelu_parts(upper)
            slope[r, cols] = steep.astype(low_type)
            acc_a[r, :] += dot(value.astype(low_type), w_proj[slot])

        each(length // big, half)

    each(tiles, forward_tile)

    def settle(b):
        r = pl.ds(pl.multiple_of(b * BLOCK, BLOCK), BLOCK)
        h_rows[r, :] = acc_a[r, :].astype(low_type)
        acc_a[r, :] = jnp.zeros((BLOCK, width), wide)

    each(blocks, settle)
    own_out = pltpu.make_async_copy(h_rows.at[spot(me), :], out_hbm.at[me], local_sem.at[5])
    own_out.start()
    own_cot.wait()

    def catch_cot(m):
        d = m
        peer = source(d)
        remote(
            cot_hbm.at[me], cot_rows.at[spot(peer), :], c_send, c_recv, d, "col", peer
        ).wait_recv()

    each(n - 1, catch_cot)
    greet_peers(cot_here)

    def backward_tile(step):
        t = tiles - 1 - step
        slot = lax.rem(t, 2)

        @pl.when(step >= 2)
        def _():
            fc_load(t, slot).wait()
            proj_load(t, slot).wait()

        @pl.when(step == 1)
        def _():
            pl.semaphore_wait(cot_here, n - 1)
            each(n - 1, lambda m: out_copy(m, to(m)).start())

        cols = pl.ds(pl.multiple_of(t * tile, tile), tile)

        def half(b):
            r = pl.ds(pl.multiple_of(b * big, big), big)
            grad_act = dot_nt(cot_rows[r, :], w_proj[slot])
            grad_upper = (grad_act * slope[r, cols].astype(wide)).astype(low_type)
            acc_a[r, :] += dot_nt(grad_upper, w_fc[slot])

        each(length // big, half)

        @pl.when(t >= 2)
        def _():
            fc_load(t - 2, slot).start()
            proj_load(t - 2, slot).start()

    each(tiles, backward_tile)
    feature_head = lax.broadcasted_iota(jnp.int32, (heads, width), 1) // HEAD
    which = lax.broadcasted_iota(jnp.int32, (heads, width), 0)
    member = jnp.where(feature_head == which, 1.0, 0.0).astype(low_type)

    def attend_gradient(b):
        r = pl.ds(pl.multiple_of(b * BLOCK, BLOCK), BLOCK)
        normed, inverse = standardize(mid[r, :])
        grad_mid = cot_rows[r, :].astype(wide) + norm_backward_pass(
            acc_a[r, :], gain2, normed, inverse
        )
        mid[r, :] = grad_mid
        grad_att = dot_nt(grad_mid.astype(low_type), w_out[...]).astype(low_type)
        att = jnp.concatenate([a_s[p, r, :] for p in range(pairs)], axis=1)
        both = grad_att.astype(wide) * att.astype(wide)
        both_low = both.astype(low_type)
        rest = (both - both_low.astype(wide)).astype(low_type)
        sums = dot_nt(member, both_low) + dot_nt(member, rest)
        for p in range(pairs):
            g_s[p, r, :] = grad_att[:, p * PAIR : (p + 1) * PAIR]
            delta[p, :, r] = sums[2 * p : 2 * p + 2, :]

    each(blocks, attend_gradient)

    def backward_loop(plan):
        def backward_pair(p):
            lanes = pl.ds(pl.multiple_of(p * PAIR, PAIR), PAIR)
            attention_backward_part(
                plan,
                rows_pre,
                starts_row,
                q_s.at[p],
                k_s.at[p],
                v_s.at[p],
                g_s.at[p],
                pk_s.at[p],
                pv_s.at[p],
                lse.at[p],
                delta.at[p],
                dp_pre.at[p],
                dp_pre.at[pairs + p],
                ke,
                ve,
                kt,
                slope,
                dk,
                dv,
                acc_a.at[:, lanes],
                acc_a.at[lanes, :],
            )

        each(pairs, backward_pair)

    def backward_by_half(lower, upper):
        @pl.when(me < reach)
        def _():
            backward_loop(lower(blocks))

        @pl.when(me >= reach)
        def _():
            backward_loop(upper(blocks))

    backward_by_half(lower_first_part, upper_first_part)

    def part_copy(d, peer):
        mine = dp_pre.at[pl.ds(peer * per_part, per_part)]
        return remote(mine, col_slots.at[me], r_send, r_recv, d, "col", peer)

    def dp_copy(d, peer):
        return remote(dp_own, dp_slots.at[me_dp], d_send, d_recv, d, "dp", peer)

    def hid_copy(d, peer):
        return remote(hid_own, hid_slots.at[me], e_send, e_recv, d, "col", peer)

    def sum_slots(slots, count):
        return lax.fori_loop(1, count, lambda j, total: total + slots[j], slots[0])

    def gradient_group(g):
        grads, places = [], []
        for j in range(group):
            rows = spot(to(g * group + j))
            places.append(rows)
            grads.append(
                jnp.concatenate(
                    [slabs[p, rows, :] for slabs in (q_s, k_s, v_s) for p in range(pairs)], axis=1
                )
            )
        back = dot_nt(jnp.concatenate(grads, axis=0), w_qkv[...])
        for j in range(group):
            at = g * group + j
            d = at
            rows = places[j]
            normed, inverse = standardize(x_rows[rows, :].astype(wide))
            total = mid[rows, :] + norm_backward_pass(
                back[j * piece : (j + 1) * piece, :], gain1, normed, inverse
            )
            here = cot_rows.at[spot(at), :]
            here[...] = total.astype(low_type)

            @pl.when(at < n - 1)
            def _():
                grad_copy(d, here, to(d)).start()

            @pl.when(at == n - 1)
            def _():
                pltpu.make_async_copy(here, grad_hbm.at[me], local_sem.at[6]).start()

    each(n - 1, lambda m: part_copy(m, to(m)).start())
    col_slots[me] = dp_pre[pl.ds(me * per_part, per_part)]
    gradient_group(jnp.int32(0))

    def catch_part(m):
        peer = source(m)
        mine = dp_pre.at[pl.ds(me * per_part, per_part)]
        remote(mine, col_slots.at[peer], r_send, r_recv, m, "col", peer).wait_recv()

    each(n - 1, catch_part)
    total = sum_slots(col_slots, n)
    total = jnp.concatenate([total[m] for m in range(per_part)], axis=1)
    dp_own[...] = total
    dp_slots[me_dp] = total
    for d in range(1, n_dp):
        dp_copy(d, lax.rem(me_dp + d, n_dp)).start()
    for d in range(1, n_dp):
        peer = lax.rem(me_dp + n_dp - d, n_dp)
        remote(dp_own, dp_slots.at[peer], d_send, d_recv, d, "dp", peer).wait_recv()
    own_low = sum_slots(dp_slots, n_dp).astype(low_type)
    part = dot_nt(own_low, w2_ref[...].astype(low_type))
    hid_own[...] = part
    hid_slots[me] = part
    each(n - 1, lambda m: hid_copy(m, to(m)).start())

    each(groups // 2 - 1, lambda g: gradient_group(g + 1))
    backward_by_half(lower_second_part, upper_second_part)
    each(groups - groups // 2, lambda g: gradient_group(g + groups // 2))
    hidden = hid[...]
    gw2_out[...] = lax.dot_general(
        hidden.astype(low_type), own_low, TN, preferred_element_type=wide
    )
    gb2_out[...] = jnp.sum(own_low.astype(wide), axis=0)

    def catch_hid(m):
        d = m
        peer = source(d)
        remote(hid_own, hid_slots.at[peer], e_send, e_recv, d, "col", peer).wait_recv()

    each(n - 1, catch_hid)
    grad_pre = (sum_slots(hid_slots, n) * (1.0 - hidden * hidden)).astype(low_type)
    table = jnp.concatenate(
        [table_ref[...], jnp.zeros((PRE - rows_pre, table_ref.shape[1]), wide)], 0
    ).astype(low_type)
    gw1_out[...] = lax.dot_general(table, grad_pre, TN, preferred_element_type=wide)
    gb1_out[...] = jnp.sum(grad_pre.astype(wide), axis=0)
    table_out[...] = dot_nt(grad_pre, w1_ref[...].astype(low_type))[:rows_pre, :]

    def finish(m):
        d = m
        peer, here = source(d), cot_rows.at[0:piece, :]
        remote(here, out_hbm.at[peer], o_send, o_recv, d, "col", peer).wait_recv()
        remote(here, grad_hbm.at[peer], g_send, g_recv, d, "col", peer).wait_recv()
        x_copy(d, to(d)).wait_send()
        starts_copy(d, to(d)).wait_send()
        pre_copy(d, to(d)).wait_send()
        cot_copy(d, to(d)).wait_send()
        out_copy(d, to(d)).wait_send()
        grad_copy(d, here, to(d)).wait_send()
        part_copy(d, to(d)).wait_send()
        hid_copy(d, to(d)).wait_send()

    each(n - 1, finish)
    for d in range(1, n_dp):
        dp_copy(d, lax.rem(me_dp + d, n_dp)).wait_send()
    own_out.wait()
    pltpu.make_async_copy(cot_rows.at[0:piece, :], grad_hbm.at[me], local_sem.at[6]).wait()


def hand_over_kernel(count, *refs):
    given, wanted, held = refs[:count], refs[count : 2 * count], refs[2 * count : 3 * count]
    sems = refs[3 * count]
    come = [pltpu.make_async_copy(given[j], held[j], sems.at[0, j]) for j in range(count)]
    go = [pltpu.make_async_copy(held[j], wanted[j], sems.at[1, j]) for j in range(count)]
    for copy in come:
        copy.start()
    for arrived, copy in zip(come, go):
        arrived.wait()
        copy.start()
    for copy in go:
        copy.wait()


def hand_over(results):
    results = list(results)
    count = len(results)
    return tuple(
        pl.pallas_call(
            functools.partial(hand_over_kernel, count),
            in_specs=[ANY] * count,
            out_specs=[ANY] * count,
            out_shape=[jax.ShapeDtypeStruct(r.shape, r.dtype) for r in results],
            scratch_shapes=[pltpu.VMEM(r.shape, r.dtype) for r in results]
            + [pltpu.SemaphoreType.DMA((2, count))],
            compiler_params=pltpu.CompilerParams(vmem_limit_bytes=VMEM_BYTES),
        )(*results)
    )


def on_device(*operands):
    n, n_dp = lax.axis_size("col"), lax.axis_size("dp")
    inputs, starts, cotangent, w_qkv, w_out = [operands[j] for j in (0, 1, 2, 5, 7)]
    w_fc, w_proj, table, w1, w2 = [operands[j] for j in (11, 13, 15, 16, 18)]
    row_count, piece, width = inputs.shape
    assert row_count == n and BLOCK % piece == 0
    length, inner = n * piece, w_fc.shape[1]
    pairs, tile = width // PAIR, min(1024, inner)
    part_width, mid_width = w2.shape[1], w1.shape[1]
    per_part = part_width // PAIR
    ext = PRE + length
    dma = pltpu.SemaphoreType.DMA
    shape = jax.ShapeDtypeStruct
    vmem = pltpu.VMEM
    slabs = vmem((pairs, length, PAIR), low_type)
    ordered = [operands[j] for j in (0, 1, 2, 5, 7, 11, 13)]
    ordered += [operands[j] for j in (3, 4, 6, 8, 9, 10, 12, 14, 15, 16, 17, 18, 19)]
    return hand_over(
        pl.pallas_call(
            functools.partial(block_kernel, n, n_dp),
            in_specs=[ANY] * 7 + [VM] * 13,
            out_specs=[ANY, ANY] + [VM] * 5,
            out_shape=[
                shape((n, piece, width), low_type),
                shape((n, piece, width), low_type),
                shape(table.shape, wide),
                shape(w1.shape, wide),
                shape((mid_width,), wide),
                shape(w2.shape, wide),
                shape((part_width,), wide),
            ],
            scratch_shapes=[
                vmem((length, width), low_type),
                vmem((length, width), low_type),
                slabs,
                slabs,
                slabs,
                slabs,
                slabs,
                vmem((length, width), wide),
                vmem((length, width), low_type),
                vmem((ext, width), wide),
                vmem((ext, inner), low_type),
                vmem(w_qkv.shape, low_type),
                vmem(w_out.shape, low_type),
                vmem((2, width, tile), low_type),
                vmem((2, tile, width), low_type),
                vmem((pairs, 2, length), wide),
                vmem((pairs, 2, length), wide),
                vmem((ext, PAIR), low_type),
                vmem((ext, PAIR), low_type),
                vmem((PAIR, ext), low_type),
                vmem((ext, PAIR), wide),
                vmem((ext, PAIR), wide),
                vmem((n,) + starts.shape, jnp.int32),
                vmem((1, length), jnp.int32),
                vmem((PRE, part_width), low_type),
                vmem((n, PRE, part_width), low_type),
                vmem((pairs, PRE, PAIR), low_type),
                vmem((pairs, PRE, PAIR), low_type),
                vmem((PRE, mid_width), wide),
                vmem((2 * pairs, PRE, PAIR), wide),
                vmem((n, per_part, PRE, PAIR), wide),
                vmem((PRE, part_width), wide),
                vmem((n_dp, PRE, part_width), wide),
                vmem((PRE, mid_width), wide),
                vmem((n, PRE, mid_width), wide),
                vmem((2, PAIR, BLOCK), wide),
            ]
            + [dma((n,))] * 14
            + [dma((n_dp,))] * 2
            + [dma((n,))] * 2
            + [dma((7,)), dma((2,)), dma((2,))]
            + [pltpu.SemaphoreType.REGULAR] * 2,
            compiler_params=pltpu.CompilerParams(
                collective_id=0, has_side_effects=True, vmem_limit_bytes=VMEM_BYTES
            ),
        )(*ordered)
    )


def solution(mesh):
    rows = P("dp", "col", None)
    return jax.shard_map(
        on_device,
        mesh=mesh,
        in_specs=(rows, P("dp", "col"), rows) + (P(),) * 15 + (P(None, "col"), P("col")),
        out_specs=(rows, rows, P(), P(), P(), P(None, "col"), P("col")),
        check_vma=False,
    )
```

```python
import functools

import jax
import jax.numpy as jnp
from jax import lax
from jax.experimental import pallas as pl
from jax.experimental.pallas import tpu as pltpu
from jax.sharding import PartitionSpec as P

H = 16
HEAD = 64
PAIR = 2 * HEAD
BLOCK = 256
PRE = 16
VMEM_BYTES = 62 << 20

epsilon = 1e-05
gelu_coef = 0.7978845608028654
cubic_coef = 0.044715
low_type = jnp.bfloat16
wide = jnp.float32
NT = (((1,), (1,)), ((), ()))
TN = (((0,), (0,)), ((), ()))
MESH = pl.DeviceIdType.MESH
ANY = pl.BlockSpec(memory_space=pl.ANY)
VM = pl.BlockSpec(memory_space=pltpu.VMEM)


def standardize(values):
    center = values - jnp.mean(values, axis=-1, keepdims=True)
    inverse = lax.rsqrt(jnp.mean(center * center, axis=-1, keepdims=True) + epsilon)
    return center * inverse, inverse


def norm_backward_pass(gradient, norm_gain, normed, inverse):
    scaled = gradient * norm_gain
    centered = scaled - jnp.mean(scaled, axis=-1, keepdims=True)
    return inverse * (centered - normed * jnp.mean(scaled * normed, axis=-1, keepdims=True))


def gelu_parts(upper):
    square = upper * upper
    tangent = jnp.tanh(upper * (gelu_coef + (gelu_coef * cubic_coef) * square))
    half = 0.5 * upper
    share = 0.5 + 0.5 * tangent
    slope = share + half * (1.0 - tangent * tangent) * (
        gelu_coef + (3.0 * gelu_coef * cubic_coef) * square
    )
    return upper * share, slope


def dot_nt(a, b):
    return lax.dot_general(a, b, NT, preferred_element_type=wide)


def dot(a, b):
    return jnp.dot(a, b, preferred_element_type=wide)


def head_mask(values, which):
    lane = lax.broadcasted_iota(jnp.int32, values.shape, 1)
    keep = (lane < HEAD) if which == 0 else (lane >= HEAD)
    return jnp.where(keep, values, jnp.zeros_like(values))


def token_mask(scores, start, block_q, block_k):
    key = block_k * BLOCK + lax.broadcasted_iota(jnp.int32, scores.shape, 0)
    keep = key >= start
    if block_q == block_k:
        query = block_q * BLOCK + lax.broadcasted_iota(jnp.int32, scores.shape, 1)
        keep = keep & (key <= query)
    return jnp.where(keep, scores, -jnp.inf)


def prefix_mask(scores, count):
    key = lax.broadcasted_iota(jnp.int32, scores.shape, 0)
    return jnp.where(key < count, scores, -jnp.inf)


def masked(scores, count, start, block_q, block_k):
    if block_k < 0:
        return prefix_mask(scores, count)
    return token_mask(scores, start, block_q, block_k)


def key_chunks(block_q):
    tokens = [(c, PRE + c * BLOCK, PRE + (c + 1) * BLOCK) for c in range(block_q + 1)]
    return [(-1, 0, PRE)] + tokens


def transposed(values):
    return values.astype(wide).T.astype(low_type)


FINAL, STORE, ADD = range(3)


def own_half_part(blocks, upper):
    first, last = (blocks // 2, blocks) if upper else (0, blocks // 2)
    return [(i, range(first, i + 1), STORE) for i in range(first, last)]


def other_part(blocks, upper):
    half = blocks // 2
    if upper:
        work = [(i, range(-1, i + 1), FINAL) for i in range(half)]
        return work + [(i, range(-1, half), ADD) for i in range(half, blocks)]
    work = [(i, range(-1, 0), ADD) for i in range(half)]
    return work + [(i, range(-1, i + 1), FINAL) for i in range(half, blocks)]


def key_rows(c):
    return (0, PRE) if c < 0 else (PRE + c * BLOCK, PRE + (c + 1) * BLOCK)


def attention_forward_part(
    work, count, starts, q, k, v, pk, pv, out, lse, ke, vt, s_all, p_all, o_two, keep, keep_stats
):
    half = q.shape[0] // 2
    used = sorted({c for _, chunks, _ in work for c in chunks})
    if used[0] < 0:
        ke[0:PRE, :] = pk[...]
        vt[:, 0:PRE] = transposed(pv[...])
    first, last = max(used[0], 0) * BLOCK, (used[-1] + 1) * BLOCK
    if last > first:
        ke[PRE + first : PRE + last, :] = k[first:last, :]
        vt[:, PRE + first : PRE + last] = transposed(v[first:last, :])
    units = [(i, chunks, mode, h) for i, chunks, mode in work for h in range(2)]

    def view(u):
        return slice((u % 2) * BLOCK, (u % 2 + 1) * BLOCK)

    def kept(i):
        first = i * BLOCK % half
        return slice(first, first + BLOCK)

    def score(u):
        i, chunks, mode, h = units[u]
        rows = slice(i * BLOCK, (i + 1) * BLOCK)
        mine = head_mask(q[rows, :], h)
        start = starts[:, rows]
        peak = keep_stats[h : h + 1, kept(i)] if mode == ADD else None
        for c in chunks:
            lo, hi = key_rows(c)
            s = masked(dot_nt(ke[lo:hi, :], mine), count, start, i, c)
            s_all[lo:hi, view(u)] = s
            top = jnp.max(s, axis=0, keepdims=True)
            peak = top if peak is None else jnp.maximum(peak, top)
        return peak

    def weigh(u, peak):
        i, chunks, mode, h = units[u]
        total = 0.0
        for c in chunks:
            lo, hi = key_rows(c)
            p = jnp.exp(s_all[lo:hi, view(u)] - peak)
            total = total + jnp.sum(p, axis=0, keepdims=True)
            p_all[lo:hi, view(u)] = p.astype(low_type)
        return total

    def collect(u, peak, total):
        i, chunks, mode, h = units[u]
        lo, hi = key_rows(chunks[0])[0], key_rows(chunks[-1])[1]
        feats = slice(h * HEAD, (h + 1) * HEAD)
        part = dot(vt[feats, lo:hi], p_all[lo:hi, view(u)])
        if mode == STORE:
            keep[feats, kept(i)] = part
            keep_stats[h : h + 1, kept(i)] = peak
            keep_stats[2 + h : 3 + h, kept(i)] = total
            return
        if mode == ADD:
            shrink = jnp.exp(keep_stats[h : h + 1, kept(i)] - peak)
            total = total + shrink * keep_stats[2 + h : 3 + h, kept(i)]
            part = part + shrink * keep[feats, kept(i)]
        lse[h : h + 1, i * BLOCK : (i + 1) * BLOCK] = peak + jnp.log(total)
        o_two[i % 2, feats, :] = part / total
        if h == 1:
            out[i * BLOCK : (i + 1) * BLOCK, :] = o_two[i % 2].T.astype(low_type)

    peak = score(0)
    for u in range(len(units)):
        following = score(u + 1) if u + 1 < len(units) else None
        total = weigh(u, peak)
        collect(u, peak, total)
        peak = following


def lower_first_part(blocks):
    low, high = range(blocks // 2), range(blocks // 2, blocks)
    work = [(i, range(-1, 0)) for i in low] + [(i, range(-1, i + 1)) for i in high]
    keys = [(c, range(c, blocks), FINAL) for c in high] + [(c, high, STORE) for c in low]
    keys += [(-1, range(blocks), FINAL)]
    return work, keys, [(i, range(-1, i + 1), FINAL) for i in high]


def lower_second_part(blocks):
    low = range(blocks // 2)
    work = [(i, range(-1, i + 1)) for i in low]
    keys = [(c, range(c, blocks // 2), ADD) for c in low]
    return work, keys, [(i, range(-1, i + 1), FINAL) for i in low]


def upper_first_part(blocks):
    half = blocks // 2
    work = [(i, range(-1, min(i + 1, half))) for i in range(blocks)]
    keys = [(c, range(max(c, 0), blocks), FINAL) for c in range(-1, half)]
    queries = [(i, chunks, FINAL if i < half else STORE) for i, chunks in work]
    return work, keys, queries


def upper_second_part(blocks):
    high = range(blocks // 2, blocks)
    work = [(i, range(blocks // 2, i + 1)) for i in high]
    keys = [(c, range(c, blocks), FINAL) for c in high]
    return work, keys, [(i, chunks, ADD) for i, chunks in work]


def attention_backward_part(
    plan, count, starts, q, k, v, g, pk, pv, lse, delta, dpk, dpv, ke, ve, kt, p_all, dk, dv, keep, keep_q
):
    work, keys, queries = plan
    length = q.shape[0]
    half = length // 2
    used = sorted({c for _, chunks in work for c in chunks})
    if used[0] < 0:
        ke[0:PRE, :] = pk[...]
        ve[0:PRE, :] = pv[...]
        kt[:, 0:PRE] = transposed(pk[...])
    first, last = max(used[0], 0) * BLOCK, (used[-1] + 1) * BLOCK
    ke[PRE + first : PRE + last, :] = k[first:last, :]
    ve[PRE + first : PRE + last, :] = v[first:last, :]
    kt[:, PRE + first : PRE + last] = transposed(k[first:last, :])

    def weigh(i, chunks, h):
        rows = slice(i * BLOCK, (i + 1) * BLOCK)
        mine, grad = head_mask(q[rows, :], h), head_mask(g[rows, :], h)
        start = starts[:, rows]
        shift, middle = lse[h : h + 1, rows], delta[h : h + 1, rows]
        p_at = slice(h * length + i * BLOCK, h * length + (i + 1) * BLOCK)
        ds_at = slice((2 + h) * length + i * BLOCK, (2 + h) * length + (i + 1) * BLOCK)
        for c in chunks:
            lo, hi = key_rows(c)
            s = masked(dot_nt(ke[lo:hi, :], mine), count, start, i, c)
            p = jnp.exp(s - shift)
            p_all[lo:hi, p_at] = p.astype(low_type)
            ds = p * (dot_nt(ve[lo:hi, :], grad) - middle)
            p_all[lo:hi, ds_at] = ds.astype(low_type)

    def collect_keys(c, members, mode, h):
        lo, hi = key_rows(c)
        a, b = members[0] * BLOCK, (members[-1] + 1) * BLOCK
        mine, grad = head_mask(q[a:b, :], h), head_mask(g[a:b, :], h)
        dv_part = dot(p_all[lo:hi, h * length + a : h * length + b], grad)
        dk_part = dot(p_all[lo:hi, (2 + h) * length + a : (2 + h) * length + b], mine)
        if h == 0:
            dv[lo:hi, :] = dv_part
            dk[lo:hi, :] = dk_part
            return
        dv_part = dv[lo:hi, :] + dv_part
        dk_part = dk[lo:hi, :] + dk_part
        if c < 0:
            dpv[...] = dv_part
            dpk[...] = dk_part
            return
        rows = slice(c * BLOCK, (c + 1) * BLOCK)
        if mode == STORE:
            keep[rows, :] = dk_part
            keep[half + rows.start : half + rows.stop, :] = dv_part
            return
        if mode == ADD:
            dk_part = dk_part + keep[rows, :]
            dv_part = dv_part + keep[half + rows.start : half + rows.stop, :]
        v[rows, :] = dv_part.astype(low_type)
        k[rows, :] = dk_part.astype(low_type)

    def collect_queries(i, chunks, mode):
        lo, hi = key_rows(chunks[0])[0], key_rows(chunks[-1])[1]
        parts = []
        for h in range(2):
            feats = slice(h * HEAD, (h + 1) * HEAD)
            ds_at = slice((2 + h) * length + i * BLOCK, (2 + h) * length + (i + 1) * BLOCK)
            parts.append(dot(kt[feats, lo:hi], p_all[lo:hi, ds_at]))
        both = jnp.concatenate(parts, 0)
        kept = slice(i * BLOCK - half, (i + 1) * BLOCK - half)
        if mode == STORE:
            keep_q[:, kept] = both
            return
        if mode == ADD:
            both = both + keep_q[:, kept]
        q[i * BLOCK : (i + 1) * BLOCK, :] = (both.T * (HEAD**-0.5)).astype(low_type)

    for h in range(2):
        for i, chunks in work:
            weigh(i, chunks, h)
    for h in range(2):
        for c, members, mode in keys:
            collect_keys(c, members, mode, h)
    for i, chunks, mode in queries:
        collect_queries(i, chunks, mode)


def block_kernel(
    n,
    n_dp,
    x_hbm,
    starts_hbm,
    cot_hbm,
    w_qkv_hbm,
    w_out_hbm,
    w_fc_hbm,
    w_proj_hbm,
    gain1_ref,
    shift1_ref,
    b_qkv_ref,
    b_out_ref,
    gain2_ref,
    shift2_ref,
    b_fc_ref,
    b_proj_ref,
    table_ref,
    w1_ref,
    b1_ref,
    w2_ref,
    b2_ref,
    out_hbm,
    grad_hbm,
    table_out,
    gw1_out,
    gb1_out,
    gw2_out,
    gb2_out,
    x_rows,
    cot_rows,
    q_s,
    k_s,
    v_s,
    a_s,
    g_s,
    mid,
    h_rows,
    acc_a,
    slope,
    w_qkv,
    w_out,
    w_fc,
    w_proj,
    lse,
    delta,
    ke,
    ve,
    kt,
    dk,
    dv,
    starts_slots,
    starts_row,
    own_pre,
    pre_slots,
    pk_s,
    pv_s,
    hid,
    dp_pre,
    col_slots,
    dp_own,
    dp_slots,
    hid_own,
    hid_slots,
    o_two,
    keep_stats,
    x_send,
    x_recv,
    s_send,
    s_recv,
    p_send,
    p_recv,
    c_send,
    c_recv,
    o_send,
    o_recv,
    g_send,
    g_recv,
    r_send,
    r_recv,
    d_send,
    d_recv,
    e_send,
    e_recv,
    local_sem,
    fc_sem,
    proj_sem,
    x_here,
    cot_here,
):
    me, me_dp = lax.axis_index("col"), lax.axis_index("dp")
    piece, width = x_hbm.shape[1], x_hbm.shape[2]
    length = n * piece
    blocks = length // BLOCK
    pairs = width // PAIR
    inner = b_fc_ref.shape[0]
    tile = w_fc.shape[2]
    tiles = inner // tile
    rows_pre = table_ref.shape[0]
    group = BLOCK // piece
    part_width = w2_ref.shape[1]
    per_part = part_width // PAIR
    groups = n // group
    heads = 2 * pairs

    def spot(at):
        return pl.ds(pl.multiple_of(at * piece, piece), piece)

    def each(count, step):
        def body(k, carry):
            step(k)
            return carry

        lax.fori_loop(0, count, body, 0)

    reach = n // 2
    mine_base = lax.div(me, reach) * reach
    other_base = reach - mine_base
    seat = lax.rem(me, reach)

    def to(m):
        same = lax.div(m, reach)
        step = lax.rem(m, reach) + same
        there, bit = other_base + same * (mine_base - other_base), 1
        while bit < reach:
            differ = lax.rem(lax.div(seat, bit) + lax.div(step, bit), 2)
            there, bit = there + differ * bit, 2 * bit
        return there

    source = to

    def remote(src, dst, send, recv, d, axis, peer):
        return pltpu.make_async_remote_copy(
            src_ref=src,
            dst_ref=dst,
            send_sem=send.at[d],
            recv_sem=recv.at[d],
            device_id={axis: peer},
            device_id_type=MESH,
        )

    def vector(ref):
        return ref[...].astype(wide).reshape(1, -1)

    def fc_load(t, slot):
        cols = pl.ds(pl.multiple_of(t * tile, tile), tile)
        return pltpu.make_async_copy(w_fc_hbm.at[:, cols], w_fc.at[slot], fc_sem.at[slot])

    def proj_load(t, slot):
        rows = pl.ds(pl.multiple_of(t * tile, tile), tile)
        return pltpu.make_async_copy(w_proj_hbm.at[rows, :], w_proj.at[slot], proj_sem.at[slot])

    load_qkv = pltpu.make_async_copy(w_qkv_hbm, w_qkv, local_sem.at[0])
    load_qkv.start()
    barrier = pltpu.get_barrier_semaphore()
    for m in range(n - 1):
        peer = to(jnp.int32(m))
        pl.semaphore_signal(barrier, inc=1, device_id={"col": peer}, device_id_type=MESH)
    for d in range(1, n_dp):
        pl.semaphore_signal(
            barrier, inc=1, device_id={"dp": lax.rem(me_dp + d, n_dp)}, device_id_type=MESH
        )
    pl.semaphore_wait(barrier, n - 1 + n_dp - 1)

    def x_copy(d, peer):
        return remote(x_hbm.at[peer], x_rows.at[spot(me), :], x_send, x_recv, d, "col", peer)

    def starts_copy(d, peer):
        return remote(starts_hbm, starts_slots.at[me], s_send, s_recv, d, "col", peer)

    def pre_copy(d, peer):
        return remote(own_pre, pre_slots.at[me], p_send, p_recv, d, "col", peer)

    def cot_copy(d, peer):
        return remote(cot_hbm.at[peer], cot_rows.at[spot(me), :], c_send, c_recv, d, "col", peer)

    def out_copy(d, peer):
        return remote(h_rows.at[spot(peer), :], out_hbm.at[me], o_send, o_recv, d, "col", peer)

    def grad_copy(d, here, peer):
        return remote(here, grad_hbm.at[me], g_send, g_recv, d, "col", peer)

    def send_inputs(m):
        x_copy(m, to(m)).start()
        starts_copy(m, to(m)).start()

    each(n - 1, send_inputs)
    own_x = pltpu.make_async_copy(x_hbm.at[me], x_rows.at[spot(me), :], local_sem.at[1])
    own_x.start()
    own_cot = pltpu.make_async_copy(cot_hbm.at[me], cot_rows.at[spot(me), :], local_sem.at[2])
    own_cot.start()
    own_starts = pltpu.make_async_copy(starts_hbm, starts_slots.at[me], local_sem.at[3])
    own_starts.start()
    load_out = pltpu.make_async_copy(w_out_hbm, w_out, local_sem.at[4])
    load_out.start()
    fc_load(0, 0).start()
    proj_load(0, 0).start()

    hidden = jnp.tanh(
        dot(table_ref[...].astype(low_type), w1_ref[...].astype(low_type)) + vector(b1_ref)
    )
    hid[...] = jnp.concatenate([hidden, jnp.zeros((PRE - rows_pre, hidden.shape[1]), wide)], 0)
    own = dot(hidden.astype(low_type), w2_ref[...].astype(low_type)) + vector(b2_ref)
    own = jnp.concatenate([own, jnp.zeros((PRE - rows_pre, part_width), wide)], 0).astype(low_type)
    own_pre[...] = own
    pre_slots[me] = own
    each(n - 1, lambda m: pre_copy(m, to(m)).start())

    gain1, shift1 = vector(gain1_ref), vector(shift1_ref)
    own_x.wait()
    load_qkv.wait()

    def greet_peers(sem):
        def greet(m):
            pl.semaphore_signal(sem, inc=1, device_id={"col": to(m)}, device_id_type=MESH)

        each(n - 1, greet)

    span = n // 2
    rows_span = span * piece

    def starts_of(first):
        for j in range(first, first + reach):
            starts_row[:, j * piece : (j + 1) * piece] = starts_slots[j, pl.ds(me, 1), :]

    def by_half(lower, upper):
        @pl.when(me < reach)
        def _():
            lower()

        @pl.when(me >= reach)
        def _():
            upper()

    def forward_loop(work):
        def forward_pair(p):
            attention_forward_part(
                work,
                rows_pre,
                starts_row,
                q_s.at[p],
                k_s.at[p],
                v_s.at[p],
                pk_s.at[p],
                pv_s.at[p],
                a_s.at[p],
                lse.at[p],
                ke,
                kt,
                acc_a,
                slope,
                o_two,
                mid.at[pl.ds(pl.multiple_of(p * PAIR, PAIR), PAIR), :],
                keep_stats.at[p],
            )

        each(pairs, forward_pair)

    def catch_starts(m):
        peer = source(m)
        remote(starts_hbm, starts_slots.at[peer], s_send, s_recv, m, "col", peer).wait_recv()

    def qkv_group(g):
        places = []
        for j in range(span):
            d = n - 1 - (g * span + j)
            rows = spot(source(d))
            places.append(rows)

            @pl.when(d < n - 1)
            def _():
                remote(
                    x_hbm.at[me], x_rows.at[rows, :], x_send, x_recv, d, "col", source(d)
                ).wait_recv()

            normed, _ = standardize(x_rows[rows, :].astype(wide))
            h_rows[j * piece : (j + 1) * piece, :] = (normed * gain1 + shift1).astype(low_type)

        @pl.when(g == 1)
        def _():
            greet_peers(x_here)

        normed = h_rows[0:rows_span, :]
        for c in range(0, 3 * width, width // 2):
            part = dot(normed, w_qkv[:, c : c + width // 2])
            part = part + b_qkv_ref[c : c + width // 2].astype(wide).reshape(1, -1)
            if c < width:
                part = part * (HEAD**-0.5)
            part = part.astype(low_type)
            slabs = (q_s, k_s, v_s)[c // width]
            for m in range(width // 2 // PAIR):
                pair = (c % width) // PAIR + m
                for j in range(span):
                    slabs[pair, places[j], :] = part[
                        j * piece : (j + 1) * piece, m * PAIR : (m + 1) * PAIR
                    ]

        @pl.when(g == 0)
        def _():
            each(reach - 1, lambda m: catch_starts(reach + m))
            own_starts.wait()
            by_half(lambda: starts_of(0), lambda: starts_of(reach))
            by_half(
                lambda: forward_loop(own_half_part(blocks, False)),
                lambda: forward_loop(own_half_part(blocks, True)),
            )

    each(2, qkv_group)

    pl.semaphore_wait(x_here, n - 1)
    each(n - 1, lambda m: cot_copy(m, to(m)).start())

    each(reach, catch_starts)
    by_half(lambda: starts_of(reach), lambda: starts_of(0))

    def catch_prefix(m):
        peer = source(m)
        remote(own_pre, pre_slots.at[peer], p_send, p_recv, m, "col", peer).wait_recv()

    each(n - 1, catch_prefix)
    for j in range(n):
        for m in range(per_part):
            pair = j * per_part + m
            slab = pre_slots[j][:, m * PAIR : (m + 1) * PAIR]
            if pair < pairs:
                pk_s[pair] = slab
            else:
                pv_s[pair - pairs] = slab

    by_half(
        lambda: forward_loop(other_part(blocks, False)),
        lambda: forward_loop(other_part(blocks, True)),
    )

    load_out.wait()
    gain2, shift2 = vector(gain2_ref), vector(shift2_ref)
    big = 2 * BLOCK

    def project(b):
        r = pl.ds(pl.multiple_of(b * BLOCK, BLOCK), BLOCK)
        att = jnp.concatenate([a_s[p, r, :] for p in range(pairs)], axis=1)
        middle = x_rows[r, :].astype(wide) + dot(att, w_out[...]) + vector(b_out_ref)
        mid[r, :] = middle
        normed, _ = standardize(middle)
        h_rows[r, :] = (normed * gain2 + shift2).astype(low_type)
        acc_a[r, :] = middle + vector(b_proj_ref)

    each(blocks, project)

    def forward_tile(t):
        slot = lax.rem(t, 2)
        fc_load(t, slot).wait()
        proj_load(t, slot).wait()

        @pl.when(t + 1 < tiles)
        def _():
            fc_load(t + 1, 1 - slot).start()
            proj_load(t + 1, 1 - slot).start()

        cols = pl.ds(pl.multiple_of(t * tile, tile), tile)
        bias = b_fc_ref[cols].astype(wide).reshape(1, -1)

        def half(b):
            r = pl.ds(pl.multiple_of(b * big, big), big)
            upper = dot(h_rows[r, :], w_fc[slot]) + bias
            value, steep = gelu_parts(upper)
            slope[r, cols] = steep.astype(low_type)
            acc_a[r, :] += dot(value.astype(low_type), w_proj[slot])

        each(length // big, half)

    each(tiles, forward_tile)

    own_cot.wait()

    def catch_cot(m):
        d = m
        peer = source(d)
        remote(
            cot_hbm.at[me], cot_rows.at[spot(peer), :], c_send, c_recv, d, "col", peer
        ).wait_recv()

    each(n - 1, catch_cot)
    greet_peers(cot_here)

    def settle(b):
        r = pl.ds(pl.multiple_of(b * BLOCK, BLOCK), BLOCK)
        h_rows[r, :] = acc_a[r, :].astype(low_type)
        acc_a[r, :] = jnp.zeros((BLOCK, width), wide)

    each(blocks, settle)
    pl.semaphore_wait(cot_here, n - 1)
    each(n - 1, lambda m: out_copy(m, to(m)).start())
    own_out = pltpu.make_async_copy(h_rows.at[spot(me), :], out_hbm.at[me], local_sem.at[5])
    own_out.start()

    def backward_tile(step):
        t = tiles - 1 - step
        slot = lax.rem(t, 2)

        @pl.when(step >= 2)
        def _():
            fc_load(t, slot).wait()
            proj_load(t, slot).wait()

        cols = pl.ds(pl.multiple_of(t * tile, tile), tile)

        def half(b):
            r = pl.ds(pl.multiple_of(b * big, big), big)
            grad_act = dot_nt(cot_rows[r, :], w_proj[slot])
            grad_upper = (grad_act * slope[r, cols].astype(wide)).astype(low_type)
            acc_a[r, :] += dot_nt(grad_upper, w_fc[slot])

        each(length // big, half)

        @pl.when(t >= 2)
        def _():
            fc_load(t - 2, slot).start()
            proj_load(t - 2, slot).start()

    each(tiles, backward_tile)
    feature_head = lax.broadcasted_iota(jnp.int32, (heads, width), 1) // HEAD
    which = lax.broadcasted_iota(jnp.int32, (heads, width), 0)
    member = jnp.where(feature_head == which, 1.0, 0.0).astype(low_type)

    def attend_gradient(b):
        r = pl.ds(pl.multiple_of(b * BLOCK, BLOCK), BLOCK)
        normed, inverse = standardize(mid[r, :])
        grad_mid = cot_rows[r, :].astype(wide) + norm_backward_pass(
            acc_a[r, :], gain2, normed, inverse
        )
        mid[r, :] = grad_mid
        grad_att = dot_nt(grad_mid.astype(low_type), w_out[...]).astype(low_type)
        att = jnp.concatenate([a_s[p, r, :] for p in range(pairs)], axis=1)
        both = grad_att.astype(wide) * att.astype(wide)
        both_low = both.astype(low_type)
        rest = (both - both_low.astype(wide)).astype(low_type)
        sums = dot_nt(member, both_low) + dot_nt(member, rest)
        for p in range(pairs):
            g_s[p, r, :] = grad_att[:, p * PAIR : (p + 1) * PAIR]
            delta[p, :, r] = sums[2 * p : 2 * p + 2, :]

    each(blocks, attend_gradient)

    def backward_loop(plan):
        def backward_pair(p):
            lanes = pl.ds(pl.multiple_of(p * PAIR, PAIR), PAIR)
            attention_backward_part(
                plan,
                rows_pre,
                starts_row,
                q_s.at[p],
                k_s.at[p],
                v_s.at[p],
                g_s.at[p],
                pk_s.at[p],
                pv_s.at[p],
                lse.at[p],
                delta.at[p],
                dp_pre.at[p],
                dp_pre.at[pairs + p],
                ke,
                ve,
                kt,
                slope,
                dk,
                dv,
                acc_a.at[:, lanes],
                acc_a.at[lanes, :],
            )

        each(pairs, backward_pair)

    def backward_by_half(lower, upper):
        by_half(lambda: backward_loop(lower(blocks)), lambda: backward_loop(upper(blocks)))

    backward_by_half(lower_first_part, upper_first_part)

    def part_copy(d, peer):
        mine = dp_pre.at[pl.ds(peer * per_part, per_part)]
        return remote(mine, col_slots.at[me], r_send, r_recv, d, "col", peer)

    def dp_copy(d, peer):
        return remote(dp_own, dp_slots.at[me_dp], d_send, d_recv, d, "dp", peer)

    def hid_copy(d, peer):
        return remote(hid_own, hid_slots.at[me], e_send, e_recv, d, "col", peer)

    def sum_slots(slots, count):
        return lax.fori_loop(1, count, lambda j, total: total + slots[j], slots[0])

    def gradient_group(g):
        grads, places = [], []
        for j in range(group):
            rows = spot(to(g * group + j))
            places.append(rows)
            grads.append(
                jnp.concatenate(
                    [slabs[p, rows, :] for slabs in (q_s, k_s, v_s) for p in range(pairs)], axis=1
                )
            )
        back = dot_nt(jnp.concatenate(grads, axis=0), w_qkv[...])
        for j in range(group):
            at = g * group + j
            rows = places[j]
            normed, inverse = standardize(x_rows[rows, :].astype(wide))
            total = mid[rows, :] + norm_backward_pass(
                back[j * piece : (j + 1) * piece, :], gain1, normed, inverse
            )
            cot_rows[spot(at), :] = total.astype(low_type)

    def send_gradient(m):
        here = cot_rows.at[spot(m), :]

        @pl.when(m < n - 1)
        def _():
            grad_copy(m, here, to(m)).start()

        @pl.when(m == n - 1)
        def _():
            pltpu.make_async_copy(here, grad_hbm.at[me], local_sem.at[6]).start()

    def leave_step(part):
        def one_group(g):
            at = part * (groups // 2) + g
            gradient_group(at)
            each(group, lambda j: send_gradient(at * group + j))

        each(groups // 2, one_group)

        @pl.when(part == 0)
        def _():
            backward_by_half(lower_second_part, upper_second_part)

    each(n - 1, lambda m: part_copy(m, to(m)).start())
    col_slots[me] = dp_pre[pl.ds(me * per_part, per_part)]
    each(2, leave_step)

    def catch_part(m):
        peer = source(m)
        mine = dp_pre.at[pl.ds(me * per_part, per_part)]
        remote(mine, col_slots.at[peer], r_send, r_recv, m, "col", peer).wait_recv()

    each(n - 1, catch_part)
    total = sum_slots(col_slots, n)
    total = jnp.concatenate([total[m] for m in range(per_part)], axis=1)
    dp_own[...] = total
    dp_slots[me_dp] = total
    for d in range(1, n_dp):
        dp_copy(d, lax.rem(me_dp + d, n_dp)).start()
    for d in range(1, n_dp):
        peer = lax.rem(me_dp + n_dp - d, n_dp)
        remote(dp_own, dp_slots.at[peer], d_send, d_recv, d, "dp", peer).wait_recv()
    own_low = sum_slots(dp_slots, n_dp).astype(low_type)
    part = dot_nt(own_low, w2_ref[...].astype(low_type))
    hid_own[...] = part
    hid_slots[me] = part
    each(n - 1, lambda m: hid_copy(m, to(m)).start())

    hidden = hid[...]
    gw2_out[...] = lax.dot_general(
        hidden.astype(low_type), own_low, TN, preferred_element_type=wide
    )
    gb2_out[...] = jnp.sum(own_low.astype(wide), axis=0)

    def catch_hid(m):
        peer = source(m)
        remote(hid_own, hid_slots.at[peer], e_send, e_recv, m, "col", peer).wait_recv()

    each(n - 1, catch_hid)
    grad_pre = (sum_slots(hid_slots, n) * (1.0 - hidden * hidden)).astype(low_type)
    table = jnp.concatenate(
        [table_ref[...], jnp.zeros((PRE - rows_pre, table_ref.shape[1]), wide)], 0
    ).astype(low_type)
    gw1_out[...] = lax.dot_general(table, grad_pre, TN, preferred_element_type=wide)
    gb1_out[...] = jnp.sum(grad_pre.astype(wide), axis=0)
    table_out[...] = dot_nt(grad_pre, w1_ref[...].astype(low_type))[:rows_pre, :]

    def finish(m):
        peer, here = source(m), cot_rows.at[0:piece, :]
        remote(here, out_hbm.at[peer], o_send, o_recv, m, "col", peer).wait_recv()
        x_copy(m, to(m)).wait_send()
        starts_copy(m, to(m)).wait_send()
        pre_copy(m, to(m)).wait_send()
        cot_copy(m, to(m)).wait_send()
        out_copy(m, to(m)).wait_send()
        part_copy(m, to(m)).wait_send()
        hid_copy(m, to(m)).wait_send()

    each(n - 1, finish)
    for d in range(1, n_dp):
        dp_copy(d, lax.rem(me_dp + d, n_dp)).wait_send()
    own_out.wait()
    pltpu.make_async_copy(cot_rows.at[0:piece, :], grad_hbm.at[me], local_sem.at[6]).wait()

    def finish_gradient(m):
        peer, here = source(m), cot_rows.at[0:piece, :]
        remote(here, grad_hbm.at[peer], g_send, g_recv, m, "col", peer).wait_recv()
        grad_copy(m, here, to(m)).wait_send()

    each(n - 1, finish_gradient)


def hand_over_kernel(count, *refs):
    given, wanted, held = refs[:count], refs[count : 2 * count], refs[2 * count : 3 * count]
    sems = refs[3 * count]
    come = [pltpu.make_async_copy(given[j], held[j], sems.at[0, j]) for j in range(count)]
    go = [pltpu.make_async_copy(held[j], wanted[j], sems.at[1, j]) for j in range(count)]
    for copy in come:
        copy.start()
    for arrived, copy in zip(come, go):
        arrived.wait()
        copy.start()
    for copy in go:
        copy.wait()


def hand_over(results):
    results = list(results)
    count = len(results)
    return tuple(
        pl.pallas_call(
            functools.partial(hand_over_kernel, count),
            in_specs=[ANY] * count,
            out_specs=[ANY] * count,
            out_shape=[jax.ShapeDtypeStruct(r.shape, r.dtype) for r in results],
            scratch_shapes=[pltpu.VMEM(r.shape, r.dtype) for r in results]
            + [pltpu.SemaphoreType.DMA((2, count))],
            compiler_params=pltpu.CompilerParams(vmem_limit_bytes=VMEM_BYTES),
        )(*results)
    )


def on_device(*operands):
    n, n_dp = lax.axis_size("col"), lax.axis_size("dp")
    inputs, starts, cotangent, w_qkv, w_out = [operands[j] for j in (0, 1, 2, 5, 7)]
    w_fc, w_proj, table, w1, w2 = [operands[j] for j in (11, 13, 15, 16, 18)]
    row_count, piece, width = inputs.shape
    assert row_count == n and BLOCK % piece == 0
    length, inner = n * piece, w_fc.shape[1]
    pairs, tile = width // PAIR, min(1024, inner)
    part_width, mid_width = w2.shape[1], w1.shape[1]
    per_part = part_width // PAIR
    ext = PRE + length
    dma = pltpu.SemaphoreType.DMA
    shape = jax.ShapeDtypeStruct
    vmem = pltpu.VMEM
    slabs = vmem((pairs, length, PAIR), low_type)
    ordered = [operands[j] for j in (0, 1, 2, 5, 7, 11, 13)]
    ordered += [operands[j] for j in (3, 4, 6, 8, 9, 10, 12, 14, 15, 16, 17, 18, 19)]
    return hand_over(
        pl.pallas_call(
            functools.partial(block_kernel, n, n_dp),
            in_specs=[ANY] * 7 + [VM] * 13,
            out_specs=[ANY, ANY] + [VM] * 5,
            out_shape=[
                shape((n, piece, width), low_type),
                shape((n, piece, width), low_type),
                shape(table.shape, wide),
                shape(w1.shape, wide),
                shape((mid_width,), wide),
                shape(w2.shape, wide),
                shape((part_width,), wide),
            ],
            scratch_shapes=[
                vmem((length, width), low_type),
                vmem((length, width), low_type),
                slabs,
                slabs,
                slabs,
                slabs,
                slabs,
                vmem((length, width), wide),
                vmem((length, width), low_type),
                vmem((ext, width), wide),
                vmem((ext, inner), low_type),
                vmem(w_qkv.shape, low_type),
                vmem(w_out.shape, low_type),
                vmem((2, width, tile), low_type),
                vmem((2, tile, width), low_type),
                vmem((pairs, 2, length), wide),
                vmem((pairs, 2, length), wide),
                vmem((ext, PAIR), low_type),
                vmem((ext, PAIR), low_type),
                vmem((PAIR, ext), low_type),
                vmem((ext, PAIR), wide),
                vmem((ext, PAIR), wide),
                vmem((n,) + starts.shape, jnp.int32),
                vmem((1, length), jnp.int32),
                vmem((PRE, part_width), low_type),
                vmem((n, PRE, part_width), low_type),
                vmem((pairs, PRE, PAIR), low_type),
                vmem((pairs, PRE, PAIR), low_type),
                vmem((PRE, mid_width), wide),
                vmem((2 * pairs, PRE, PAIR), wide),
                vmem((n, per_part, PRE, PAIR), wide),
                vmem((PRE, part_width), wide),
                vmem((n_dp, PRE, part_width), wide),
                vmem((PRE, mid_width), wide),
                vmem((n, PRE, mid_width), wide),
                vmem((2, PAIR, BLOCK), wide),
                vmem((pairs, 4, length // 2), wide),
            ]
            + [dma((n,))] * 14
            + [dma((n_dp,))] * 2
            + [dma((n,))] * 2
            + [dma((7,)), dma((2,)), dma((2,))]
            + [pltpu.SemaphoreType.REGULAR] * 2,
            compiler_params=pltpu.CompilerParams(
                collective_id=0, has_side_effects=True, vmem_limit_bytes=VMEM_BYTES
            ),
        )(*ordered)
    )


def solution(mesh):
    rows = P("dp", "col", None)
    return jax.shard_map(
        on_device,
        mesh=mesh,
        in_specs=(rows, P("dp", "col"), rows) + (P(),) * 15 + (P(None, "col"), P("col")),
        out_specs=(rows, rows, P(), P(), P(), P(None, "col"), P("col")),
        check_vma=False,
    )
```

```python
import functools

import jax
import jax.numpy as jnp
from jax import lax
from jax.experimental import pallas as pl
from jax.experimental.pallas import tpu as pltpu
from jax.sharding import PartitionSpec as P

H = 16
HEAD = 64
PAIR = 2 * HEAD
BLOCK = 256
PRE = 16
VMEM_BYTES = 62 << 20

epsilon = 1e-05
gelu_coef = 0.7978845608028654
cubic_coef = 0.044715
low_type = jnp.bfloat16
wide = jnp.float32
NT = (((1,), (1,)), ((), ()))
TN = (((0,), (0,)), ((), ()))
MESH = pl.DeviceIdType.MESH
ANY = pl.BlockSpec(memory_space=pl.ANY)
VM = pl.BlockSpec(memory_space=pltpu.VMEM)


def standardize(values):
    center = values - jnp.mean(values, axis=-1, keepdims=True)
    inverse = lax.rsqrt(jnp.mean(center * center, axis=-1, keepdims=True) + epsilon)
    return center * inverse, inverse


def norm_backward_pass(gradient, norm_gain, normed, inverse):
    scaled = gradient * norm_gain
    centered = scaled - jnp.mean(scaled, axis=-1, keepdims=True)
    return inverse * (centered - normed * jnp.mean(scaled * normed, axis=-1, keepdims=True))


def gelu_parts(upper):
    square = upper * upper
    tangent = jnp.tanh(upper * (gelu_coef + (gelu_coef * cubic_coef) * square))
    half = 0.5 * upper
    share = 0.5 + 0.5 * tangent
    slope = share + half * (1.0 - tangent * tangent) * (
        gelu_coef + (3.0 * gelu_coef * cubic_coef) * square
    )
    return upper * share, slope


def dot_nt(a, b):
    return lax.dot_general(a, b, NT, preferred_element_type=wide)


def dot(a, b):
    return jnp.dot(a, b, preferred_element_type=wide)


def head_mask(values, which):
    lane = lax.broadcasted_iota(jnp.int32, values.shape, 1)
    keep = (lane < HEAD) if which == 0 else (lane >= HEAD)
    return jnp.where(keep, values, jnp.zeros_like(values))


def token_mask(scores, start, block_q, block_k):
    key = block_k * BLOCK + lax.broadcasted_iota(jnp.int32, scores.shape, 0)
    keep = key >= start
    if block_q == block_k:
        query = block_q * BLOCK + lax.broadcasted_iota(jnp.int32, scores.shape, 1)
        keep = keep & (key <= query)
    return jnp.where(keep, scores, -jnp.inf)


def prefix_mask(scores, count):
    key = lax.broadcasted_iota(jnp.int32, scores.shape, 0)
    return jnp.where(key < count, scores, -jnp.inf)


def masked(scores, count, start, block_q, block_k):
    if block_k < 0:
        return prefix_mask(scores, count)
    return token_mask(scores, start, block_q, block_k)


def key_chunks(block_q):
    tokens = [(c, PRE + c * BLOCK, PRE + (c + 1) * BLOCK) for c in range(block_q + 1)]
    return [(-1, 0, PRE)] + tokens


def transposed(values):
    return values.astype(wide).T.astype(low_type)


FINAL, STORE, ADD = range(3)


def own_half_part(blocks, upper):
    first, last = (blocks // 2, blocks) if upper else (0, blocks // 2)
    return [(i, range(first, i + 1), STORE) for i in range(first, last)]


def other_part(blocks, upper):
    half = blocks // 2
    if upper:
        work = [(i, range(-1, i + 1), FINAL) for i in range(half)]
        return work + [(i, range(-1, half), ADD) for i in range(half, blocks)]
    work = [(i, range(-1, 0), ADD) for i in range(half)]
    return work + [(i, range(-1, i + 1), FINAL) for i in range(half, blocks)]


def key_rows(c):
    return (0, PRE) if c < 0 else (PRE + c * BLOCK, PRE + (c + 1) * BLOCK)


def attention_forward_part(
    work, count, starts, q, k, v, pk, pv, out, lse, ke, vt, s_all, p_all, o_two, keep, keep_stats
):
    half = q.shape[0] // 2
    used = sorted({c for _, chunks, _ in work for c in chunks})
    if used[0] < 0:
        ke[0:PRE, :] = pk[...]
        vt[:, 0:PRE] = transposed(pv[...])
    first, last = max(used[0], 0) * BLOCK, (used[-1] + 1) * BLOCK
    if last > first:
        ke[PRE + first : PRE + last, :] = k[first:last, :]
        vt[:, PRE + first : PRE + last] = transposed(v[first:last, :])
    units = [(i, chunks, mode, h) for i, chunks, mode in work for h in range(2)]

    def view(u):
        return slice((u % 2) * BLOCK, (u % 2 + 1) * BLOCK)

    def kept(i):
        first = i * BLOCK % half
        return slice(first, first + BLOCK)

    def score(u):
        i, chunks, mode, h = units[u]
        rows = slice(i * BLOCK, (i + 1) * BLOCK)
        mine = head_mask(q[rows, :], h)
        start = starts[:, rows]
        peak = keep_stats[h : h + 1, kept(i)] if mode == ADD else None
        for c in chunks:
            lo, hi = key_rows(c)
            s = masked(dot_nt(ke[lo:hi, :], mine), count, start, i, c)
            s_all[lo:hi, view(u)] = s
            top = jnp.max(s, axis=0, keepdims=True)
            peak = top if peak is None else jnp.maximum(peak, top)
        return peak

    def weigh(u, peak):
        i, chunks, mode, h = units[u]
        total = 0.0
        for c in chunks:
            lo, hi = key_rows(c)
            p = jnp.exp(s_all[lo:hi, view(u)] - peak)
            total = total + jnp.sum(p, axis=0, keepdims=True)
            p_all[lo:hi, view(u)] = p.astype(low_type)
        return total

    def collect(u, peak, total):
        i, chunks, mode, h = units[u]
        lo, hi = key_rows(chunks[0])[0], key_rows(chunks[-1])[1]
        feats = slice(h * HEAD, (h + 1) * HEAD)
        part = dot(vt[feats, lo:hi], p_all[lo:hi, view(u)])
        if mode == STORE:
            keep[feats, kept(i)] = part
            keep_stats[h : h + 1, kept(i)] = peak
            keep_stats[2 + h : 3 + h, kept(i)] = total
            return
        if mode == ADD:
            shrink = jnp.exp(keep_stats[h : h + 1, kept(i)] - peak)
            total = total + shrink * keep_stats[2 + h : 3 + h, kept(i)]
            part = part + shrink * keep[feats, kept(i)]
        lse[h : h + 1, i * BLOCK : (i + 1) * BLOCK] = peak + jnp.log(total)
        o_two[i % 2, feats, :] = part / total
        if h == 1:
            out[i * BLOCK : (i + 1) * BLOCK, :] = o_two[i % 2].T.astype(low_type)

    peak = score(0)
    for u in range(len(units)):
        following = score(u + 1) if u + 1 < len(units) else None
        total = weigh(u, peak)
        collect(u, peak, total)
        peak = following


def lower_first_part(blocks):
    low, high = range(blocks // 2), range(blocks // 2, blocks)
    work = [(i, range(-1, 0)) for i in low] + [(i, range(-1, i + 1)) for i in high]
    keys = [(c, range(c, blocks), FINAL) for c in high] + [(c, high, STORE) for c in low]
    keys += [(-1, range(blocks), FINAL)]
    return work, keys, [(i, range(-1, i + 1), FINAL) for i in high]


def lower_second_part(blocks):
    low = range(blocks // 2)
    work = [(i, range(-1, i + 1)) for i in low]
    keys = [(c, range(c, blocks // 2), ADD) for c in low]
    return work, keys, [(i, range(-1, i + 1), FINAL) for i in low]


def upper_first_part(blocks):
    half = blocks // 2
    work = [(i, range(-1, min(i + 1, half))) for i in range(blocks)]
    keys = [(c, range(max(c, 0), blocks), FINAL) for c in range(-1, half)]
    queries = [(i, chunks, FINAL if i < half else STORE) for i, chunks in work]
    return work, keys, queries


def upper_second_part(blocks):
    high = range(blocks // 2, blocks)
    work = [(i, range(blocks // 2, i + 1)) for i in high]
    keys = [(c, range(c, blocks), FINAL) for c in high]
    return work, keys, [(i, chunks, ADD) for i, chunks in work]


def attention_backward_part(
    plan, count, starts, q, k, v, g, pk, pv, lse, delta, dpk, dpv, ke, ve, kt, p_all, dk, dv, keep, keep_q
):
    work, keys, queries = plan
    length = q.shape[0]
    half = length // 2
    used = sorted({c for _, chunks in work for c in chunks})
    if used[0] < 0:
        ke[0:PRE, :] = pk[...]
        ve[0:PRE, :] = pv[...]
        kt[:, 0:PRE] = transposed(pk[...])
    first, last = max(used[0], 0) * BLOCK, (used[-1] + 1) * BLOCK
    ke[PRE + first : PRE + last, :] = k[first:last, :]
    ve[PRE + first : PRE + last, :] = v[first:last, :]
    kt[:, PRE + first : PRE + last] = transposed(k[first:last, :])

    def weigh(i, chunks, h):
        rows = slice(i * BLOCK, (i + 1) * BLOCK)
        mine, grad = head_mask(q[rows, :], h), head_mask(g[rows, :], h)
        start = starts[:, rows]
        shift, middle = lse[h : h + 1, rows], delta[h : h + 1, rows]
        p_at = slice(h * length + i * BLOCK, h * length + (i + 1) * BLOCK)
        ds_at = slice((2 + h) * length + i * BLOCK, (2 + h) * length + (i + 1) * BLOCK)
        for c in chunks:
            lo, hi = key_rows(c)
            s = masked(dot_nt(ke[lo:hi, :], mine), count, start, i, c)
            p = jnp.exp(s - shift)
            p_all[lo:hi, p_at] = p.astype(low_type)
            ds = p * (dot_nt(ve[lo:hi, :], grad) - middle)
            p_all[lo:hi, ds_at] = ds.astype(low_type)

    def collect_keys(c, members, mode, h):
        lo, hi = key_rows(c)
        a, b = members[0] * BLOCK, (members[-1] + 1) * BLOCK
        mine, grad = head_mask(q[a:b, :], h), head_mask(g[a:b, :], h)
        dv_part = dot(p_all[lo:hi, h * length + a : h * length + b], grad)
        dk_part = dot(p_all[lo:hi, (2 + h) * length + a : (2 + h) * length + b], mine)
        if h == 0:
            dv[lo:hi, :] = dv_part
            dk[lo:hi, :] = dk_part
            return
        dv_part = dv[lo:hi, :] + dv_part
        dk_part = dk[lo:hi, :] + dk_part
        if c < 0:
            dpv[...] = dv_part
            dpk[...] = dk_part
            return
        rows = slice(c * BLOCK, (c + 1) * BLOCK)
        if mode == STORE:
            keep[rows, :] = dk_part
            keep[half + rows.start : half + rows.stop, :] = dv_part
            return
        if mode == ADD:
            dk_part = dk_part + keep[rows, :]
            dv_part = dv_part + keep[half + rows.start : half + rows.stop, :]
        v[rows, :] = dv_part.astype(low_type)
        k[rows, :] = dk_part.astype(low_type)

    def collect_queries(i, chunks, mode):
        lo, hi = key_rows(chunks[0])[0], key_rows(chunks[-1])[1]
        parts = []
        for h in range(2):
            feats = slice(h * HEAD, (h + 1) * HEAD)
            ds_at = slice((2 + h) * length + i * BLOCK, (2 + h) * length + (i + 1) * BLOCK)
            parts.append(dot(kt[feats, lo:hi], p_all[lo:hi, ds_at]))
        both = jnp.concatenate(parts, 0)
        kept = slice(i * BLOCK - half, (i + 1) * BLOCK - half)
        if mode == STORE:
            keep_q[:, kept] = both
            return
        if mode == ADD:
            both = both + keep_q[:, kept]
        q[i * BLOCK : (i + 1) * BLOCK, :] = (both.T * (HEAD**-0.5)).astype(low_type)

    for h in range(2):
        for i, chunks in work:
            weigh(i, chunks, h)
    for h in range(2):
        for c, members, mode in keys:
            collect_keys(c, members, mode, h)
    for i, chunks, mode in queries:
        collect_queries(i, chunks, mode)


def block_kernel(
    n,
    n_dp,
    x_hbm,
    starts_hbm,
    cot_hbm,
    w_qkv_hbm,
    w_out_hbm,
    w_fc_hbm,
    w_proj_hbm,
    gain1_ref,
    shift1_ref,
    b_qkv_ref,
    b_out_ref,
    gain2_ref,
    shift2_ref,
    b_fc_ref,
    b_proj_ref,
    table_ref,
    w1_ref,
    b1_ref,
    w2_ref,
    b2_ref,
    out_hbm,
    grad_hbm,
    table_out,
    gw1_out,
    gb1_out,
    gw2_out,
    gb2_out,
    x_rows,
    cot_rows,
    q_s,
    k_s,
    v_s,
    a_s,
    g_s,
    mid,
    h_rows,
    acc_a,
    slope,
    w_qkv,
    w_out,
    w_fc,
    w_proj,
    lse,
    delta,
    ke,
    ve,
    kt,
    dk,
    dv,
    starts_slots,
    starts_row,
    own_pre,
    pre_slots,
    pk_s,
    pv_s,
    hid,
    dp_pre,
    col_slots,
    dp_own,
    dp_slots,
    hid_own,
    hid_slots,
    o_two,
    keep_stats,
    x_send,
    x_recv,
    s_send,
    s_recv,
    p_send,
    p_recv,
    c_send,
    c_recv,
    o_send,
    o_recv,
    g_send,
    g_recv,
    r_send,
    r_recv,
    d_send,
    d_recv,
    e_send,
    e_recv,
    local_sem,
    fc_sem,
    proj_sem,
    x_here,
    cot_here,
):
    me, me_dp = lax.axis_index("col"), lax.axis_index("dp")
    piece, width = x_hbm.shape[1], x_hbm.shape[2]
    length = n * piece
    blocks = length // BLOCK
    pairs = width // PAIR
    inner = b_fc_ref.shape[0]
    tile = w_fc.shape[2]
    tiles = inner // tile
    rows_pre = table_ref.shape[0]
    group = BLOCK // piece
    part_width = w2_ref.shape[1]
    per_part = part_width // PAIR
    groups = n // group
    heads = 2 * pairs

    def spot(at):
        return pl.ds(pl.multiple_of(at * piece, piece), piece)

    def each(count, step):
        def body(k, carry):
            step(k)
            return carry

        lax.fori_loop(0, count, body, 0)

    reach = n // 2
    mine_base = lax.div(me, reach) * reach
    other_base = reach - mine_base
    seat = lax.rem(me, reach)

    def to(m):
        same = lax.div(m, reach)
        step = lax.rem(m, reach) + same
        there, bit = other_base + same * (mine_base - other_base), 1
        while bit < reach:
            differ = lax.rem(lax.div(seat, bit) + lax.div(step, bit), 2)
            there, bit = there + differ * bit, 2 * bit
        return there

    source = to

    def remote(src, dst, send, recv, d, axis, peer):
        return pltpu.make_async_remote_copy(
            src_ref=src,
            dst_ref=dst,
            send_sem=send.at[d],
            recv_sem=recv.at[d],
            device_id={axis: peer},
            device_id_type=MESH,
        )

    def vector(ref):
        return ref[...].astype(wide).reshape(1, -1)

    def fc_load(t, slot):
        cols = pl.ds(pl.multiple_of(t * tile, tile), tile)
        return pltpu.make_async_copy(w_fc_hbm.at[:, cols], w_fc.at[slot], fc_sem.at[slot])

    def proj_load(t, slot):
        rows = pl.ds(pl.multiple_of(t * tile, tile), tile)
        return pltpu.make_async_copy(w_proj_hbm.at[rows, :], w_proj.at[slot], proj_sem.at[slot])

    load_qkv = pltpu.make_async_copy(w_qkv_hbm, w_qkv, local_sem.at[0])
    load_qkv.start()
    barrier = pltpu.get_barrier_semaphore()
    for m in range(n - 1):
        peer = to(jnp.int32(m))
        pl.semaphore_signal(barrier, inc=1, device_id={"col": peer}, device_id_type=MESH)
    for d in range(1, n_dp):
        pl.semaphore_signal(
            barrier, inc=1, device_id={"dp": lax.rem(me_dp + d, n_dp)}, device_id_type=MESH
        )
    pl.semaphore_wait(barrier, n - 1 + n_dp - 1)

    def x_copy(d, peer):
        return remote(x_hbm.at[peer], x_rows.at[spot(me), :], x_send, x_recv, d, "col", peer)

    def starts_copy(d, peer):
        return remote(starts_hbm, starts_slots.at[me], s_send, s_recv, d, "col", peer)

    def pre_copy(d, peer):
        return remote(own_pre, pre_slots.at[me], p_send, p_recv, d, "col", peer)

    def cot_copy(d, peer):
        return remote(cot_hbm.at[peer], cot_rows.at[spot(me), :], c_send, c_recv, d, "col", peer)

    def out_copy(d, peer):
        return remote(h_rows.at[spot(peer), :], out_hbm.at[me], o_send, o_recv, d, "col", peer)

    def grad_copy(d, here, peer):
        return remote(here, grad_hbm.at[me], g_send, g_recv, d, "col", peer)

    def send_inputs(m):
        x_copy(m, to(m)).start()
        starts_copy(m, to(m)).start()

    each(n - 1, send_inputs)
    own_x = pltpu.make_async_copy(x_hbm.at[me], x_rows.at[spot(me), :], local_sem.at[1])
    own_x.start()
    own_cot = pltpu.make_async_copy(cot_hbm.at[me], cot_rows.at[spot(me), :], local_sem.at[2])
    own_cot.start()
    own_starts = pltpu.make_async_copy(starts_hbm, starts_slots.at[me], local_sem.at[3])
    own_starts.start()
    load_out = pltpu.make_async_copy(w_out_hbm, w_out, local_sem.at[4])
    load_out.start()
    fc_load(0, 0).start()
    proj_load(0, 0).start()

    hidden = jnp.tanh(
        dot(table_ref[...].astype(low_type), w1_ref[...].astype(low_type)) + vector(b1_ref)
    )
    hid[...] = jnp.concatenate([hidden, jnp.zeros((PRE - rows_pre, hidden.shape[1]), wide)], 0)
    own = dot(hidden.astype(low_type), w2_ref[...].astype(low_type)) + vector(b2_ref)
    own = jnp.concatenate([own, jnp.zeros((PRE - rows_pre, part_width), wide)], 0).astype(low_type)
    own_pre[...] = own
    pre_slots[me] = own
    each(n - 1, lambda m: pre_copy(m, to(m)).start())

    gain1, shift1 = vector(gain1_ref), vector(shift1_ref)
    own_x.wait()
    load_qkv.wait()

    def greet_peers(sem):
        def greet(m):
            pl.semaphore_signal(sem, inc=1, device_id={"col": to(m)}, device_id_type=MESH)

        each(n - 1, greet)

    span = n // 2
    rows_span = span * piece

    def starts_of(first):
        for j in range(first, first + reach):
            starts_row[:, j * piece : (j + 1) * piece] = starts_slots[j, pl.ds(me, 1), :]

    def by_half(lower, upper):
        @pl.when(me < reach)
        def _():
            lower()

        @pl.when(me >= reach)
        def _():
            upper()

    def forward_loop(work):
        def forward_pair(p):
            attention_forward_part(
                work,
                rows_pre,
                starts_row,
                q_s.at[p],
                k_s.at[p],
                v_s.at[p],
                pk_s.at[p],
                pv_s.at[p],
                a_s.at[p],
                lse.at[p],
                ke,
                kt,
                acc_a,
                slope,
                o_two,
                mid.at[pl.ds(pl.multiple_of(p * PAIR, PAIR), PAIR), :],
                keep_stats.at[p],
            )

        each(pairs, forward_pair)

    def catch_starts(m):
        peer = source(m)
        remote(starts_hbm, starts_slots.at[peer], s_send, s_recv, m, "col", peer).wait_recv()

    def send_cotangent():
        pl.semaphore_wait(x_here, n - 1)
        each(n - 1, lambda m: cot_copy(m, to(m)).start())

    def qkv_group(g):
        places = []
        for j in range(span):
            d = n - 1 - (g * span + j)
            rows = spot(source(d))
            places.append(rows)

            @pl.when(d < n - 1)
            def _():
                remote(
                    x_hbm.at[me], x_rows.at[rows, :], x_send, x_recv, d, "col", source(d)
                ).wait_recv()

            normed, _ = standardize(x_rows[rows, :].astype(wide))
            h_rows[j * piece : (j + 1) * piece, :] = (normed * gain1 + shift1).astype(low_type)

        @pl.when(g == 1)
        def _():
            greet_peers(x_here)

        normed = h_rows[0:rows_span, :]
        for c in range(0, 3 * width, width // 2):
            part = dot(normed, w_qkv[:, c : c + width // 2])
            part = part + b_qkv_ref[c : c + width // 2].astype(wide).reshape(1, -1)
            if c < width:
                part = part * (HEAD**-0.5)
            part = part.astype(low_type)
            slabs = (q_s, k_s, v_s)[c // width]
            for m in range(width // 2 // PAIR):
                pair = (c % width) // PAIR + m
                for j in range(span):
                    slabs[pair, places[j], :] = part[
                        j * piece : (j + 1) * piece, m * PAIR : (m + 1) * PAIR
                    ]
            if c == width // 2:
                pl.when(g == 1)(send_cotangent)

        @pl.when(g == 0)
        def _():
            each(reach - 1, lambda m: catch_starts(reach + m))
            own_starts.wait()
            by_half(lambda: starts_of(0), lambda: starts_of(reach))
            by_half(
                lambda: forward_loop(own_half_part(blocks, False)),
                lambda: forward_loop(own_half_part(blocks, True)),
            )

    each(2, qkv_group)

    each(reach, catch_starts)
    by_half(lambda: starts_of(reach), lambda: starts_of(0))

    def catch_prefix(m):
        peer = source(m)
        remote(own_pre, pre_slots.at[peer], p_send, p_recv, m, "col", peer).wait_recv()

    each(n - 1, catch_prefix)
    for j in range(n):
        for m in range(per_part):
            pair = j * per_part + m
            slab = pre_slots[j][:, m * PAIR : (m + 1) * PAIR]
            if pair < pairs:
                pk_s[pair] = slab
            else:
                pv_s[pair - pairs] = slab

    by_half(
        lambda: forward_loop(other_part(blocks, False)),
        lambda: forward_loop(other_part(blocks, True)),
    )

    load_out.wait()
    gain2, shift2 = vector(gain2_ref), vector(shift2_ref)
    big = 2 * BLOCK
    halves = [slice(r, r + big) for r in range(0, length, big)]

    def pairwise(step):
        def two(b):
            step(2 * b)
            step(2 * b + 1)

        each(blocks // 2, two)

    def project(b):
        r = pl.ds(pl.multiple_of(b * BLOCK, BLOCK), BLOCK)
        att = jnp.concatenate([a_s[p, r, :] for p in range(pairs)], axis=1)
        middle = x_rows[r, :].astype(wide) + dot(att, w_out[...]) + vector(b_out_ref)
        mid[r, :] = middle
        normed, _ = standardize(middle)
        h_rows[r, :] = (normed * gain2 + shift2).astype(low_type)
        acc_a[r, :] = middle + vector(b_proj_ref)

    pairwise(project)

    def forward_tile(t):
        slot = lax.rem(t, 2)
        fc_load(t, slot).wait()
        proj_load(t, slot).wait()

        @pl.when(t + 1 < tiles)
        def _():
            fc_load(t + 1, 1 - slot).start()
            proj_load(t + 1, 1 - slot).start()

        cols = pl.ds(pl.multiple_of(t * tile, tile), tile)
        bias = b_fc_ref[cols].astype(wide).reshape(1, -1)

        for r in halves:
            upper = dot(h_rows[r, :], w_fc[slot]) + bias
            value, steep = gelu_parts(upper)
            slope[r, cols] = steep.astype(low_type)
            acc_a[r, :] += dot(value.astype(low_type), w_proj[slot])

    each(tiles, forward_tile)

    def settle(b):
        r = pl.ds(pl.multiple_of(b * BLOCK, BLOCK), BLOCK)
        h_rows[r, :] = acc_a[r, :].astype(low_type)
        acc_a[r, :] = jnp.zeros((BLOCK, width), wide)

    each(blocks, settle)
    own_out = pltpu.make_async_copy(h_rows.at[spot(me), :], out_hbm.at[me], local_sem.at[5])
    own_out.start()
    own_cot.wait()

    def catch_cot(m):
        d = m
        peer = source(d)
        remote(
            cot_hbm.at[me], cot_rows.at[spot(peer), :], c_send, c_recv, d, "col", peer
        ).wait_recv()

    each(n - 1, catch_cot)
    greet_peers(cot_here)


    def backward_tile(step):
        t = tiles - 1 - step
        slot = lax.rem(t, 2)

        @pl.when(step >= 2)
        def _():
            fc_load(t, slot).wait()
            proj_load(t, slot).wait()

        @pl.when(step == 1)
        def _():
            pl.semaphore_wait(cot_here, n - 1)
            each(n - 1, lambda m: out_copy(m, to(m)).start())

        cols = pl.ds(pl.multiple_of(t * tile, tile), tile)
        for r in halves:
            grad_act = dot_nt(cot_rows[r, :], w_proj[slot])
            grad_upper = (grad_act * slope[r, cols].astype(wide)).astype(low_type)
            acc_a[r, :] += dot_nt(grad_upper, w_fc[slot])

        @pl.when(t >= 2)
        def _():
            fc_load(t - 2, slot).start()
            proj_load(t - 2, slot).start()

    each(tiles, backward_tile)
    feature_head = lax.broadcasted_iota(jnp.int32, (heads, width), 1) // HEAD
    which = lax.broadcasted_iota(jnp.int32, (heads, width), 0)
    member = jnp.where(feature_head == which, 1.0, 0.0).astype(low_type)

    def attend_gradient(b):
        r = pl.ds(pl.multiple_of(b * BLOCK, BLOCK), BLOCK)
        normed, inverse = standardize(mid[r, :])
        grad_mid = cot_rows[r, :].astype(wide) + norm_backward_pass(
            acc_a[r, :], gain2, normed, inverse
        )
        mid[r, :] = grad_mid
        grad_att = dot_nt(grad_mid.astype(low_type), w_out[...]).astype(low_type)
        att = jnp.concatenate([a_s[p, r, :] for p in range(pairs)], axis=1)
        both = grad_att.astype(wide) * att.astype(wide)
        both_low = both.astype(low_type)
        rest = (both - both_low.astype(wide)).astype(low_type)
        sums = dot_nt(member, both_low) + dot_nt(member, rest)
        for p in range(pairs):
            g_s[p, r, :] = grad_att[:, p * PAIR : (p + 1) * PAIR]
            delta[p, :, r] = sums[2 * p : 2 * p + 2, :]

    pairwise(attend_gradient)

    def backward_loop(plan):
        def backward_pair(p):
            lanes = pl.ds(pl.multiple_of(p * PAIR, PAIR), PAIR)
            attention_backward_part(
                plan,
                rows_pre,
                starts_row,
                q_s.at[p],
                k_s.at[p],
                v_s.at[p],
                g_s.at[p],
                pk_s.at[p],
                pv_s.at[p],
                lse.at[p],
                delta.at[p],
                dp_pre.at[p],
                dp_pre.at[pairs + p],
                ke,
                ve,
                kt,
                slope,
                dk,
                dv,
                acc_a.at[:, lanes],
                acc_a.at[lanes, :],
            )

        each(pairs, backward_pair)

    def backward_by_half(lower, upper):
        by_half(lambda: backward_loop(lower(blocks)), lambda: backward_loop(upper(blocks)))

    backward_by_half(lower_first_part, upper_first_part)

    def part_copy(d, peer):
        mine = dp_pre.at[pl.ds(peer * per_part, per_part)]
        return remote(mine, col_slots.at[me], r_send, r_recv, d, "col", peer)

    def dp_copy(d, peer):
        return remote(dp_own, dp_slots.at[me_dp], d_send, d_recv, d, "dp", peer)

    def hid_copy(d, peer):
        return remote(hid_own, hid_slots.at[me], e_send, e_recv, d, "col", peer)

    def sum_slots(slots, count):
        return lax.fori_loop(1, count, lambda j, total: total + slots[j], slots[0])

    def gradient_group(g):
        grads, places = [], []
        for j in range(group):
            rows = spot(to(g * group + j))
            places.append(rows)
            grads.append(
                jnp.concatenate(
                    [slabs[p, rows, :] for slabs in (q_s, k_s, v_s) for p in range(pairs)], axis=1
                )
            )
        back = dot_nt(jnp.concatenate(grads, axis=0), w_qkv[...])
        for j in range(group):
            at = g * group + j
            rows = places[j]
            normed, inverse = standardize(x_rows[rows, :].astype(wide))
            total = mid[rows, :] + norm_backward_pass(
                back[j * piece : (j + 1) * piece, :], gain1, normed, inverse
            )
            cot_rows[spot(at), :] = total.astype(low_type)

    def send_gradient(m):
        here = cot_rows.at[spot(m), :]

        @pl.when(m < n - 1)
        def _():
            grad_copy(m, here, to(m)).start()

        @pl.when(m == n - 1)
        def _():
            pltpu.make_async_copy(here, grad_hbm.at[me], local_sem.at[6]).start()

    def leave_step(part):
        def one_group(g):
            at = part * (groups // 2) + g
            gradient_group(at)
            each(group, lambda j: send_gradient(at * group + j))

        each(groups // 2, one_group)

        @pl.when(part == 0)
        def _():
            backward_by_half(lower_second_part, upper_second_part)

    each(n - 1, lambda m: part_copy(m, to(m)).start())
    col_slots[me] = dp_pre[pl.ds(me * per_part, per_part)]
    each(2, leave_step)

    def catch_part(m):
        peer = source(m)
        mine = dp_pre.at[pl.ds(me * per_part, per_part)]
        remote(mine, col_slots.at[peer], r_send, r_recv, m, "col", peer).wait_recv()

    each(n - 1, catch_part)
    total = sum_slots(col_slots, n)
    total = jnp.concatenate([total[m] for m in range(per_part)], axis=1)
    dp_own[...] = total
    dp_slots[me_dp] = total
    for d in range(1, n_dp):
        dp_copy(d, lax.rem(me_dp + d, n_dp)).start()
    for d in range(1, n_dp):
        peer = lax.rem(me_dp + n_dp - d, n_dp)
        remote(dp_own, dp_slots.at[peer], d_send, d_recv, d, "dp", peer).wait_recv()
    own_low = sum_slots(dp_slots, n_dp).astype(low_type)
    part = dot_nt(own_low, w2_ref[...].astype(low_type))
    hid_own[...] = part
    hid_slots[me] = part
    each(n - 1, lambda m: hid_copy(m, to(m)).start())

    hidden = hid[...]
    gw2_out[...] = lax.dot_general(
        hidden.astype(low_type), own_low, TN, preferred_element_type=wide
    )
    gb2_out[...] = jnp.sum(own_low.astype(wide), axis=0)

    def catch_hid(m):
        peer = source(m)
        remote(hid_own, hid_slots.at[peer], e_send, e_recv, m, "col", peer).wait_recv()

    each(n - 1, catch_hid)
    grad_pre = (sum_slots(hid_slots, n) * (1.0 - hidden * hidden)).astype(low_type)
    table = jnp.concatenate(
        [table_ref[...], jnp.zeros((PRE - rows_pre, table_ref.shape[1]), wide)], 0
    ).astype(low_type)
    gw1_out[...] = lax.dot_general(table, grad_pre, TN, preferred_element_type=wide)
    gb1_out[...] = jnp.sum(grad_pre.astype(wide), axis=0)
    table_out[...] = dot_nt(grad_pre, w1_ref[...].astype(low_type))[:rows_pre, :]

    def finish(m):
        peer, here = source(m), cot_rows.at[0:piece, :]
        remote(here, out_hbm.at[peer], o_send, o_recv, m, "col", peer).wait_recv()
        x_copy(m, to(m)).wait_send()
        starts_copy(m, to(m)).wait_send()
        pre_copy(m, to(m)).wait_send()
        cot_copy(m, to(m)).wait_send()
        out_copy(m, to(m)).wait_send()
        part_copy(m, to(m)).wait_send()
        hid_copy(m, to(m)).wait_send()

    each(n - 1, finish)
    for d in range(1, n_dp):
        dp_copy(d, lax.rem(me_dp + d, n_dp)).wait_send()
    own_out.wait()
    pltpu.make_async_copy(cot_rows.at[0:piece, :], grad_hbm.at[me], local_sem.at[6]).wait()

    def finish_gradient(m):
        peer, here = source(m), cot_rows.at[0:piece, :]
        remote(here, grad_hbm.at[peer], g_send, g_recv, m, "col", peer).wait_recv()
        grad_copy(m, here, to(m)).wait_send()

    each(n - 1, finish_gradient)


def hand_over_kernel(count, *refs):
    given, wanted, held = refs[:count], refs[count : 2 * count], refs[2 * count : 3 * count]
    sems = refs[3 * count]
    come = [pltpu.make_async_copy(given[j], held[j], sems.at[0, j]) for j in range(count)]
    go = [pltpu.make_async_copy(held[j], wanted[j], sems.at[1, j]) for j in range(count)]
    for copy in come:
        copy.start()
    for arrived, copy in zip(come, go):
        arrived.wait()
        copy.start()
    for copy in go:
        copy.wait()


def hand_over(results):
    results = list(results)
    count = len(results)
    return tuple(
        pl.pallas_call(
            functools.partial(hand_over_kernel, count),
            in_specs=[ANY] * count,
            out_specs=[ANY] * count,
            out_shape=[jax.ShapeDtypeStruct(r.shape, r.dtype) for r in results],
            scratch_shapes=[pltpu.VMEM(r.shape, r.dtype) for r in results]
            + [pltpu.SemaphoreType.DMA((2, count))],
            compiler_params=pltpu.CompilerParams(vmem_limit_bytes=VMEM_BYTES),
        )(*results)
    )


def on_device(*operands):
    n, n_dp = lax.axis_size("col"), lax.axis_size("dp")
    inputs, starts, cotangent, w_qkv, w_out = [operands[j] for j in (0, 1, 2, 5, 7)]
    w_fc, w_proj, table, w1, w2 = [operands[j] for j in (11, 13, 15, 16, 18)]
    row_count, piece, width = inputs.shape
    assert row_count == n and BLOCK % piece == 0
    length, inner = n * piece, w_fc.shape[1]
    pairs, tile = width // PAIR, min(1024, inner)
    part_width, mid_width = w2.shape[1], w1.shape[1]
    per_part = part_width // PAIR
    ext = PRE + length
    dma = pltpu.SemaphoreType.DMA
    shape = jax.ShapeDtypeStruct
    vmem = pltpu.VMEM
    slabs = vmem((pairs, length, PAIR), low_type)
    ordered = [operands[j] for j in (0, 1, 2, 5, 7, 11, 13)]
    ordered += [operands[j] for j in (3, 4, 6, 8, 9, 10, 12, 14, 15, 16, 17, 18, 19)]
    return hand_over(
        pl.pallas_call(
            functools.partial(block_kernel, n, n_dp),
            in_specs=[ANY] * 7 + [VM] * 13,
            out_specs=[ANY, ANY] + [VM] * 5,
            out_shape=[
                shape((n, piece, width), low_type),
                shape((n, piece, width), low_type),
                shape(table.shape, wide),
                shape(w1.shape, wide),
                shape((mid_width,), wide),
                shape(w2.shape, wide),
                shape((part_width,), wide),
            ],
            scratch_shapes=[
                vmem((length, width), low_type),
                vmem((length, width), low_type),
                slabs,
                slabs,
                slabs,
                slabs,
                slabs,
                vmem((length, width), wide),
                vmem((length, width), low_type),
                vmem((ext, width), wide),
                vmem((ext, inner), low_type),
                vmem(w_qkv.shape, low_type),
                vmem(w_out.shape, low_type),
                vmem((2, width, tile), low_type),
                vmem((2, tile, width), low_type),
                vmem((pairs, 2, length), wide),
                vmem((pairs, 2, length), wide),
                vmem((ext, PAIR), low_type),
                vmem((ext, PAIR), low_type),
                vmem((PAIR, ext), low_type),
                vmem((ext, PAIR), wide),
                vmem((ext, PAIR), wide),
                vmem((n,) + starts.shape, jnp.int32),
                vmem((1, length), jnp.int32),
                vmem((PRE, part_width), low_type),
                vmem((n, PRE, part_width), low_type),
                vmem((pairs, PRE, PAIR), low_type),
                vmem((pairs, PRE, PAIR), low_type),
                vmem((PRE, mid_width), wide),
                vmem((2 * pairs, PRE, PAIR), wide),
                vmem((n, per_part, PRE, PAIR), wide),
                vmem((PRE, part_width), wide),
                vmem((n_dp, PRE, part_width), wide),
                vmem((PRE, mid_width), wide),
                vmem((n, PRE, mid_width), wide),
                vmem((2, PAIR, BLOCK), wide),
                vmem((pairs, 4, length // 2), wide),
            ]
            + [dma((n,))] * 14
            + [dma((n_dp,))] * 2
            + [dma((n,))] * 2
            + [dma((7,)), dma((2,)), dma((2,))]
            + [pltpu.SemaphoreType.REGULAR] * 2,
            compiler_params=pltpu.CompilerParams(
                collective_id=0, has_side_effects=True, vmem_limit_bytes=VMEM_BYTES
            ),
        )(*ordered)
    )


def solution(mesh):
    rows = P("dp", "col", None)
    return jax.shard_map(
        on_device,
        mesh=mesh,
        in_specs=(rows, P("dp", "col"), rows) + (P(),) * 15 + (P(None, "col"), P("col")),
        out_specs=(rows, rows, P(), P(), P(), P(None, "col"), P("col")),
        check_vma=False,
    )
```

```python
import functools

import jax
import jax.numpy as jnp
from jax import lax
from jax.experimental import pallas as pl
from jax.experimental.pallas import tpu as pltpu
from jax.sharding import PartitionSpec as P

H = 16
HEAD = 64
PAIR = 2 * HEAD
BLOCK = 256
PRE = 16
VMEM_BYTES = 62 << 20

epsilon = 1e-05
gelu_coef = 0.7978845608028654
cubic_coef = 0.044715
low_type = jnp.bfloat16
wide = jnp.float32
NT = (((1,), (1,)), ((), ()))
TN = (((0,), (0,)), ((), ()))
MESH = pl.DeviceIdType.MESH
ANY = pl.BlockSpec(memory_space=pl.ANY)
VM = pl.BlockSpec(memory_space=pltpu.VMEM)


def standardize(values):
    center = values - jnp.mean(values, axis=-1, keepdims=True)
    inverse = lax.rsqrt(jnp.mean(center * center, axis=-1, keepdims=True) + epsilon)
    return center * inverse, inverse


def norm_backward_pass(gradient, norm_gain, normed, inverse):
    scaled = gradient * norm_gain
    centered = scaled - jnp.mean(scaled, axis=-1, keepdims=True)
    return inverse * (centered - normed * jnp.mean(scaled * normed, axis=-1, keepdims=True))


def gelu_parts(upper):
    square = upper * upper
    tangent = jnp.tanh(upper * (gelu_coef + (gelu_coef * cubic_coef) * square))
    half = 0.5 * upper
    share = 0.5 + 0.5 * tangent
    slope = share + half * (1.0 - tangent * tangent) * (
        gelu_coef + (3.0 * gelu_coef * cubic_coef) * square
    )
    return upper * share, slope


def dot_nt(a, b):
    return lax.dot_general(a, b, NT, preferred_element_type=wide)


def dot(a, b):
    return jnp.dot(a, b, preferred_element_type=wide)


def head_mask(values, which):
    lane = lax.broadcasted_iota(jnp.int32, values.shape, 1)
    keep = (lane < HEAD) if which == 0 else (lane >= HEAD)
    return jnp.where(keep, values, jnp.zeros_like(values))


def token_mask(scores, start, block_q, block_k):
    key = block_k * BLOCK + lax.broadcasted_iota(jnp.int32, scores.shape, 0)
    keep = key >= start
    if block_q == block_k:
        query = block_q * BLOCK + lax.broadcasted_iota(jnp.int32, scores.shape, 1)
        keep = keep & (key <= query)
    return jnp.where(keep, scores, -jnp.inf)


def prefix_mask(scores, count):
    key = lax.broadcasted_iota(jnp.int32, scores.shape, 0)
    return jnp.where(key < count, scores, -jnp.inf)


def masked(scores, count, start, block_q, block_k):
    if block_k < 0:
        return prefix_mask(scores, count)
    return token_mask(scores, start, block_q, block_k)


def key_chunks(block_q):
    tokens = [(c, PRE + c * BLOCK, PRE + (c + 1) * BLOCK) for c in range(block_q + 1)]
    return [(-1, 0, PRE)] + tokens


def transposed(values):
    return values.astype(wide).T.astype(low_type)


FINAL, STORE, ADD = range(3)


def own_half_part(blocks, upper):
    first, last = (blocks // 2, blocks) if upper else (0, blocks // 2)
    return [(i, range(first, i + 1), STORE) for i in range(first, last)]


def other_part(blocks, upper):
    half = blocks // 2
    if upper:
        work = [(i, range(-1, i + 1), FINAL) for i in range(half)]
        return work + [(i, range(-1, half), ADD) for i in range(half, blocks)]
    work = [(i, range(-1, 0), ADD) for i in range(half)]
    return work + [(i, range(-1, i + 1), FINAL) for i in range(half, blocks)]


def key_rows(c):
    return (0, PRE) if c < 0 else (PRE + c * BLOCK, PRE + (c + 1) * BLOCK)


def attention_forward_part(
    work, count, starts, q, k, v, pk, pv, out, lse, ke, vt, s_all, p_all, o_two, keep, keep_stats
):
    half = q.shape[0] // 2
    used = sorted({c for _, chunks, _ in work for c in chunks})
    if used[0] < 0:
        ke[0:PRE, :] = pk[...]
        vt[:, 0:PRE] = transposed(pv[...])
    first, last = max(used[0], 0) * BLOCK, (used[-1] + 1) * BLOCK
    if last > first:
        ke[PRE + first : PRE + last, :] = k[first:last, :]
        vt[:, PRE + first : PRE + last] = transposed(v[first:last, :])
    units = [(i, chunks, mode, h) for i, chunks, mode in work for h in range(2)]

    def view(u):
        return slice((u % 2) * BLOCK, (u % 2 + 1) * BLOCK)

    def kept(i):
        first = i * BLOCK % half
        return slice(first, first + BLOCK)

    def score(u):
        i, chunks, mode, h = units[u]
        rows = slice(i * BLOCK, (i + 1) * BLOCK)
        mine = head_mask(q[rows, :], h)
        start = starts[:, rows]
        peak = keep_stats[h : h + 1, kept(i)] if mode == ADD else None
        for c in chunks:
            lo, hi = key_rows(c)
            s = masked(dot_nt(ke[lo:hi, :], mine), count, start, i, c)
            s_all[lo:hi, view(u)] = s
            top = jnp.max(s, axis=0, keepdims=True)
            peak = top if peak is None else jnp.maximum(peak, top)
        return peak

    def weigh(u, peak):
        i, chunks, mode, h = units[u]
        total = 0.0
        for c in chunks:
            lo, hi = key_rows(c)
            p = jnp.exp(s_all[lo:hi, view(u)] - peak)
            total = total + jnp.sum(p, axis=0, keepdims=True)
            p_all[lo:hi, view(u)] = p.astype(low_type)
        return total

    def collect(u, peak, total):
        i, chunks, mode, h = units[u]
        lo, hi = key_rows(chunks[0])[0], key_rows(chunks[-1])[1]
        feats = slice(h * HEAD, (h + 1) * HEAD)
        part = dot(vt[feats, lo:hi], p_all[lo:hi, view(u)])
        if mode == STORE:
            keep[feats, kept(i)] = part
            keep_stats[h : h + 1, kept(i)] = peak
            keep_stats[2 + h : 3 + h, kept(i)] = total
            return
        if mode == ADD:
            shrink = jnp.exp(keep_stats[h : h + 1, kept(i)] - peak)
            total = total + shrink * keep_stats[2 + h : 3 + h, kept(i)]
            part = part + shrink * keep[feats, kept(i)]
        lse[h : h + 1, i * BLOCK : (i + 1) * BLOCK] = peak + jnp.log(total)
        o_two[i % 2, feats, :] = part / total
        if h == 1:
            out[i * BLOCK : (i + 1) * BLOCK, :] = o_two[i % 2].T.astype(low_type)

    peak = score(0)
    for u in range(len(units)):
        following = score(u + 1) if u + 1 < len(units) else None
        total = weigh(u, peak)
        collect(u, peak, total)
        peak = following


def lower_first_part(blocks):
    low, high = range(blocks // 2), range(blocks // 2, blocks)
    work = [(i, range(-1, 0)) for i in low] + [(i, range(-1, i + 1)) for i in high]
    keys = [(c, range(c, blocks), FINAL) for c in high] + [(c, high, STORE) for c in low]
    keys += [(-1, range(blocks), FINAL)]
    return work, keys, [(i, range(-1, i + 1), FINAL) for i in high]


def lower_second_part(blocks):
    low = range(blocks // 2)
    work = [(i, range(-1, i + 1)) for i in low]
    keys = [(c, range(c, blocks // 2), ADD) for c in low]
    return work, keys, [(i, range(-1, i + 1), FINAL) for i in low]


def upper_first_part(blocks):
    half = blocks // 2
    work = [(i, range(-1, min(i + 1, half))) for i in range(blocks)]
    keys = [(c, range(max(c, 0), blocks), FINAL) for c in range(-1, half)]
    queries = [(i, chunks, FINAL if i < half else STORE) for i, chunks in work]
    return work, keys, queries


def upper_second_part(blocks):
    high = range(blocks // 2, blocks)
    work = [(i, range(blocks // 2, i + 1)) for i in high]
    keys = [(c, range(c, blocks), FINAL) for c in high]
    return work, keys, [(i, chunks, ADD) for i, chunks in work]


def attention_backward_part(
    plan, count, starts, q, k, v, g, pk, pv, lse, delta, dpk, dpv, ke, ve, kt, p_all, dk, dv, keep, keep_q
):
    work, keys, queries = plan
    length = q.shape[0]
    half = length // 2
    used = sorted({c for _, chunks in work for c in chunks})
    if used[0] < 0:
        ke[0:PRE, :] = pk[...]
        ve[0:PRE, :] = pv[...]
        kt[:, 0:PRE] = transposed(pk[...])
    first, last = max(used[0], 0) * BLOCK, (used[-1] + 1) * BLOCK
    ke[PRE + first : PRE + last, :] = k[first:last, :]
    ve[PRE + first : PRE + last, :] = v[first:last, :]
    kt[:, PRE + first : PRE + last] = transposed(k[first:last, :])

    def weigh(i, chunks, h):
        rows = slice(i * BLOCK, (i + 1) * BLOCK)
        mine, grad = head_mask(q[rows, :], h), head_mask(g[rows, :], h)
        start = starts[:, rows]
        shift, middle = lse[h : h + 1, rows], delta[h : h + 1, rows]
        p_at = slice(h * length + i * BLOCK, h * length + (i + 1) * BLOCK)
        ds_at = slice((2 + h) * length + i * BLOCK, (2 + h) * length + (i + 1) * BLOCK)
        for c in chunks:
            lo, hi = key_rows(c)
            s = masked(dot_nt(ke[lo:hi, :], mine), count, start, i, c)
            p = jnp.exp(s - shift)
            p_all[lo:hi, p_at] = p.astype(low_type)
            ds = p * (dot_nt(ve[lo:hi, :], grad) - middle)
            p_all[lo:hi, ds_at] = ds.astype(low_type)

    def collect_keys(c, members, mode, h):
        lo, hi = key_rows(c)
        a, b = members[0] * BLOCK, (members[-1] + 1) * BLOCK
        mine, grad = head_mask(q[a:b, :], h), head_mask(g[a:b, :], h)
        dv_part = dot(p_all[lo:hi, h * length + a : h * length + b], grad)
        dk_part = dot(p_all[lo:hi, (2 + h) * length + a : (2 + h) * length + b], mine)
        if h == 0:
            dv[lo:hi, :] = dv_part
            dk[lo:hi, :] = dk_part
            return
        dv_part = dv[lo:hi, :] + dv_part
        dk_part = dk[lo:hi, :] + dk_part
        if c < 0:
            dpv[...] = dv_part
            dpk[...] = dk_part
            return
        rows = slice(c * BLOCK, (c + 1) * BLOCK)
        if mode == STORE:
            keep[rows, :] = dk_part
            keep[half + rows.start : half + rows.stop, :] = dv_part
            return
        if mode == ADD:
            dk_part = dk_part + keep[rows, :]
            dv_part = dv_part + keep[half + rows.start : half + rows.stop, :]
        v[rows, :] = dv_part.astype(low_type)
        k[rows, :] = dk_part.astype(low_type)

    def collect_queries(i, chunks, mode):
        lo, hi = key_rows(chunks[0])[0], key_rows(chunks[-1])[1]
        parts = []
        for h in range(2):
            feats = slice(h * HEAD, (h + 1) * HEAD)
            ds_at = slice((2 + h) * length + i * BLOCK, (2 + h) * length + (i + 1) * BLOCK)
            parts.append(dot(kt[feats, lo:hi], p_all[lo:hi, ds_at]))
        both = jnp.concatenate(parts, 0)
        kept = slice(i * BLOCK - half, (i + 1) * BLOCK - half)
        if mode == STORE:
            keep_q[:, kept] = both
            return
        if mode == ADD:
            both = both + keep_q[:, kept]
        q[i * BLOCK : (i + 1) * BLOCK, :] = (both.T * (HEAD**-0.5)).astype(low_type)

    for h in range(2):
        for i, chunks in work:
            weigh(i, chunks, h)
    for h in range(2):
        for c, members, mode in keys:
            collect_keys(c, members, mode, h)
    for i, chunks, mode in queries:
        collect_queries(i, chunks, mode)


def block_kernel(
    n,
    n_dp,
    x_hbm,
    starts_hbm,
    cot_hbm,
    w_qkv_hbm,
    w_out_hbm,
    w_fc_hbm,
    w_proj_hbm,
    gain1_ref,
    shift1_ref,
    b_qkv_ref,
    b_out_ref,
    gain2_ref,
    shift2_ref,
    b_fc_ref,
    b_proj_ref,
    table_ref,
    w1_ref,
    b1_ref,
    w2_ref,
    b2_ref,
    out_hbm,
    grad_hbm,
    table_out,
    gw1_out,
    gb1_out,
    gw2_out,
    gb2_out,
    x_rows,
    cot_rows,
    q_s,
    k_s,
    v_s,
    a_s,
    g_s,
    mid,
    h_rows,
    acc_a,
    slope,
    w_qkv,
    w_out,
    w_fc,
    w_proj,
    lse,
    delta,
    ke,
    ve,
    kt,
    dk,
    dv,
    starts_slots,
    starts_row,
    own_pre,
    pre_slots,
    pk_s,
    pv_s,
    hid,
    dp_pre,
    col_slots,
    dp_own,
    dp_slots,
    hid_own,
    hid_slots,
    o_two,
    keep_stats,
    x_send,
    x_recv,
    s_send,
    s_recv,
    p_send,
    p_recv,
    c_send,
    c_recv,
    o_send,
    o_recv,
    g_send,
    g_recv,
    r_send,
    r_recv,
    d_send,
    d_recv,
    e_send,
    e_recv,
    local_sem,
    fc_sem,
    proj_sem,
    x_here,
    cot_here,
):
    me, me_dp = lax.axis_index("col"), lax.axis_index("dp")
    piece, width = x_hbm.shape[1], x_hbm.shape[2]
    length = n * piece
    blocks = length // BLOCK
    pairs = width // PAIR
    inner = b_fc_ref.shape[0]
    tile = w_fc.shape[2]
    tiles = inner // tile
    rows_pre = table_ref.shape[0]
    group = BLOCK // piece
    part_width = w2_ref.shape[1]
    per_part = part_width // PAIR
    groups = n // group
    heads = 2 * pairs

    def spot(at):
        return pl.ds(pl.multiple_of(at * piece, piece), piece)

    def each(count, step):
        def body(k, carry):
            step(k)
            return carry

        lax.fori_loop(0, count, body, 0)

    reach = n // 2
    mine_base = lax.div(me, reach) * reach
    other_base = reach - mine_base
    seat = lax.rem(me, reach)

    def to(m):
        same = lax.div(m, reach)
        step = lax.rem(m, reach) + same
        there, bit = other_base + same * (mine_base - other_base), 1
        while bit < reach:
            differ = lax.rem(lax.div(seat, bit) + lax.div(step, bit), 2)
            there, bit = there + differ * bit, 2 * bit
        return there

    source = to

    def remote(src, dst, send, recv, d, axis, peer):
        return pltpu.make_async_remote_copy(
            src_ref=src,
            dst_ref=dst,
            send_sem=send.at[d],
            recv_sem=recv.at[d],
            device_id={axis: peer},
            device_id_type=MESH,
        )

    def vector(ref):
        return ref[...].astype(wide).reshape(1, -1)

    def fc_load(t, slot):
        cols = pl.ds(pl.multiple_of(t * tile, tile), tile)
        return pltpu.make_async_copy(w_fc_hbm.at[:, cols], w_fc.at[slot], fc_sem.at[slot])

    def proj_load(t, slot):
        rows = pl.ds(pl.multiple_of(t * tile, tile), tile)
        return pltpu.make_async_copy(w_proj_hbm.at[rows, :], w_proj.at[slot], proj_sem.at[slot])

    load_qkv = pltpu.make_async_copy(w_qkv_hbm, w_qkv, local_sem.at[0])
    load_qkv.start()
    barrier = pltpu.get_barrier_semaphore()
    for m in range(n - 1):
        peer = to(jnp.int32(m))
        pl.semaphore_signal(barrier, inc=1, device_id={"col": peer}, device_id_type=MESH)
    for d in range(1, n_dp):
        pl.semaphore_signal(
            barrier, inc=1, device_id={"dp": lax.rem(me_dp + d, n_dp)}, device_id_type=MESH
        )
    pl.semaphore_wait(barrier, n - 1 + n_dp - 1)

    def x_copy(d, peer):
        return remote(x_hbm.at[peer], x_rows.at[spot(me), :], x_send, x_recv, d, "col", peer)

    def starts_copy(d, peer):
        return remote(starts_hbm, starts_slots.at[me], s_send, s_recv, d, "col", peer)

    def pre_copy(d, peer):
        return remote(own_pre, pre_slots.at[me], p_send, p_recv, d, "col", peer)

    def cot_copy(d, peer):
        return remote(cot_hbm.at[peer], cot_rows.at[spot(me), :], c_send, c_recv, d, "col", peer)

    def out_copy(d, peer):
        return remote(h_rows.at[spot(peer), :], out_hbm.at[me], o_send, o_recv, d, "col", peer)

    def grad_copy(d, here, peer):
        return remote(here, grad_hbm.at[me], g_send, g_recv, d, "col", peer)

    def send_inputs(m):
        x_copy(m, to(m)).start()
        starts_copy(m, to(m)).start()

    each(n - 1, send_inputs)
    own_x = pltpu.make_async_copy(x_hbm.at[me], x_rows.at[spot(me), :], local_sem.at[1])
    own_x.start()
    own_cot = pltpu.make_async_copy(cot_hbm.at[me], cot_rows.at[spot(me), :], local_sem.at[2])
    own_cot.start()
    own_starts = pltpu.make_async_copy(starts_hbm, starts_slots.at[me], local_sem.at[3])
    own_starts.start()
    load_out = pltpu.make_async_copy(w_out_hbm, w_out, local_sem.at[4])
    load_out.start()
    fc_load(0, 0).start()
    proj_load(0, 0).start()

    hidden = jnp.tanh(
        dot(table_ref[...].astype(low_type), w1_ref[...].astype(low_type)) + vector(b1_ref)
    )
    hid[...] = jnp.concatenate([hidden, jnp.zeros((PRE - rows_pre, hidden.shape[1]), wide)], 0)
    own = dot(hidden.astype(low_type), w2_ref[...].astype(low_type)) + vector(b2_ref)
    own = jnp.concatenate([own, jnp.zeros((PRE - rows_pre, part_width), wide)], 0).astype(low_type)
    own_pre[...] = own
    pre_slots[me] = own
    each(n - 1, lambda m: pre_copy(m, to(m)).start())

    gain1, shift1 = vector(gain1_ref), vector(shift1_ref)
    own_x.wait()
    load_qkv.wait()

    def greet_peers(sem):
        def greet(m):
            pl.semaphore_signal(sem, inc=1, device_id={"col": to(m)}, device_id_type=MESH)

        each(n - 1, greet)

    span = n // 2
    rows_span = span * piece

    def starts_of(first):
        for j in range(first, first + reach):
            starts_row[:, j * piece : (j + 1) * piece] = starts_slots[j, pl.ds(me, 1), :]

    def by_half(lower, upper):
        @pl.when(me < reach)
        def _():
            lower()

        @pl.when(me >= reach)
        def _():
            upper()

    def forward_loop(work):
        def forward_pair(p):
            attention_forward_part(
                work,
                rows_pre,
                starts_row,
                q_s.at[p],
                k_s.at[p],
                v_s.at[p],
                pk_s.at[p],
                pv_s.at[p],
                a_s.at[p],
                lse.at[p],
                ke,
                kt,
                acc_a,
                slope,
                o_two,
                mid.at[pl.ds(pl.multiple_of(p * PAIR, PAIR), PAIR), :],
                keep_stats.at[p],
            )

        each(pairs, forward_pair)

    def catch_starts(m):
        peer = source(m)
        remote(starts_hbm, starts_slots.at[peer], s_send, s_recv, m, "col", peer).wait_recv()

    def send_cotangent():
        pl.semaphore_wait(x_here, n - 1)
        each(n - 1, lambda m: cot_copy(m, to(m)).start())

    def qkv_group(g):
        places = []
        for j in range(span):
            d = n - 1 - (g * span + j)
            rows = spot(source(d))
            places.append(rows)

            @pl.when(d < n - 1)
            def _():
                remote(
                    x_hbm.at[me], x_rows.at[rows, :], x_send, x_recv, d, "col", source(d)
                ).wait_recv()

            normed, _ = standardize(x_rows[rows, :].astype(wide))
            h_rows[j * piece : (j + 1) * piece, :] = (normed * gain1 + shift1).astype(low_type)

        @pl.when(g == 1)
        def _():
            greet_peers(x_here)

        normed = h_rows[0:rows_span, :]
        for c in range(0, 3 * width, width // 2):
            part = dot(normed, w_qkv[:, c : c + width // 2])
            part = part + b_qkv_ref[c : c + width // 2].astype(wide).reshape(1, -1)
            if c < width:
                part = part * (HEAD**-0.5)
            part = part.astype(low_type)
            slabs = (q_s, k_s, v_s)[c // width]
            for m in range(width // 2 // PAIR):
                pair = (c % width) // PAIR + m
                for j in range(span):
                    slabs[pair, places[j], :] = part[
                        j * piece : (j + 1) * piece, m * PAIR : (m + 1) * PAIR
                    ]
            if c == width // 2:
                pl.when(g == 1)(send_cotangent)

        @pl.when(g == 0)
        def _():
            each(reach - 1, lambda m: catch_starts(reach + m))
            own_starts.wait()
            by_half(lambda: starts_of(0), lambda: starts_of(reach))
            by_half(
                lambda: forward_loop(own_half_part(blocks, False)),
                lambda: forward_loop(own_half_part(blocks, True)),
            )

    each(2, qkv_group)

    each(reach, catch_starts)
    by_half(lambda: starts_of(reach), lambda: starts_of(0))

    def catch_prefix(m):
        peer = source(m)
        remote(own_pre, pre_slots.at[peer], p_send, p_recv, m, "col", peer).wait_recv()

    each(n - 1, catch_prefix)
    for j in range(n):
        for m in range(per_part):
            pair = j * per_part + m
            slab = pre_slots[j][:, m * PAIR : (m + 1) * PAIR]
            if pair < pairs:
                pk_s[pair] = slab
            else:
                pv_s[pair - pairs] = slab

    by_half(
        lambda: forward_loop(other_part(blocks, False)),
        lambda: forward_loop(other_part(blocks, True)),
    )

    load_out.wait()
    gain2, shift2 = vector(gain2_ref), vector(shift2_ref)
    big = 2 * BLOCK
    halves = [slice(r, r + big) for r in range(0, length, big)]

    def pairwise(step):
        def two(b):
            step(2 * b)
            step(2 * b + 1)

        each(blocks // 2, two)

    def project(b):
        r = pl.ds(pl.multiple_of(b * BLOCK, BLOCK), BLOCK)
        att = jnp.concatenate([a_s[p, r, :] for p in range(pairs)], axis=1)
        middle = x_rows[r, :].astype(wide) + dot(att, w_out[...]) + vector(b_out_ref)
        mid[r, :] = middle
        normed, _ = standardize(middle)
        h_rows[r, :] = (normed * gain2 + shift2).astype(low_type)
        acc_a[r, :] = middle + vector(b_proj_ref)

    pairwise(project)

    def forward_tile(t):
        slot = lax.rem(t, 2)
        fc_load(t, slot).wait()
        proj_load(t, slot).wait()

        @pl.when(t + 1 < tiles)
        def _():
            fc_load(t + 1, 1 - slot).start()
            proj_load(t + 1, 1 - slot).start()

        cols = pl.ds(pl.multiple_of(t * tile, tile), tile)
        bias = b_fc_ref[cols].astype(wide).reshape(1, -1)

        for r in halves:
            upper = dot(h_rows[r, :], w_fc[slot]) + bias
            value, steep = gelu_parts(upper)
            slope[r, cols] = steep.astype(low_type)
            acc_a[r, :] += dot(value.astype(low_type), w_proj[slot])

    each(tiles, forward_tile)

    def settle(b):
        r = pl.ds(pl.multiple_of(b * BLOCK, BLOCK), BLOCK)
        h_rows[r, :] = acc_a[r, :].astype(low_type)
        acc_a[r, :] = jnp.zeros((BLOCK, width), wide)

    each(blocks, settle)
    own_out = pltpu.make_async_copy(h_rows.at[spot(me), :], out_hbm.at[me], local_sem.at[5])
    own_out.start()
    own_cot.wait()

    def catch_cot(m):
        d = m
        peer = source(d)
        remote(
            cot_hbm.at[me], cot_rows.at[spot(peer), :], c_send, c_recv, d, "col", peer
        ).wait_recv()

    each(n - 1, catch_cot)
    greet_peers(cot_here)


    def backward_tile(step):
        t = tiles - 1 - step
        slot = lax.rem(t, 2)

        @pl.when(step >= 2)
        def _():
            fc_load(t, slot).wait()
            proj_load(t, slot).wait()

        @pl.when(step == 1)
        def _():
            pl.semaphore_wait(cot_here, n - 1)
            each(n - 1, lambda m: out_copy(m, to(m)).start())

        cols = pl.ds(pl.multiple_of(t * tile, tile), tile)
        for r in halves:
            grad_act = dot_nt(cot_rows[r, :], w_proj[slot])
            grad_upper = (grad_act * slope[r, cols].astype(wide)).astype(low_type)
            acc_a[r, :] += dot_nt(grad_upper, w_fc[slot])

        @pl.when(t >= 2)
        def _():
            fc_load(t - 2, slot).start()
            proj_load(t - 2, slot).start()

    each(tiles, backward_tile)
    feature_head = lax.broadcasted_iota(jnp.int32, (heads, width), 1) // HEAD
    which = lax.broadcasted_iota(jnp.int32, (heads, width), 0)
    member = jnp.where(feature_head == which, 1.0, 0.0).astype(low_type)

    def attend_gradient(b):
        r = pl.ds(pl.multiple_of(b * BLOCK, BLOCK), BLOCK)
        normed, inverse = standardize(mid[r, :])
        grad_mid = cot_rows[r, :].astype(wide) + norm_backward_pass(
            acc_a[r, :], gain2, normed, inverse
        )
        mid[r, :] = grad_mid
        grad_att = dot_nt(grad_mid.astype(low_type), w_out[...]).astype(low_type)
        att = jnp.concatenate([a_s[p, r, :] for p in range(pairs)], axis=1)
        both = grad_att.astype(wide) * att.astype(wide)
        both_low = both.astype(low_type)
        rest = (both - both_low.astype(wide)).astype(low_type)
        sums = dot_nt(member, both_low) + dot_nt(member, rest)
        for p in range(pairs):
            g_s[p, r, :] = grad_att[:, p * PAIR : (p + 1) * PAIR]
            delta[p, :, r] = sums[2 * p : 2 * p + 2, :]

    pairwise(attend_gradient)

    def backward_loop(plan):
        def backward_pair(p):
            lanes = pl.ds(pl.multiple_of(p * PAIR, PAIR), PAIR)
            attention_backward_part(
                plan,
                rows_pre,
                starts_row,
                q_s.at[p],
                k_s.at[p],
                v_s.at[p],
                g_s.at[p],
                pk_s.at[p],
                pv_s.at[p],
                lse.at[p],
                delta.at[p],
                dp_pre.at[p],
                dp_pre.at[pairs + p],
                ke,
                ve,
                kt,
                slope,
                dk,
                dv,
                acc_a.at[:, lanes],
                acc_a.at[lanes, :],
            )

        each(pairs, backward_pair)

    def backward_by_half(lower, upper):
        by_half(lambda: backward_loop(lower(blocks)), lambda: backward_loop(upper(blocks)))

    backward_by_half(lower_first_part, upper_first_part)

    def part_copy(d, peer):
        mine = dp_pre.at[pl.ds(peer * per_part, per_part)]
        return remote(mine, col_slots.at[me], r_send, r_recv, d, "col", peer)

    def dp_copy(d, peer):
        return remote(dp_own, dp_slots.at[me_dp], d_send, d_recv, d, "dp", peer)

    def hid_copy(d, peer):
        return remote(hid_own, hid_slots.at[me], e_send, e_recv, d, "col", peer)

    def sum_slots(slots, count):
        return lax.fori_loop(1, count, lambda j, total: total + slots[j], slots[0])

    def gradient_group(g):
        grads, places = [], []
        for j in range(group):
            rows = spot(to(g * group + j))
            places.append(rows)
            grads.append(
                jnp.concatenate(
                    [slabs[p, rows, :] for slabs in (q_s, k_s, v_s) for p in range(pairs)], axis=1
                )
            )
        back = dot_nt(jnp.concatenate(grads, axis=0), w_qkv[...])
        for j in range(group):
            at = g * group + j
            rows = places[j]
            normed, inverse = standardize(x_rows[rows, :].astype(wide))
            total = mid[rows, :] + norm_backward_pass(
                back[j * piece : (j + 1) * piece, :], gain1, normed, inverse
            )
            cot_rows[spot(at), :] = total.astype(low_type)

    def send_gradient(m):
        here = cot_rows.at[spot(m), :]

        @pl.when(m < n - 1)
        def _():
            grad_copy(m, here, to(m)).start()

        @pl.when(m == n - 1)
        def _():
            pltpu.make_async_copy(here, grad_hbm.at[me], local_sem.at[6]).start()

    def leave_step(part):
        def one_group(g):
            at = part * (groups // 2) + g
            gradient_group(at)
            each(group, lambda j: send_gradient(at * group + j))

        each(groups // 2, one_group)

        @pl.when(part == 0)
        def _():
            backward_by_half(lower_second_part, upper_second_part)

    each(2, leave_step)

    each(n - 1, lambda m: part_copy(m, to(m)).start())
    col_slots[me] = dp_pre[pl.ds(me * per_part, per_part)]

    def catch_part(m):
        peer = source(m)
        mine = dp_pre.at[pl.ds(me * per_part, per_part)]
        remote(mine, col_slots.at[peer], r_send, r_recv, m, "col", peer).wait_recv()

    each(n - 1, catch_part)
    total = sum_slots(col_slots, n)
    total = jnp.concatenate([total[m] for m in range(per_part)], axis=1)
    dp_own[...] = total
    dp_slots[me_dp] = total
    for d in range(1, n_dp):
        dp_copy(d, lax.rem(me_dp + d, n_dp)).start()
    for d in range(1, n_dp):
        peer = lax.rem(me_dp + n_dp - d, n_dp)
        remote(dp_own, dp_slots.at[peer], d_send, d_recv, d, "dp", peer).wait_recv()
    own_low = sum_slots(dp_slots, n_dp).astype(low_type)
    part = dot_nt(own_low, w2_ref[...].astype(low_type))
    hid_own[...] = part
    hid_slots[me] = part
    each(n - 1, lambda m: hid_copy(m, to(m)).start())

    hidden = hid[...]
    gw2_out[...] = lax.dot_general(
        hidden.astype(low_type), own_low, TN, preferred_element_type=wide
    )
    gb2_out[...] = jnp.sum(own_low.astype(wide), axis=0)

    def catch_hid(m):
        peer = source(m)
        remote(hid_own, hid_slots.at[peer], e_send, e_recv, m, "col", peer).wait_recv()

    each(n - 1, catch_hid)
    grad_pre = (sum_slots(hid_slots, n) * (1.0 - hidden * hidden)).astype(low_type)
    table = jnp.concatenate(
        [table_ref[...], jnp.zeros((PRE - rows_pre, table_ref.shape[1]), wide)], 0
    ).astype(low_type)
    gw1_out[...] = lax.dot_general(table, grad_pre, TN, preferred_element_type=wide)
    gb1_out[...] = jnp.sum(grad_pre.astype(wide), axis=0)
    table_out[...] = dot_nt(grad_pre, w1_ref[...].astype(low_type))[:rows_pre, :]

    def finish(m):
        peer, here = source(m), cot_rows.at[0:piece, :]
        remote(here, out_hbm.at[peer], o_send, o_recv, m, "col", peer).wait_recv()
        x_copy(m, to(m)).wait_send()
        starts_copy(m, to(m)).wait_send()
        pre_copy(m, to(m)).wait_send()
        cot_copy(m, to(m)).wait_send()
        out_copy(m, to(m)).wait_send()
        part_copy(m, to(m)).wait_send()
        hid_copy(m, to(m)).wait_send()

    each(n - 1, finish)
    for d in range(1, n_dp):
        dp_copy(d, lax.rem(me_dp + d, n_dp)).wait_send()
    own_out.wait()
    pltpu.make_async_copy(cot_rows.at[0:piece, :], grad_hbm.at[me], local_sem.at[6]).wait()

    def finish_gradient(m):
        peer, here = source(m), cot_rows.at[0:piece, :]
        remote(here, grad_hbm.at[peer], g_send, g_recv, m, "col", peer).wait_recv()
        grad_copy(m, here, to(m)).wait_send()

    each(n - 1, finish_gradient)


def hand_over_kernel(count, *refs):
    given, wanted, held = refs[:count], refs[count : 2 * count], refs[2 * count : 3 * count]
    sems = refs[3 * count]
    come = [pltpu.make_async_copy(given[j], held[j], sems.at[0, j]) for j in range(count)]
    go = [pltpu.make_async_copy(held[j], wanted[j], sems.at[1, j]) for j in range(count)]
    for copy in come:
        copy.start()
    for arrived, copy in zip(come, go):
        arrived.wait()
        copy.start()
    for copy in go:
        copy.wait()


def hand_over(results):
    results = list(results)
    count = len(results)
    return tuple(
        pl.pallas_call(
            functools.partial(hand_over_kernel, count),
            in_specs=[ANY] * count,
            out_specs=[ANY] * count,
            out_shape=[jax.ShapeDtypeStruct(r.shape, r.dtype) for r in results],
            scratch_shapes=[pltpu.VMEM(r.shape, r.dtype) for r in results]
            + [pltpu.SemaphoreType.DMA((2, count))],
            compiler_params=pltpu.CompilerParams(vmem_limit_bytes=VMEM_BYTES),
        )(*results)
    )


def on_device(*operands):
    n, n_dp = lax.axis_size("col"), lax.axis_size("dp")
    inputs, starts, cotangent, w_qkv, w_out = [operands[j] for j in (0, 1, 2, 5, 7)]
    w_fc, w_proj, table, w1, w2 = [operands[j] for j in (11, 13, 15, 16, 18)]
    row_count, piece, width = inputs.shape
    assert row_count == n and BLOCK % piece == 0
    length, inner = n * piece, w_fc.shape[1]
    pairs, tile = width // PAIR, min(1024, inner)
    part_width, mid_width = w2.shape[1], w1.shape[1]
    per_part = part_width // PAIR
    ext = PRE + length
    dma = pltpu.SemaphoreType.DMA
    shape = jax.ShapeDtypeStruct
    vmem = pltpu.VMEM
    slabs = vmem((pairs, length, PAIR), low_type)
    ordered = [operands[j] for j in (0, 1, 2, 5, 7, 11, 13)]
    ordered += [operands[j] for j in (3, 4, 6, 8, 9, 10, 12, 14, 15, 16, 17, 18, 19)]
    return hand_over(
        pl.pallas_call(
            functools.partial(block_kernel, n, n_dp),
            in_specs=[ANY] * 7 + [VM] * 13,
            out_specs=[ANY, ANY] + [VM] * 5,
            out_shape=[
                shape((n, piece, width), low_type),
                shape((n, piece, width), low_type),
                shape(table.shape, wide),
                shape(w1.shape, wide),
                shape((mid_width,), wide),
                shape(w2.shape, wide),
                shape((part_width,), wide),
            ],
            scratch_shapes=[
                vmem((length, width), low_type),
                vmem((length, width), low_type),
                slabs,
                slabs,
                slabs,
                slabs,
                slabs,
                vmem((length, width), wide),
                vmem((length, width), low_type),
                vmem((ext, width), wide),
                vmem((ext, inner), low_type),
                vmem(w_qkv.shape, low_type),
                vmem(w_out.shape, low_type),
                vmem((2, width, tile), low_type),
                vmem((2, tile, width), low_type),
                vmem((pairs, 2, length), wide),
                vmem((pairs, 2, length), wide),
                vmem((ext, PAIR), low_type),
                vmem((ext, PAIR), low_type),
                vmem((PAIR, ext), low_type),
                vmem((ext, PAIR), wide),
                vmem((ext, PAIR), wide),
                vmem((n,) + starts.shape, jnp.int32),
                vmem((1, length), jnp.int32),
                vmem((PRE, part_width), low_type),
                vmem((n, PRE, part_width), low_type),
                vmem((pairs, PRE, PAIR), low_type),
                vmem((pairs, PRE, PAIR), low_type),
                vmem((PRE, mid_width), wide),
                vmem((2 * pairs, PRE, PAIR), wide),
                vmem((n, per_part, PRE, PAIR), wide),
                vmem((PRE, part_width), wide),
                vmem((n_dp, PRE, part_width), wide),
                vmem((PRE, mid_width), wide),
                vmem((n, PRE, mid_width), wide),
                vmem((2, PAIR, BLOCK), wide),
                vmem((pairs, 4, length // 2), wide),
            ]
            + [dma((n,))] * 14
            + [dma((n_dp,))] * 2
            + [dma((n,))] * 2
            + [dma((7,)), dma((2,)), dma((2,))]
            + [pltpu.SemaphoreType.REGULAR] * 2,
            compiler_params=pltpu.CompilerParams(
                collective_id=0, has_side_effects=True, vmem_limit_bytes=VMEM_BYTES
            ),
        )(*ordered)
    )


def solution(mesh):
    rows = P("dp", "col", None)
    return jax.shard_map(
        on_device,
        mesh=mesh,
        in_specs=(rows, P("dp", "col"), rows) + (P(),) * 15 + (P(None, "col"), P("col")),
        out_specs=(rows, rows, P(), P(), P(), P(None, "col"), P("col")),
        check_vma=False,
    )
```
